32 devices in a mesh: page: 8 (over z, x), win: 4 (over y, core).
Axes of the slice: x: 2, y: 2, z: 4, core: 2. Of those that a mesh axis runs over, the one named last changes fastest.
Arguments:
- visual: bfloat16 [8, 48, 36, 768], P('page', 'win'), may hold values from -6 to 6
- queries: bfloat16 [8, 256, 768], P('page'), may hold values from -6 to 6
- query_lengths: int32 [8], P('page'), may hold values from 1 to 256, as said below
- column_regions: int32 [8, 36], P('page'), may hold values from 0 to 2, never falling along the last dimension, each value on 1 to 18 neighbouring positions
- gain_window: bfloat16 [768], P('win'), may hold values from 0.099609375 to 1.8984375
- window_qkv: bfloat16 [768, 2304], P('win'), may hold values from -0.21875 to 0.21875
- window_out: bfloat16 [768, 768], P('win'), may hold values from -0.875 to 0.875
- position_bias: bfloat16 [12, 529], P('win'), may hold values from -4 to 4
- gain_visual: bfloat16 [768], P('win'), may hold values from 0.099609375 to 1.8984375
- gain_query: bfloat16 [768], P('win'), may hold values from 0.099609375 to 1.8984375
- attend_query: bfloat16 [768, 768], P('win'), may hold values from -0.21875 to 0.21875
- attend_kv: bfloat16 [768, 1536], P('win'), may hold values from -0.21875 to 0.21875
- attend_out: bfloat16 [768, 768], P('win'), may hold values from -1.25 to 1.25
- cross_query: bfloat16 [768, 768], P('win'), may hold values from -0.21875 to 0.21875
- cross_kv: bfloat16 [768, 1536], P('win'), may hold values from -0.21875 to 0.21875
- cross_out: bfloat16 [768, 768], P('win'), may hold values from -0.625 to 0.625
- gain_feed: bfloat16 [768], P('win'), may hold values from 0.099609375 to 1.8984375
- visual_up: bfloat16 [768, 3072], P('win'), may hold values from -0.21875 to 0.21875
- visual_down: bfloat16 [3072, 768], P('win'), may hold values from -0.15625 to 0.15625
- gain_query_feed: bfloat16 [768], P('win'), may hold values from 0.099609375 to 1.8984375
- query_up: bfloat16 [768, 3072], P('win'), may hold values from -0.21875 to 0.21875
- query_down: bfloat16 [3072, 768], P('win'), may hold values from -0.15625 to 0.15625
- cotangent_visual: bfloat16 [8, 48, 36, 768], P('page', 'win'), may hold values from -6 to 6
- cotangent_query: bfloat16 [8, 256, 768], P('page'), may hold values from -6 to 6
Outputs:
- visual_out: bfloat16 [8, 48, 36, 768], P('page', 'win')
- query_out: bfloat16 [8, 256, 768], P('page')
- visual_grad: bfloat16 [8, 48, 36, 768], P('page', 'win')
- query_grad: bfloat16 [8, 256, 768], P('page')
- grad_gain_window: float32 [768], P('win')
- grad_window_qkv: float32 [768, 2304], P('win')
- grad_window_out: float32 [768, 768], P('win')
- grad_position_bias: float32 [12, 529], P('win')
- grad_gain_visual: float32 [768], P('win')
- grad_gain_query: float32 [768], P('win')
- grad_attend_query: float32 [768, 768], P('win')
- grad_attend_kv: float32 [768, 1536], P('win')
- grad_attend_out: float32 [768, 768], P('win')
- grad_cross_query: float32 [768, 768], P('win')
- grad_cross_kv: float32 [768, 1536], P('win')
- grad_cross_out: float32 [768, 768], P('win')
- grad_gain_feed: float32 [768], P('win')
- grad_visual_up: float32 [768, 3072], P('win')
- grad_visual_down: float32 [3072, 768], P('win')
- grad_gain_query_feed: float32 [768], P('win')
- grad_query_up: float32 [768, 3072], P('win')
- grad_query_down: float32 [3072, 768], P('win')
The draws below stay inside these ranges and needn't reach their ends.
Inputs may be any that keep to these rules, and one draw needn't show every extreme that they name: `query_lengths`: the longest page of every draw has exactly 256 live query slots. `column_regions`: region numbers never fall from left to right along a page's columns, and each of the 3 numbers covers at least one column.
All inputs are finite; a program needn't handle non-finite values.
Results may differ from the reference program's by a relative error of at most 0.02.
Values may be sent and summed in bfloat16 or wider, within the bound.
No kernel may reach another device: no remote copies, remote signals or barrier semaphores. Data moves between devices by JAX's collectives and lax.ppermute only.
A program may use at most 256 MiB of HBM per device.

```python
import math
import jax
import jax.numpy as jnp
import numpy as np
from jax import lax

D = 768
HEADS = 12
FF = 3072
WS = 12
REGIONS = 3
QMAX = 256
WIDTH = 36
ROWS = 48
PAGES = 8
OFFSETS = 529
N_WIN = 4


def draw_query_lengths(key, part):
    key = jax.random.fold_in(key, 11)
    key_exp, key_len, key_top = jax.random.split(key, 3)
    exponents = jax.random.randint(key_exp, (PAGES,), 0, 4)
    ceilings = QMAX // jnp.left_shift(jnp.ones((PAGES,), jnp.int32), exponents)
    lengths_drawn = jax.random.randint(key_len, (PAGES,), 1, ceilings + 1)
    longest = jax.random.randint(key_top, (), 0, PAGES)
    return jnp.where(jnp.arange(PAGES) == longest, QMAX, lengths_drawn).astype(jnp.int32)


def steps_of(rng, extent, cuts, low, largest):
    loudness, own = 1.0, jax.random.fold_in(rng, 6)
    for dim, parts in cuts:
        draws = jnp.exp(jax.random.uniform(jax.random.fold_in(own, dim), (parts,), jnp.float32, low / len(cuts), largest / len(cuts)))
        loudness = loudness * jnp.repeat(draws, extent[dim] // parts).reshape([-1 if axis == dim else 1 for axis in range(len(extent))])
    return loudness


def length_profile(number_of, total, bound, skew):
    loads = [(1 << 20) // math.isqrt(standing ** skew) + 1 for standing in range(2, number_of + 1)]
    spare, counts = total - bound - (number_of - 1), [1] * (number_of - 1)
    while spare > 0:
        free = [i for i in range(number_of - 1) if counts[i] < bound]
        mass, remaining = sum([loads[i] for i in free]), spare
        for i in free:
            addition = min(bound - counts[i], max(1, remaining * loads[i] // mass), spare)
            counts[i] = counts[i] + addition
            spare = spare - addition
    return np.array([bound] + counts)


def uneven(key, count, total, most, skew):
    if count == 2:
        one = jax.random.randint(key, (), max(1, total - most), min(most, total - 1) + 1)
        return jnp.stack([one, total - one])
    lengths = jnp.asarray(length_profile(count, total, most, skew), jnp.int32)
    couples = (count - 1) // 2
    donor, taker = lengths[1:1 + 2 * couples:2], lengths[2:2 + 2 * couples:2]
    room = jnp.minimum(donor - 1, most - taker)
    moved = jax.random.randint(jax.random.fold_in(key, 1), (couples,), 0, 1 << 20) % (room + 1)
    lengths = lengths.at[1:1 + 2 * couples:2].set(donor - moved).at[2:2 + 2 * couples:2].set(taker + moved)
    return lengths[jax.random.permutation(jax.random.fold_in(key, 2), count)]


def scatter_about(stream_key, dims, scale, most, cuts=(), kind=jnp.bfloat16):
    result = scale * jax.random.normal(stream_key, dims, jnp.float32)
    if cuts:
        result = result * steps_of(stream_key, dims, cuts, -0.22, 0.18)
    return jnp.clip(result, -most, most).astype(kind)


def setup_inputs(seed: int = 0) -> dict:
    streams_of = jax.random.split(jax.random.key(seed), 25)
    return {
        "visual": scatter_about(streams_of[0], (PAGES, ROWS, WIDTH, D), 1.0, 6.0, ((0, 8), (1, 4))),
        "queries": scatter_about(streams_of[1], (PAGES, QMAX, D), 1.0, 6.0, ((0, 8),)),
        "query_lengths": draw_query_lengths(jax.random.fold_in(streams_of[24], 71), 0),
        "column_regions": jax.vmap(lambda own: jnp.searchsorted(jnp.cumsum(uneven(own, REGIONS, WIDTH, WIDTH // 2, 0)), jnp.arange(WIDTH), side="right"))(jax.random.split(streams_of[3], PAGES)).reshape((PAGES, WIDTH)).astype(jnp.int32),
        "gain_window": jnp.clip(1.0 + 0.18 * jax.random.normal(streams_of[4], (D,), jnp.float32), 0.099609375, 1.8984375).astype(jnp.bfloat16),
        "window_qkv": scatter_about(streams_of[5], (D, 3 * D), D ** -0.5, 0.21875, ((0, 4),)),
        "window_out": scatter_about(streams_of[6], (D, D), (D // 16) ** -0.5, 0.875, ((0, 4),)),
        "position_bias": scatter_about(streams_of[7], (HEADS, OFFSETS), 1.0, 4.0, ((0, 4),)),
        "gain_visual": jnp.clip(1.0 + 0.18 * jax.random.normal(streams_of[8], (D,), jnp.float32), 0.099609375, 1.8984375).astype(jnp.bfloat16),
        "gain_query": jnp.clip(1.0 + 0.18 * jax.random.normal(streams_of[9], (D,), jnp.float32), 0.099609375, 1.8984375).astype(jnp.bfloat16),
        "attend_query": scatter_about(streams_of[10], (D, D), D ** -0.5, 0.21875, ((0, 4),)),
        "attend_kv": scatter_about(streams_of[11], (D, 2 * D), D ** -0.5, 0.21875, ((0, 4),)),
        "attend_out": scatter_about(streams_of[12], (D, D), (D // 32) ** -0.5, 1.25, ((0, 4),)),
        "cross_query": scatter_about(streams_of[13], (D, D), D ** -0.5, 0.21875, ((0, 4),)),
        "cross_kv": scatter_about(streams_of[14], (D, 2 * D), D ** -0.5, 0.21875, ((0, 4),)),
        "cross_out": scatter_about(streams_of[15], (D, D), (D // 8) ** -0.5, 0.625, ((0, 4),)),
        "gain_feed": jnp.clip(1.0 + 0.18 * jax.random.normal(streams_of[16], (D,), jnp.float32), 0.099609375, 1.8984375).astype(jnp.bfloat16),
        "visual_up": scatter_about(streams_of[17], (D, FF), D ** -0.5, 0.21875, ((0, 4),)),
        "visual_down": scatter_about(streams_of[18], (FF, D), (FF // 2) ** -0.5, 0.15625, ((0, 4),)),
        "gain_query_feed": jnp.clip(1.0 + 0.18 * jax.random.normal(streams_of[19], (D,), jnp.float32), 0.099609375, 1.8984375).astype(jnp.bfloat16),
        "query_up": scatter_about(streams_of[20], (D, FF), D ** -0.5, 0.21875, ((0, 4),)),
        "query_down": scatter_about(streams_of[21], (FF, D), (FF // 2) ** -0.5, 0.15625, ((0, 4),)),
        "cotangent_visual": scatter_about(streams_of[22], (PAGES, ROWS, WIDTH, D), 1.0, 6.0, ((0, 8), (1, 4))),
        "cotangent_query": scatter_about(streams_of[23], (PAGES, QMAX, D), 1.0, 6.0, ((0, 8),)),
    }


@jax.custom_vjp
def low(v):
    return lax.optimization_barrier(v.astype(jnp.bfloat16)).astype(jnp.float32)

@jax.custom_vjp
def low_back(v):
    return v

def low_keep(v):
    return (low(v), None)

def low_pass(kept, grad):
    return (grad,)

def back_keep(v):
    return (v, None)

def back_low(kept, grad):
    return (low(grad),)
low.defvjp(low_keep, low_pass)
low_back.defvjp(back_keep, back_low)
highest = lax.Precision.HIGHEST
masked_fill = -1000000000.0

def both_ways(tensor):
    return low(low_back(tensor))

def product(left_op, right_op):
    return jnp.dot(left_op, right_op, precision=highest)

def layer_norm(tensor, gain_vec):
    centre = tensor - lax.optimization_barrier(jnp.mean(tensor, axis=-1, keepdims=True))
    spread = lax.optimization_barrier(jnp.mean(centre * centre, axis=-1, keepdims=True))
    return centre * lax.rsqrt(spread + 1e-05) * gain_vec

def attention(queries_in, keys_in, values_in, extra, allowed):
    count_q = queries_in.shape[0]
    count_k = keys_in.shape[0]
    head_size = D // HEADS
    query_heads = queries_in.reshape(count_q, HEADS, head_size)
    key_heads = keys_in.reshape(count_k, HEADS, head_size)
    value_heads = values_in.reshape(count_k, HEADS, head_size)
    scores = jnp.einsum('qhd,khd->hqk', query_heads, key_heads, precision=highest) * head_size ** (-0.5) + extra
    scores = jnp.where(allowed, low_back(scores), masked_fill)
    weights = low(jax.nn.softmax(scores, axis=-1))
    mixed = jnp.einsum('hqk,khd->qhd', weights, value_heads, precision=highest)
    return both_ways(mixed.reshape(count_q, D))

def page_layer(params, visual_page, query_page, length, regions):
    gain_window, window_qkv, window_out, position_bias, gain_visual, gain_query, attend_query, attend_kv, attend_out, cross_query, cross_kv, cross_out, gain_feed, visual_up, visual_down, gain_query_feed, query_up, query_down = params
    half_win = WS // 2
    page_rows = WS * N_WIN
    columns = WIDTH // WS + 1
    stripes = N_WIN + 1
    normed = low(layer_norm(visual_page, gain_window))
    packed = both_ways(product(normed.reshape(-1, D), window_qkv)).reshape(page_rows, WIDTH, 3 * D)
    padded = jnp.pad(packed, ((half_win, half_win), (half_win, half_win), (0, 0)))
    windows = padded.reshape(stripes, WS, columns, WS, 3 * D).transpose(0, 2, 1, 3, 4)
    windows = windows.reshape(stripes * columns, WS * WS, 3 * D)
    row_ids = jnp.arange(page_rows + WS, dtype=jnp.int32) - half_win
    col_ids = jnp.arange(WIDTH + WS, dtype=jnp.int32) - half_win
    row_ok = (row_ids >= 0) & (row_ids < page_rows)
    col_ok = (col_ids >= 0) & (col_ids < WIDTH)
    region_pad = jnp.pad(regions, (half_win, half_win), constant_values=-1)
    cell_ok = row_ok[:, None] & col_ok[None, :]
    cell_region = jnp.broadcast_to(region_pad[None, :], cell_ok.shape)

    def window_view(grid_in):
        return grid_in.reshape(stripes, WS, columns, WS).transpose(0, 2, 1, 3).reshape(stripes * columns, WS * WS)
    key_ok = window_view(cell_ok)
    key_region = window_view(cell_region)
    allowed = key_ok[:, None, :] & (key_region[:, :, None] == key_region[:, None, :])
    places = jnp.arange(WS * WS, dtype=jnp.int32)
    place_row = places // WS
    place_col = places % WS
    offsets = (place_row[:, None] - place_row[None, :] + WS - 1) * (2 * WS - 1) + place_col[:, None] - place_col[None, :] + WS - 1
    bias = jnp.take(position_bias, offsets, axis=1)
    mixed = jax.vmap(attention, in_axes=(0, 0, 0, None, 0))(windows[..., :D], windows[..., D:2 * D], windows[..., 2 * D:], bias, allowed[:, None])
    grid_out = mixed.reshape(stripes, columns, WS, WS, D).transpose(0, 2, 1, 3, 4).reshape(page_rows + WS, WIDTH + WS, D)
    heads_grid = grid_out[half_win:half_win + page_rows, half_win:half_win + WIDTH].reshape(-1, D)
    visual_mid = visual_page.reshape(-1, D) + low_back(product(heads_grid, window_out))
    norm_visual = low(layer_norm(visual_mid, gain_visual))
    norm_query = low(layer_norm(query_page, gain_query))
    query_proj = both_ways(product(norm_query, attend_query))
    visual_kv = both_ways(product(norm_visual, attend_kv))
    query_kv = both_ways(product(norm_query, attend_kv))
    slot_ids = jnp.arange(QMAX, dtype=jnp.int32)
    live = slot_ids < length
    causal = (slot_ids[None, :] <= slot_ids[:, None]) & live[None, :]
    reach = jnp.concatenate((jnp.ones((QMAX, visual_mid.shape[0]), dtype=bool), causal), axis=1)
    key_all = jnp.concatenate((visual_kv[:, :D], query_kv[:, :D]), axis=0)
    value_all = jnp.concatenate((visual_kv[:, D:], query_kv[:, D:]), axis=0)
    query_mixed = attention(query_proj, key_all, value_all, 0.0, reach[None])
    query_mid = query_page + low_back(product(query_mixed, attend_out))
    cross_proj = both_ways(product(norm_visual, cross_query))
    cross_pair = both_ways(product(norm_query, cross_kv))
    cross_allowed = jnp.broadcast_to(live[None, None, :], (1, visual_mid.shape[0], QMAX))
    cross_mixed = attention(cross_proj, cross_pair[:, :D], cross_pair[:, D:], 0.0, cross_allowed)
    visual_late = visual_mid + low_back(product(cross_mixed, cross_out))
    feed_norm = low(layer_norm(visual_late, gain_feed))
    feed_hidden = low_back(product(feed_norm, visual_up))
    feed_act = low(jax.nn.gelu(feed_hidden, approximate=False))
    visual_final = visual_late + low_back(product(feed_act, visual_down))
    query_norm = low(layer_norm(query_mid, gain_query_feed))
    query_hidden = low_back(product(query_norm, query_up))
    query_act = low(jax.nn.gelu(query_hidden, approximate=False))
    query_final = query_mid + low_back(product(query_act, query_down))
    return (visual_final.reshape(page_rows, WIDTH, D), query_final)

def reference(visual, queries, query_lengths, column_regions, gain_window, window_qkv, window_out, position_bias, gain_visual, gain_query, attend_query, attend_kv, attend_out, cross_query, cross_kv, cross_out, gain_feed, visual_up, visual_down, gain_query_feed, query_up, query_down, cotangent_visual, cotangent_query):
    params = (gain_window.astype(jnp.float32), window_qkv.astype(jnp.float32), window_out.astype(jnp.float32), position_bias.astype(jnp.float32), gain_visual.astype(jnp.float32), gain_query.astype(jnp.float32), attend_query.astype(jnp.float32), attend_kv.astype(jnp.float32), attend_out.astype(jnp.float32), cross_query.astype(jnp.float32), cross_kv.astype(jnp.float32), cross_out.astype(jnp.float32), gain_feed.astype(jnp.float32), visual_up.astype(jnp.float32), visual_down.astype(jnp.float32), gain_query_feed.astype(jnp.float32), query_up.astype(jnp.float32), query_down.astype(jnp.float32))

    def forward(weights_all, visual_all, query_all):

        def per_page(items):
            return page_layer(weights_all, items[0], items[1], items[2], items[3])
        return lax.map(jax.checkpoint(per_page), (visual_all, query_all, query_lengths, column_regions))
    outputs, pullback = jax.vjp(forward, params, visual.astype(jnp.float32), queries.astype(jnp.float32))
    weight_grads, visual_back, query_back = pullback((cotangent_visual.astype(jnp.float32), cotangent_query.astype(jnp.float32)))
    return (outputs[0].astype(jnp.bfloat16), outputs[1].astype(jnp.bfloat16), visual_back.astype(jnp.bfloat16), query_back.astype(jnp.bfloat16), weight_grads[0], weight_grads[1], weight_grads[2], weight_grads[3], weight_grads[4], weight_grads[5], weight_grads[6], weight_grads[7], weight_grads[8], weight_grads[9], weight_grads[10], weight_grads[11], weight_grads[12], weight_grads[13], weight_grads[14], weight_grads[15], weight_grads[16], weight_grads[17])
```

```python
import functools

import jax
import jax.numpy as jnp
import numpy as np
from jax import lax
from jax.experimental import pallas as pl
from jax.experimental.pallas import tpu as pltpu
from jax.sharding import PartitionSpec as P

HEADS = 12
WS = 12
SPAN = 2 * WS - 1
LANES = 256

epsilon = 1e-05
masked_fill = -1000000000.0
bf16 = jnp.bfloat16
f32 = jnp.float32
VMEM_BYTES = 48 * 1024 * 1024


def swap(tensor, axis, bit):
    count = lax.axis_size(axis)
    return lax.ppermute(tensor, axis, [(i, i ^ bit) for i in range(count)])


def bits_of(count):
    bits = []
    while count > 1:
        count //= 2
        bits.append(count)
    return bits


def gather_blocks(block, axis="win"):
    for bit in bits_of(lax.axis_size(axis)):
        block = jnp.concatenate([block, swap(block, axis, bit)], axis=0)
    return block


def scatter_sum(parts, axis="win"):
    bits = bits_of(lax.axis_size(axis))
    for bit in reversed(bits):
        half = parts.shape[0] // 2
        arrived = swap(parts[half:].astype(bf16), axis, bit)
        parts = parts[:half].astype(f32) + arrived.astype(f32)
    return parts


def total_sum(part, axis="win"):
    for bit in reversed(bits_of(lax.axis_size(axis))):
        mine = lax.reduce_precision(part.astype(f32), 8, 7)
        part = mine + swap(mine.astype(bf16), axis, bit).astype(f32)
    return part


def tiny_sum(part, axes):
    for axis in axes:
        for bit in reversed(bits_of(lax.axis_size(axis))):
            part = part + swap(part, axis, bit)
    return part


def pick(stack, index):
    return lax.dynamic_index_in_dim(stack, index, 0, False)


def trade(stack, axis="win"):
    count = lax.axis_size(axis)
    me = lax.axis_index(axis)
    return [pick(stack, me)] + [swap(pick(stack, me ^ k), axis, k) for k in range(1, count)]


def in_order(blocks, axis="win"):
    me = lax.axis_index(axis)
    stack = jnp.stack(blocks) if isinstance(blocks, (list, tuple)) else blocks
    return [pick(stack, me ^ j) for j in range(lax.axis_size(axis))]


def xor_order(count):
    order = [0]
    for bit in bits_of(count):
        order = order + [k ^ bit for k in order]
    return order


def rounded(tensor):
    return lax.reduce_precision(tensor, 8, 7)


def add_low(left, right):
    return rounded(left.astype(f32) + right.astype(f32)).astype(bf16)


def line_pairs(pairs):
    return [(2 * a + x, 2 * b + x) for a, b in pairs for x in (0, 1)]


INWARD = line_pairs([(0, 1), (3, 2)])
MIDDLE = line_pairs([(1, 2), (2, 1)])
OUTWARD = line_pairs([(1, 0), (2, 3)])
SIDE = [(i, i ^ 1) for i in range(8)]
MIDDLE_SIDE = [(i, i ^ 1) for i in range(2, 6)]


def page_total_across(tensor):
    half = tensor.shape[0] // 2
    me = lax.axis_index("page")
    side, depth = me % 2, me // 2
    stack = tensor.reshape((2, half) + tensor.shape[1:])
    own = add_low(pick(stack, side), lax.ppermute(pick(stack, 1 - side), "page", SIDE))
    own = add_low(own, lax.ppermute(own, "page", INWARD))
    own = add_low(own, lax.ppermute(own, "page", MIDDLE))
    outer = (depth == 0) | (depth == 3)
    own = jnp.where(outer, lax.ppermute(own, "page", OUTWARD), own)
    other = lax.ppermute(own, "page", SIDE)
    first = side == 0
    return jnp.concatenate([jnp.where(first, own, other), jnp.where(first, other, own)], axis=0)


def page_total_along(tensor):
    half = tensor.shape[0] // 2
    depth = lax.axis_index("page") // 2
    own = add_low(tensor, lax.ppermute(tensor, "page", INWARD))
    stack = own.reshape((2, half) + tensor.shape[1:])
    low = depth < 2
    keep = jnp.where(low, stack[0], stack[1])
    give = jnp.where(low, stack[1], stack[0])
    keep = add_low(keep, lax.ppermute(give, "page", MIDDLE))
    keep = add_low(keep, lax.ppermute(keep, "page", MIDDLE_SIDE))
    other = lax.ppermute(keep, "page", MIDDLE)
    full = jnp.concatenate([jnp.where(low, keep, other), jnp.where(low, other, keep)], axis=0)
    outer = (depth == 0) | (depth == 3)
    return jnp.where(outer, lax.ppermute(full, "page", OUTWARD), full)


def page_total(across, along):
    if lax.axis_size("page") == 8:
        return page_total_across(across), page_total_along(along)
    return lax.psum(across, "page"), lax.psum(along, "page")


def normalise(tensor):
    centre = tensor - jnp.mean(tensor, axis=-1, keepdims=True)
    spread = lax.rsqrt(jnp.mean(centre * centre, axis=-1, keepdims=True) + epsilon)
    return centre * spread, spread


def norm_low(tensor, gain):
    return (normalise(tensor)[0] * gain).astype(bf16)


def norm_back(tensor, gain, upstream):
    unit, spread = normalise(tensor)
    scaled = upstream * gain
    return spread * (
        scaled
        - jnp.mean(scaled, axis=-1, keepdims=True)
        - unit * jnp.mean(scaled * unit, axis=-1, keepdims=True)
    )


def gelu_both(hidden):
    phi = 0.5 * (1.0 + lax.erf(hidden * np.float32(np.sqrt(0.5))))
    density = jnp.exp(-0.5 * hidden * hidden) * np.float32(1.0 / np.sqrt(2.0 * np.pi))
    return hidden * phi, phi + hidden * density


def matmul(left, right):
    return jnp.dot(left, right, preferred_element_type=f32)


def left_tmul(left, right):
    return lax.dot_general(left, right, (((0,), (0,)), ((), ())), preferred_element_type=f32)


def right_tmul(left, right):
    return lax.dot_general(left, right, (((1,), (1,)), ((), ())), preferred_element_type=f32)


def pad_lanes(tensor, width):
    return jnp.pad(tensor, ((0, 0), (0, width - tensor.shape[1])))


def head_mask(head, head_size, width, scale):
    lane = lax.broadcasted_iota(jnp.int32, (1, width), 1)
    inside = (lane >= head * head_size) & (lane < (head + 1) * head_size)
    return jnp.where(inside, np.float32(scale), np.float32(0.0)).astype(bf16)


def softmax_rows(scores):
    peak = jnp.max(scores, axis=-1, keepdims=True)
    mass = jnp.exp(scores - peak)
    return mass * (1.0 / jnp.sum(mass, axis=-1, keepdims=True))


def window_probs(query, key, mask, heads, head_size, scale):
    stacked = jnp.concatenate(
        [query * head_mask(h, head_size, query.shape[1], scale) for h in range(heads)], axis=0
    )
    return stacked, softmax_rows(right_tmul(stacked, key) + mask)


def window_forward_kernel(heads, head_size, scale, packed, spread, gathered, slots, rows, out):
    cells = WS * WS
    win = matmul(spread[...], packed[...]).astype(bf16)
    count = win.shape[0] // cells
    width = win.shape[1] // 3
    mixed = []
    for j in range(count):
        part = win[j * cells : (j + 1) * cells]
        query, key, value = part[:, :width], part[:, width : 2 * width], part[:, 2 * width :]
        mask = slots[j * heads * cells : (j + 1) * heads * cells, :] + rows[0]
        _, probs = window_probs(query, key, mask, heads, head_size, scale)
        probs = probs.astype(bf16)
        total = None
        for h in range(heads):
            term = matmul(
                probs[h * cells : (h + 1) * cells], value * head_mask(h, head_size, width, 1.0)
            )
            total = term if total is None else total + term
        mixed.append(total.astype(bf16))
    grid = matmul(gathered[...], jnp.concatenate(mixed, axis=0)).astype(bf16)
    out[...] = grid[:, : out.shape[1]]


def window_backward_kernel(
    heads, head_size, scale, packed, upstream, spread, gathered, slots, rows, out, bias_out, bias_sum
):
    cells = WS * WS
    win = matmul(spread[...], packed[...]).astype(bf16)
    top = matmul(spread[...], upstream[...]).astype(bf16)
    count = win.shape[0] // cells
    width = win.shape[1] // 3

    @pl.when(pl.program_id(0) == 0)
    def _():
        bias_sum[...] = jnp.zeros_like(bias_sum)

    results = []
    for j in range(count):
        part = win[j * cells : (j + 1) * cells]
        query, key, value = part[:, :width], part[:, width : 2 * width], part[:, 2 * width :]
        given = top[j * cells : (j + 1) * cells]
        mask = slots[j * heads * cells : (j + 1) * heads * cells, :] + rows[0]
        stacked, probs = window_probs(query, key, mask, heads, head_size, scale)
        given = jnp.concatenate(
            [given * head_mask(h, head_size, width, 1.0) for h in range(heads)], axis=0
        )
        dprobs = right_tmul(given, value)
        inner = jnp.sum(probs * dprobs, axis=-1, keepdims=True)
        dscores = (probs * (dprobs - inner)).astype(bf16)
        bias_sum[...] += dscores.astype(f32)
        dquery = None
        for h in range(heads):
            term = matmul(
                dscores[h * cells : (h + 1) * cells], key * head_mask(h, head_size, width, scale)
            )
            dquery = term if dquery is None else dquery + term
        dkey = left_tmul(dscores, stacked)
        dvalue = left_tmul(probs.astype(bf16), given)
        results.append(
            jnp.concatenate([dquery.astype(bf16), dkey.astype(bf16), dvalue.astype(bf16)], axis=1)
        )
    out[...] = matmul(gathered[...], jnp.concatenate(results, axis=0)).astype(bf16)

    @pl.when(pl.program_id(0) == pl.num_programs(0) - 1)
    def _():
        bias_out[...] = bias_sum[...]


def query_scores(query, keys_vis, keys_qry, causal, mask):
    masked = query * mask
    return masked, right_tmul(masked, keys_vis), right_tmul(masked, keys_qry) + causal


def joint_softmax(score_vis, score_qry):
    peak = jnp.maximum(
        jnp.max(score_vis, axis=-1, keepdims=True), jnp.max(score_qry, axis=-1, keepdims=True)
    )
    mass_vis = jnp.exp(score_vis - peak)
    mass_qry = jnp.exp(score_qry - peak)
    inverse = 1.0 / (
        jnp.sum(mass_vis, axis=-1, keepdims=True) + jnp.sum(mass_qry, axis=-1, keepdims=True)
    )
    return mass_vis * inverse, mass_qry * inverse


def query_forward_kernel(
    heads, head_size, scale, query, keys_qry, values_qry, keys_vis, values_vis, causal, out
):
    width = query.shape[1]
    total = None
    for h in range(heads):
        _, score_vis, score_qry = query_scores(
            query[...], keys_vis[...], keys_qry[...], causal[...], head_mask(h, head_size, width, scale)
        )
        prob_vis, prob_qry = joint_softmax(score_vis, score_qry)
        mask = head_mask(h, head_size, width, 1.0)
        term = matmul(prob_vis.astype(bf16), values_vis[...] * mask)
        term = term + matmul(prob_qry.astype(bf16), values_qry[...] * mask)
        total = term if total is None else total + term
    out[...] = total.astype(bf16)[:, : out.shape[1]]


def query_backward_kernel(
    heads,
    head_size,
    scale,
    query,
    keys_qry,
    values_qry,
    keys_vis,
    values_vis,
    causal,
    upstream,
    dquery,
    dkeys_qry,
    dvalues_qry,
    dkeys_vis,
    dvalues_vis,
):
    width = query.shape[1]
    sums = [None] * 5

    def add(place, term):
        sums[place] = term if sums[place] is None else sums[place] + term

    for h in range(heads):
        masked, score_vis, score_qry = query_scores(
            query[...], keys_vis[...], keys_qry[...], causal[...], head_mask(h, head_size, width, scale)
        )
        prob_vis, prob_qry = joint_softmax(score_vis, score_qry)
        given = upstream[...] * head_mask(h, head_size, width, 1.0)
        dprob_vis = right_tmul(given, values_vis[...])
        dprob_qry = right_tmul(given, values_qry[...])
        inner = jnp.sum(prob_vis * dprob_vis, axis=-1, keepdims=True) + jnp.sum(
            prob_qry * dprob_qry, axis=-1, keepdims=True
        )
        dscore_vis = (prob_vis * (dprob_vis - inner)).astype(bf16)
        dscore_qry = (prob_qry * (dprob_qry - inner)).astype(bf16)
        mask = head_mask(h, head_size, width, scale)
        add(0, matmul(dscore_vis, keys_vis[...] * mask) + matmul(dscore_qry, keys_qry[...] * mask))
        add(1, left_tmul(dscore_qry, masked))
        add(2, left_tmul(prob_qry.astype(bf16), given))
        add(3, left_tmul(dscore_vis, masked))
        add(4, left_tmul(prob_vis.astype(bf16), given))
    for ref, value in zip((dquery, dkeys_qry, dvalues_qry, dkeys_vis, dvalues_vis), sums):
        ref[...] = value.astype(bf16)


def cross_forward_kernel(heads, head_size, scale, query, keys, values, live, out):
    width = query.shape[1]
    total = None
    for h in range(heads):
        masked = query[...] * head_mask(h, head_size, width, scale)
        probs = softmax_rows(right_tmul(masked, keys[...]) + live[...])
        term = matmul(probs.astype(bf16), values[...] * head_mask(h, head_size, width, 1.0))
        total = term if total is None else total + term
    out[...] = total.astype(bf16)[:, : out.shape[1]]


def cross_backward_kernel(
    heads, head_size, scale, query, keys, values, live, upstream, dquery, dkeys, dvalues
):
    width = query.shape[1]

    @pl.when(pl.program_id(0) == 0)
    def _():
        dkeys[...] = jnp.zeros_like(dkeys)
        dvalues[...] = jnp.zeros_like(dvalues)

    total = None
    for h in range(heads):
        masked = query[...] * head_mask(h, head_size, width, scale)
        probs = softmax_rows(right_tmul(masked, keys[...]) + live[...])
        given = upstream[...] * head_mask(h, head_size, width, 1.0)
        dprobs = right_tmul(given, values[...])
        inner = jnp.sum(probs * dprobs, axis=-1, keepdims=True)
        dscores = (probs * (dprobs - inner)).astype(bf16)
        term = matmul(dscores, keys[...] * head_mask(h, head_size, width, scale))
        total = term if total is None else total + term
        dkeys[...] += left_tmul(dscores, masked)
        dvalues[...] += left_tmul(probs.astype(bf16), given)
    dquery[...] = total.astype(bf16)


def params():
    return pltpu.CompilerParams(vmem_limit_bytes=VMEM_BYTES)


def whole(shape):
    return pl.BlockSpec(shape, lambda *_: (0,) * len(shape))


def window_places(page_width):
    half = WS // 2
    columns = page_width // WS + 1
    matrix = np.zeros((columns * WS * WS, WS * page_width), np.float32)
    for j in range(columns):
        for r in range(WS):
            for c in range(WS):
                column = j * WS + c - half
                if 0 <= column < page_width:
                    matrix[j * WS * WS + r * WS + c, r * page_width + column] = 1.0
    return matrix


def bias_slots(table, regions, page_width):
    half = WS // 2
    columns = page_width // WS + 1
    heads = table.shape[0]
    flipped = table.reshape(heads, SPAN, SPAN)[:, ::-1, ::-1]
    wide = jnp.stack([flipped[:, :, WS - 1 - c : 2 * WS - 1 - c] for c in range(WS)], axis=1)
    wide = wide.reshape(heads, WS, SPAN * WS)
    bias = jnp.stack(
        [wide[:, :, (WS - 1 - r) * WS : (2 * WS - 1 - r) * WS] for r in range(WS)], axis=1
    ).reshape(heads, WS * WS, WS * WS)
    padded = jnp.pad(regions, (half, half), constant_values=-1).reshape(columns, WS)
    of_place = jnp.tile(padded, (1, WS))
    allowed = (of_place[:, :, None] == of_place[:, None, :]) & (of_place[:, None, :] >= 0)
    mask = jnp.where(allowed, 0.0, masked_fill).astype(f32)
    slots = bias[None] + mask[:, None]
    return slots.reshape(columns * heads * WS * WS, WS * WS)


def bias_gather(grad, heads):
    shaped = grad.reshape(heads, WS, WS, WS * WS)
    wide = sum(
        jnp.pad(shaped[:, r], ((0, 0), (0, 0), ((WS - 1 - r) * WS, r * WS))) for r in range(WS)
    ).reshape(heads, WS, SPAN, WS)
    flipped = wide[:, :, ::-1, ::-1]
    table = sum(jnp.pad(flipped[:, c], ((0, 0), (0, 0), (c, WS - 1 - c))) for c in range(WS))
    return table.reshape(heads, SPAN * SPAN)


def body(
    visual,
    queries,
    query_lengths,
    column_regions,
    gain_window,
    window_qkv,
    window_out,
    position_bias,
    gain_visual,
    gain_query,
    attend_query,
    attend_kv,
    attend_out,
    cross_query,
    cross_kv,
    cross_out,
    gain_feed,
    visual_up,
    visual_down,
    gain_query_feed,
    query_up,
    query_down,
    cotangent_visual,
    cotangent_query,
):
    shards = lax.axis_size("win")
    me = lax.axis_index("win")
    row_count, page_width, model = visual.shape[1:]
    own = row_count * page_width
    tokens = own * shards
    slots_count = queries.shape[1]
    heads = HEADS // shards
    head_size = model // HEADS
    part = heads * head_size
    wide = -(-part // LANES) * LANES
    scale = head_size ** (-0.5)
    half_cells = WS // 2 * page_width
    stripes = shards + 1
    stripe = WS * page_width

    def column_blocks(weight, pieces):
        step = weight.shape[1] // (pieces * shards)
        return [
            [weight[:, (s * shards + j) * step : (s * shards + j + 1) * step] for s in range(pieces)]
            for j in range(shards)
        ]

    def columns_here(*items):
        blocks = [column_blocks(w, n) for w, n in items]
        stack = jnp.stack(
            [jnp.concatenate(sum([b[j] for b in blocks], []), axis=1) for j in range(shards)]
        )
        return jnp.concatenate(in_order(trade(stack)), axis=0)

    def widen(weight, pieces):
        return jnp.concatenate(
            [pad_lanes(weight[:, s * part : (s + 1) * part], wide) for s in range(pieces)], axis=1
        )

    def narrow(weight, pieces):
        return [weight[:, s * wide : s * wide + part] for s in range(pieces)]

    vis_low = gather_blocks(visual[0].reshape(own, model))
    gains = jnp.stack(
        [gain_window, gain_visual, gain_query, gain_feed, gain_query_feed]
    )
    gain_rows = gather_blocks(gains[None])
    gain_order = in_order([gain_rows[xor_order(shards).index(k)] for k in range(shards)])
    gains_all = jnp.concatenate(gain_order, axis=1).astype(f32)
    g_window, g_visual, g_query, g_feed, g_qfeed = [gains_all[i] for i in range(5)]
    qkv_w = widen(columns_here((window_qkv, 3)), 3)
    mixed_w = columns_here((attend_kv, 2), (cross_query, 1), (attend_query, 1), (cross_kv, 2))
    vis_w = widen(mixed_w[:, : 3 * part], 3)
    qry_w = widen(
        jnp.concatenate([mixed_w[:, 3 * part : 4 * part], mixed_w[:, : 2 * part], mixed_w[:, 4 * part :]], axis=1),
        5,
    )
    outs = gather_blocks(jnp.stack([window_out, cross_out, attend_out])[None])
    outs = [outs[:, i].reshape(model, model) for i in range(3)]
    up_w = columns_here((visual_up, 1), (query_up, 1))
    hidden_count = up_w.shape[1] // 2
    vup_w, qup_w = up_w[:, :hidden_count], up_w[:, hidden_count:]
    top_low = gather_blocks(cotangent_visual[0].reshape(own, model))

    vis = vis_low.astype(f32)
    norm_win = norm_low(vis, g_window)
    packed = matmul(norm_win, qkv_w).astype(bf16)

    order = xor_order(shards)

    def to_page(tensor):
        blocks = tensor.reshape((shards, own) + tensor.shape[1:])
        place = jnp.asarray(np.argsort(order), jnp.int32)
        ordered = [pick(blocks, place[me ^ j]) for j in range(shards)]
        zeros = jnp.zeros((half_cells,) + tensor.shape[1:], tensor.dtype)
        return jnp.concatenate([zeros] + ordered + [zeros], axis=0)

    def from_page(tensor):
        blocks = tensor[half_cells : half_cells + tokens].reshape((shards, own) + tensor.shape[1:])
        return jnp.concatenate([pick(blocks, me ^ k) for k in order], axis=0)

    packed_page = to_page(packed)
    slots = bias_slots(position_bias.astype(f32), column_regions[0], page_width)
    places = window_places(page_width)
    spread = jnp.asarray(places, bf16)
    collect = jnp.asarray(places.T, bf16)
    row_mask = np.zeros((stripes, 1, WS * WS), np.float32)
    row_mask[0, :, : WS * WS // 2] = masked_fill
    row_mask[-1, :, WS * WS // 2 :] = masked_fill
    row_mask = jnp.asarray(row_mask)
    static = (heads, head_size, scale)
    window_specs = [
        whole(spread.shape),
        whole(collect.shape),
        whole(slots.shape),
        pl.BlockSpec((1, 1, WS * WS), lambda i: (i, 0, 0)),
    ]
    heads_page = pl.pallas_call(
        functools.partial(window_forward_kernel, *static),
        grid=(stripes,),
        in_specs=[pl.BlockSpec((stripe, 3 * wide), lambda i: (i, 0))] + window_specs,
        out_specs=pl.BlockSpec((stripe, part), lambda i: (i, 0)),
        out_shape=jax.ShapeDtypeStruct((stripes * stripe, part), bf16),
        compiler_params=params(),
    )(packed_page, spread, collect, slots, row_mask)
    heads_win = from_page(heads_page)

    def gather_features(tensor, by_token):
        parts = gather_blocks(tensor[None])
        columns = []
        for place in range(shards):
            piece = parts[place]
            if by_token:
                blocks = piece.reshape(shards, own, part)
                piece = jnp.concatenate([blocks[order.index(k ^ order[place])] for k in order], axis=0)
            columns.append(piece)
        return jnp.concatenate(columns, axis=1)

    mid = vis + matmul(gather_features(heads_win, True), outs[0])
    norm_vis = norm_low(mid, g_visual)
    proj_vis = matmul(norm_vis, vis_w).astype(bf16)

    query_in = queries[0].astype(f32)
    norm_qry = norm_low(query_in, g_query)
    proj_qry = matmul(norm_qry, qry_w).astype(bf16)
    length = query_lengths[0]
    slot_ids = jnp.arange(slots_count, dtype=jnp.int32)
    live = slot_ids < length
    live_mask = jnp.where(live, 0.0, masked_fill).astype(f32)[None]
    reach = (slot_ids[None, :] <= slot_ids[:, None]) & live[None, :]
    causal_mask = jnp.where(reach, 0.0, masked_fill).astype(f32)

    def qry_piece(i):
        return pl.BlockSpec((slots_count, wide), lambda *_: (0, i))

    def vis_piece(i):
        return pl.BlockSpec((tokens, wide), lambda *_: (0, i))

    query_specs = [
        qry_piece(0),
        qry_piece(1),
        qry_piece(2),
        vis_piece(0),
        vis_piece(1),
        whole(causal_mask.shape),
    ]
    query_args = (proj_qry, proj_qry, proj_qry, proj_vis, proj_vis, causal_mask)
    heads_qry = pl.pallas_call(
        functools.partial(query_forward_kernel, *static),
        grid=(1,),
        in_specs=query_specs,
        out_specs=whole((slots_count, part)),
        out_shape=jax.ShapeDtypeStruct((slots_count, part), bf16),
        compiler_params=params(),
    )(*query_args)
    query_mid = query_in + matmul(gather_features(heads_qry, False), outs[2])

    block = own
    cross_specs = [
        pl.BlockSpec((block, wide), lambda i: (i, 2)),
        qry_piece(3),
        qry_piece(4),
        whole(live_mask.shape),
    ]
    cross_args = (proj_vis, proj_qry, proj_qry, live_mask)
    heads_cross = pl.pallas_call(
        functools.partial(cross_forward_kernel, *static),
        grid=(tokens // block,),
        in_specs=cross_specs,
        out_specs=pl.BlockSpec((block, part), lambda i: (i, 0)),
        out_shape=jax.ShapeDtypeStruct((tokens, part), bf16),
        compiler_params=params(),
    )(*cross_args)
    late = mid + matmul(gather_features(heads_cross, True), outs[1])

    norm_feed = norm_low(late, g_feed)
    act_vis, slope_vis = gelu_both(matmul(norm_feed, vup_w))
    act_vis = act_vis.astype(bf16)
    visual_final = late[:own] + scatter_sum(matmul(act_vis, visual_down).astype(bf16))

    norm_qfeed = norm_low(query_mid, g_qfeed)
    act_qry, slope_qry = gelu_both(matmul(norm_qfeed, qup_w))
    act_qry = act_qry.astype(bf16)
    query_final = query_mid + total_sum(matmul(act_qry, query_down))

    dhid_qry = (right_tmul(cotangent_query[0], query_down) * slope_qry).astype(bf16)
    grad_query_down = left_tmul(act_qry, cotangent_query[0])
    grad_query_up = left_tmul(norm_qfeed, dhid_qry)
    dqfeed = total_sum(right_tmul(dhid_qry, qup_w))
    grad_qmid = cotangent_query[0].astype(f32) + norm_back(query_mid, g_qfeed, dqfeed)

    dhid_vis = (right_tmul(top_low, visual_down) * slope_vis).astype(bf16)
    grad_visual_down = left_tmul(act_vis, top_low)
    grad_visual_up = left_tmul(norm_feed, dhid_vis)
    dfeed = scatter_sum(right_tmul(dhid_vis, vup_w).astype(bf16))
    grad_late = cotangent_visual[0].reshape(own, model).astype(f32) + norm_back(
        late[:own], g_feed, dfeed
    )

    dz_attend = grad_qmid.astype(bf16)
    grad_attend_out = left_tmul(heads_qry, dz_attend)
    dheads_qry = pad_lanes(right_tmul(dz_attend, attend_out).astype(bf16), wide)
    qry_out = jax.ShapeDtypeStruct((slots_count, wide), bf16)
    vis_out = jax.ShapeDtypeStruct((tokens, wide), bf16)
    dq, dkq, dvq, dkv, dvv = pl.pallas_call(
        functools.partial(query_backward_kernel, *static),
        grid=(1,),
        in_specs=query_specs + [whole((slots_count, wide))],
        out_specs=[whole(qry_out.shape)] * 3 + [whole(vis_out.shape)] * 2,
        out_shape=[qry_out] * 3 + [vis_out] * 2,
        compiler_params=params(),
    )(*query_args, dheads_qry)

    dz_cross = gather_blocks(grad_late.astype(bf16))
    grad_cross_out = left_tmul(heads_cross, dz_cross)
    dheads_cross = pad_lanes(right_tmul(dz_cross, cross_out).astype(bf16), wide)
    dcq, dck, dcv = pl.pallas_call(
        functools.partial(cross_backward_kernel, *static),
        grid=(tokens // block,),
        in_specs=cross_specs + [pl.BlockSpec((block, wide), lambda i: (i, 0))],
        out_specs=[pl.BlockSpec((block, wide), lambda i: (i, 0))]
        + [whole((slots_count, wide))] * 2,
        out_shape=[vis_out] + [jax.ShapeDtypeStruct((slots_count, wide), f32)] * 2,
        compiler_params=params(),
    )(*cross_args, dheads_cross)
    dproj_vis = jnp.concatenate([dkv, dvv, dcq], axis=1)
    dproj_qry = jnp.concatenate([dq, dkq, dvq, dck.astype(bf16), dcv.astype(bf16)], axis=1)
    grad_vis_w = left_tmul(norm_vis, dproj_vis)
    grad_qry_w = left_tmul(norm_qry, dproj_qry)

    dnorm_vis = scatter_sum(right_tmul(dproj_vis, vis_w).astype(bf16))
    grad_mid = grad_late + norm_back(mid[:own], g_visual, dnorm_vis)
    dnorm_qry = total_sum(right_tmul(dproj_qry, qry_w))
    query_back = (grad_qmid + norm_back(query_in, g_query, dnorm_qry)).astype(bf16)

    dz_window = gather_blocks(grad_mid.astype(bf16))
    grad_window_out = left_tmul(heads_win, dz_window)
    dheads_win = to_page(pad_lanes(right_tmul(dz_window, window_out).astype(bf16), wide))
    dpacked_page, bias_grad = pl.pallas_call(
        functools.partial(window_backward_kernel, *static),
        grid=(stripes,),
        in_specs=[
            pl.BlockSpec((stripe, 3 * wide), lambda i: (i, 0)),
            pl.BlockSpec((stripe, wide), lambda i: (i, 0)),
        ]
        + window_specs,
        out_specs=[
            pl.BlockSpec((stripe, 3 * wide), lambda i: (i, 0)),
            whole((heads * WS * WS, WS * WS)),
        ],
        out_shape=[
            jax.ShapeDtypeStruct((stripes * stripe, 3 * wide), bf16),
            jax.ShapeDtypeStruct((heads * WS * WS, WS * WS), f32),
        ],
        scratch_shapes=[pltpu.VMEM((heads * WS * WS, WS * WS), f32)],
        compiler_params=params(),
    )(packed_page, dheads_win, spread, collect, slots, row_mask)
    dpacked = from_page(dpacked_page)
    grad_qkv_w = left_tmul(norm_win, dpacked)
    dnorm_win = scatter_sum(right_tmul(dpacked, qkv_w).astype(bf16))
    visual_back = (grad_mid + norm_back(vis[:own], g_window, dnorm_win)).astype(bf16)

    def gain_grad(gain, *pairs):
        return sum(jnp.sum(w.astype(f32) * g, axis=1) for w, g in pairs) / gain

    gain_grads = jnp.stack(
        [
            gain_grad(g_window, (qkv_w, grad_qkv_w)),
            gain_grad(g_visual, (vis_w, grad_vis_w)),
            gain_grad(g_query, (qry_w, grad_qry_w)),
            gain_grad(g_feed, (vup_w, grad_visual_up)),
            gain_grad(g_qfeed, (qup_w, grad_query_up)),
        ]
    )
    small = jnp.concatenate(
        [
            tiny_sum(gain_grads, ("win",)).reshape(-1),
            bias_gather(bias_grad, heads).reshape(-1),
        ]
    )
    small = tiny_sum(small, ("page",))
    gain_total = lax.dynamic_slice_in_dim(
        small[: 5 * model].reshape(5, model), me * (model // shards), model // shards, 1
    )
    bias_total = small[5 * model :].reshape(heads, SPAN * SPAN)

    def rows_here(*blocks):
        cols = jnp.concatenate([b.astype(bf16) for b in blocks], axis=1)
        stack = cols.reshape(shards, cols.shape[0] // shards, cols.shape[1])
        return jnp.concatenate(trade(stack), axis=0)

    def laid_out(blocks, widths):
        ordered = in_order(blocks.reshape((shards, blocks.shape[0] // shards, blocks.shape[1])))
        result, start = [], 0
        for step, pieces in widths:
            result.append(
                jnp.concatenate(
                    [
                        b[:, start + s * step : start + (s + 1) * step]
                        for s in range(pieces)
                        for b in ordered
                    ],
                    axis=1,
                ).astype(f32)
            )
            start += step * pieces
        return result

    vup_t, vdown_t = page_total(rows_here(grad_visual_up), grad_visual_down.astype(bf16))
    qup_t, qdown_t = page_total(rows_here(grad_query_up), grad_query_down.astype(bf16))
    gk, gv, gcq = narrow(grad_vis_w, 3)
    gaq, gkq, gvq, gck, gcv = narrow(grad_qry_w, 5)
    mixed_t, attend_t = page_total(
        rows_here(gk + gkq, gv + gvq, gcq, gaq, gck, gcv),
        jnp.concatenate([grad_cross_out, grad_attend_out], axis=0).astype(bf16),
    )
    qkv_t, wout_t = page_total(rows_here(*narrow(grad_qkv_w, 3)), grad_window_out.astype(bf16))
    (out_qkv,) = laid_out(qkv_t, [(part, 3)])
    out_akv, out_cq, out_aq, out_ckv = laid_out(mixed_t, [(part, 2), (part, 1), (part, 1), (part, 2)])
    (out_vup,) = laid_out(vup_t, [(hidden_count, 1)])
    (out_qup,) = laid_out(qup_t, [(hidden_count, 1)])
    rows = model // shards

    return (
        visual_final.reshape(1, row_count, page_width, model).astype(bf16),
        query_final.reshape(1, slots_count, model).astype(bf16),
        visual_back.reshape(1, row_count, page_width, model),
        query_back.reshape(1, slots_count, model),
        gain_total[0],
        out_qkv,
        wout_t.astype(f32),
        bias_total,
        gain_total[1],
        gain_total[2],
        out_aq,
        out_akv,
        attend_t[rows:].astype(f32),
        out_cq,
        out_ckv,
        attend_t[:rows].astype(f32),
        gain_total[3],
        out_vup,
        vdown_t.astype(f32),
        gain_total[4],
        out_qup,
        qdown_t.astype(f32),
    )


def solution(mesh):
    tokens_spec = P("page", "win", None, None)
    slots_spec = P("page", None, None)
    gain, weight = P("win"), P("win", None)
    parameters = (
        gain, weight, weight, weight, gain, gain, weight, weight, weight, weight, weight, weight,
        gain, weight, weight, gain, weight, weight,
    )
    return jax.shard_map(
        body,
        mesh=mesh,
        in_specs=(tokens_spec, slots_spec, P("page"), P("page", None)) + parameters + (tokens_spec, slots_spec),
        out_specs=(tokens_spec, slots_spec, tokens_spec, slots_spec) + parameters,
        check_vma=False,
    )
```

```python
import functools

import jax
import jax.numpy as jnp
import numpy as np
from jax import lax
from jax.experimental import pallas as pl
from jax.experimental.pallas import tpu as pltpu
from jax.sharding import PartitionSpec as P

HEADS = 12
WS = 12
SPAN = 2 * WS - 1
LANES = 256

epsilon = 1e-05
masked_fill = -1000000000.0
bf16 = jnp.bfloat16
f32 = jnp.float32
VMEM_BYTES = 48 * 1024 * 1024


def swap(tensor, axis, bit):
    count = lax.axis_size(axis)
    return lax.ppermute(tensor, axis, [(i, i ^ bit) for i in range(count)])


def bits_of(count):
    bits = []
    while count > 1:
        count //= 2
        bits.append(count)
    return bits


def gather_blocks(block, axis="win"):
    for bit in bits_of(lax.axis_size(axis)):
        block = jnp.concatenate([block, swap(block, axis, bit)], axis=0)
    return block


def scatter_sum(parts, axis="win"):
    bits = bits_of(lax.axis_size(axis))
    for bit in reversed(bits):
        half = parts.shape[0] // 2
        arrived = swap(parts[half:].astype(bf16), axis, bit)
        parts = parts[:half].astype(f32) + arrived.astype(f32)
    return parts


def total_sum(part, axis="win"):
    for bit in reversed(bits_of(lax.axis_size(axis))):
        mine = lax.reduce_precision(part.astype(f32), 8, 7)
        last = mine.astype(bf16)
        part = mine + swap(last, axis, bit).astype(f32)
    return part, last


def tiny_sum(part, axes):
    for axis in axes:
        for bit in reversed(bits_of(lax.axis_size(axis))):
            part = part + swap(part, axis, bit)
    return part


def pick(stack, index):
    return lax.dynamic_index_in_dim(stack, index, 0, False)


def trade(stack, axis="win"):
    count = lax.axis_size(axis)
    me = lax.axis_index(axis)
    return [pick(stack, me)] + [swap(pick(stack, me ^ k), axis, k) for k in range(1, count)]


def in_order(blocks, axis="win"):
    me = lax.axis_index(axis)
    stack = jnp.stack(blocks) if isinstance(blocks, (list, tuple)) else blocks
    return [pick(stack, me ^ j) for j in range(lax.axis_size(axis))]


def xor_order(count):
    order = [0]
    for bit in bits_of(count):
        order = order + [k ^ bit for k in order]
    return order


def rounded(tensor):
    return lax.reduce_precision(tensor, 8, 7)


def add_low(left, right):
    return rounded(left.astype(f32) + right.astype(f32)).astype(bf16)


LINE = 4


def line_swap(tensor, k):
    pairs = [(2 * a + x, 2 * (a ^ k) + x) for a in range(LINE) for x in (0, 1)]
    return lax.ppermute(tensor, "page", pairs)


def line_scatter(parts, depth):
    terms = [pick(parts, depth)] + [line_swap(pick(parts, depth ^ k), k) for k in range(1, LINE)]
    return rounded(total([t.astype(f32) for t in terms])).astype(bf16)


def line_gather(own):
    return [own] + [line_swap(own, k) for k in range(1, LINE)]


def exchange(blocks):
    return [blocks[0]] + [swap(blocks[k], "win", k) for k in range(1, len(blocks))]


def tie(first, *later):
    return lax.optimization_barrier((first,) + later)[1:]


def gather_four(block, axis="win"):
    count = lax.axis_size(axis)
    parts = [block]
    for bit in bits_of(count):
        parts = parts + [swap(p, axis, bit) for p in parts]
    return parts


def scatter_pieces(keep, send):
    bits = bits_of(lax.axis_size("win"))
    arrived = swap(send, "win", bits[-1])
    half = keep.shape[0] // 2
    second = (keep[half:].astype(f32) + arrived[half:].astype(f32)).astype(bf16)
    return (keep, arrived, swap(second, "win", bits[0])), second


def normalise(tensor):
    centre = tensor - jnp.mean(tensor, axis=-1, keepdims=True)
    spread = lax.rsqrt(jnp.mean(centre * centre, axis=-1, keepdims=True) + epsilon)
    return centre * spread, spread


def norm_low(tensor, gain):
    return (normalise(tensor)[0] * gain).astype(bf16)


def norm_back(tensor, gain, upstream):
    unit, spread = normalise(tensor)
    scaled = upstream * gain
    return spread * (
        scaled
        - jnp.mean(scaled, axis=-1, keepdims=True)
        - unit * jnp.mean(scaled * unit, axis=-1, keepdims=True)
    )


def gelu_both(hidden):
    phi = 0.5 * (1.0 + lax.erf(hidden * np.float32(np.sqrt(0.5))))
    density = jnp.exp(-0.5 * hidden * hidden) * np.float32(1.0 / np.sqrt(2.0 * np.pi))
    return hidden * phi, phi + hidden * density


def matmul(left, right):
    return jnp.dot(left, right, preferred_element_type=f32)


def left_tmul(left, right):
    return lax.dot_general(left, right, (((0,), (0,)), ((), ())), preferred_element_type=f32)


def right_tmul(left, right):
    return lax.dot_general(left, right, (((1,), (1,)), ((), ())), preferred_element_type=f32)


def pad_lanes(tensor, width):
    return jnp.pad(tensor, ((0, 0), (0, width - tensor.shape[1])))


def head_mask(head, head_size, width, scale):
    lane = lax.broadcasted_iota(jnp.int32, (1, width), 1)
    inside = (lane >= head * head_size) & (lane < (head + 1) * head_size)
    return jnp.where(inside, np.float32(scale), np.float32(0.0)).astype(bf16)


def softmax_rows(scores):
    peak = jnp.max(scores, axis=-1, keepdims=True)
    mass = jnp.exp(scores - peak)
    return mass * (1.0 / jnp.sum(mass, axis=-1, keepdims=True))


def by_head(tensor, heads, head_size, scale):
    return [tensor * head_mask(h, head_size, tensor.shape[1], scale) for h in range(heads)]


def total(terms):
    result = terms[0]
    for term in terms[1:]:
        result = result + term
    return result


def window_rows(spread_top, spread_low, before, after, window, cells):
    half = cells // 2
    return jnp.concatenate(
        [spread_top[window * half : (window + 1) * half], spread_low[window * half : (window + 1) * half]],
        axis=0,
    ).astype(bf16)


def pack_lanes(tensor, wide):
    rows, part = tensor.shape
    first = packed_rows(rows, part, wide)
    spare = wide - part
    tail = tensor[first:]
    side = [tail[:, s : s + spare] for s in range(0, part, spare)]
    rest = first - tail.shape[0] * len(side)
    side.append(jnp.zeros((rest, spare), tensor.dtype))
    return jnp.concatenate([tensor[:first], jnp.concatenate(side, axis=0)], axis=1)


def packed_rows(rows, part, wide):
    return -(-rows * part // (wide * 16)) * 16


def unpack_lanes(packed, rows, part):
    first, wide = packed.shape
    spare, tail = wide - part, rows - first
    side = packed[:, part:]
    last = jnp.concatenate([side[s * tail : (s + 1) * tail] for s in range(part // spare)], axis=1)
    return jnp.concatenate([packed[:, :part], last], axis=0)


def pick_block(blocks, place, target):
    for k, block in enumerate(blocks):

        @pl.when(place == k)
        def _(block=block):
            target[...] = block[: target.shape[0], :]


def window_forward_kernel(
    heads, head_size, scale, place, near, second, third, fourth, chunk, top_in, low_in, top_out, low_out,
    slots, rows, visual, weight, gains, norm, packed, mixed, before, after, held, chosen,
):
    step, last = pl.program_id(0), pl.num_programs(0) - 1
    cells = WS * WS
    half = cells // 2
    width = weight.shape[1] // 3
    blocks = (near, second, third, fourth)
    shards = len(blocks)
    me = place[shards]
    own, piece = chosen.shape[0], chunk.shape[0]

    @pl.when(step == 0)
    def _():
        before[...] = jnp.zeros_like(before)
        held[...] = jnp.zeros_like(held)
        order = xor_order(shards)
        starts = (None, own, own, own + piece)
        for p, k in enumerate(order):
            source = chunk[...] if p == 0 else blocks[p][starts[p] : starts[p] + piece, :]
            weight[pl.ds(pl.multiple_of((me ^ k) * piece, piece), piece), :] = source
        for device in range(shards):

            @pl.when(me == device)
            def _(device=device):
                lines = [None] * shards
                for p, k in enumerate(order):
                    lines[device ^ k] = blocks[p][blocks[p].shape[0] - 16 :, :piece].astype(f32)
                gains[...] = jnp.concatenate(lines, axis=1)

    @pl.when(step < last)
    def _():
        pick_block(blocks, place[jnp.minimum(step, last - 1)], chosen)
        visual[...] = chosen[...]
        low = norm_low(chosen[...].astype(f32), gains[0:1, :])
        norm[...] = low
        after[...] = matmul(low, weight[...]).astype(bf16)
        packed[...] = after[...]

    @pl.when(step == last)
    def _():
        after[...] = jnp.zeros_like(after)

    top = matmul(top_in[...], before[...])
    low = matmul(low_in[...], after[...])
    upper, lower = [], []
    for j in range(top.shape[0] // half):
        part = window_rows(top, low, before, after, j, cells)
        query, key, value = part[:, :width], part[:, width : 2 * width], part[:, 2 * width :]
        stacked = jnp.concatenate(by_head(query, heads, head_size, scale), axis=0)
        mask = slots[j * heads * cells : (j + 1) * heads * cells, :] + rows[0]
        probs = softmax_rows(right_tmul(stacked, key) + mask).astype(bf16)
        values = by_head(value, heads, head_size, 1.0)
        result = total([matmul(probs[h * cells : (h + 1) * cells], values[h]) for h in range(heads)])
        upper.append(result[:half])
        lower.append(result[half:])
    above = matmul(top_out[...], jnp.concatenate(upper, axis=0).astype(bf16))
    below = matmul(low_out[...], jnp.concatenate(lower, axis=0).astype(bf16))

    @pl.when(step > 0)
    def _():
        block = jnp.concatenate([held[...], above], axis=0)
        mixed[...] = pack_lanes(block[:, : heads * head_size], width).astype(bf16)

    held[...] = below
    before[...] = after[...]


def window_backward_kernel(
    heads, head_size, scale, place, near, second, third, fourth, packed, mixed, weight_out, weight, top_in,
    low_in, top_out, low_out, slots, rows, grads, dnorm, bias_out, out_grad, before, after, top_before,
    top_after, held, upper, lower, upstream,
):
    step, last = pl.program_id(0), pl.num_programs(0) - 1
    cells = WS * WS
    half = cells // 2
    width = weight.shape[1] // 3

    @pl.when(step == 0)
    def _():
        before[...] = jnp.zeros_like(before)
        top_before[...] = jnp.zeros_like(top_before)
        bias_out[...] = jnp.zeros_like(bias_out)
        out_grad[...] = jnp.zeros_like(out_grad)
        held[...] = jnp.zeros_like(held)

    @pl.when(step < last)
    def _():
        pick_block((near, second, third, fourth), place[jnp.minimum(step, last - 1)], upstream)
        after[...] = packed[...]
        top_after[...] = right_tmul(upstream[...], weight_out[...]).astype(bf16)
        whole_heads = unpack_lanes(mixed[...], upstream.shape[0], heads * head_size)
        out_grad[...] += left_tmul(whole_heads, upstream[...])

    @pl.when(step == last)
    def _():
        after[...] = jnp.zeros_like(after)
        top_after[...] = jnp.zeros_like(top_after)

    top = matmul(top_in[...], before[...])
    low = matmul(low_in[...], after[...])
    given_top = matmul(top_in[...], top_before[...])
    given_low = matmul(low_in[...], top_after[...])
    for j in range(top.shape[0] // half):
        part = window_rows(top, low, before, after, j, cells)
        given = window_rows(given_top, given_low, before, after, j, cells)
        query, key, value = part[:, :width], part[:, width : 2 * width], part[:, 2 * width :]
        stacked = jnp.concatenate(by_head(query, heads, head_size, scale), axis=0)
        mask = slots[j * heads * cells : (j + 1) * heads * cells, :] + rows[0]
        probs = softmax_rows(right_tmul(stacked, key) + mask)
        given = jnp.concatenate(by_head(given, heads, head_size, 1.0), axis=0)
        dprobs = right_tmul(given, value)
        inner = jnp.sum(probs * dprobs, axis=-1, keepdims=True)
        dscores = (probs * (dprobs - inner)).astype(bf16)
        bias_out[...] += dscores.astype(f32)
        keys = by_head(key, heads, head_size, scale)
        dquery = total([matmul(dscores[h * cells : (h + 1) * cells], keys[h]) for h in range(heads)])
        dkey = left_tmul(dscores, stacked)
        dvalue = left_tmul(probs.astype(bf16), given)
        for s, result in enumerate((dquery, dkey, dvalue)):
            upper[j * half : (j + 1) * half, s * width : (s + 1) * width] = result[:half]
            lower[j * half : (j + 1) * half, s * width : (s + 1) * width] = result[half:]
    above = matmul(top_out[...], upper[...].astype(bf16))
    below = matmul(low_out[...], lower[...].astype(bf16))

    block = jnp.concatenate([held[...], above], axis=0).astype(bf16)
    grads[...] = block
    held[...] = below
    dnorm[...] = right_tmul(block, weight[...]).astype(bf16)
    before[...] = after[...]
    top_before[...] = top_after[...]


def middle_kernel(
    heads, head_size, scale, visual, own, second, third, fourth, out_own, out_second, out_third, out_fourth,
    gains, weight, keys, values, live, mid, norm, proj, mixed,
):
    pieces = (own, second, third, fourth)
    weights = (out_own, out_second, out_third, out_fourth)
    part = heads * head_size
    result = visual[...].astype(f32) + total(
        [matmul(unpack_lanes(p[...], mid.shape[0], part), w[...]) for p, w in zip(pieces, weights)]
    )
    mid[...] = result
    low = norm_low(result, gains[1:2, :])
    norm[...] = low
    packed = matmul(low, weight[...]).astype(bf16)
    proj[...] = packed
    width = keys.shape[1]
    query = by_head(packed[:, 2 * width :], heads, head_size, scale)
    value = by_head(values[...], heads, head_size, 1.0)
    terms = []
    for h in range(heads):
        probs = softmax_rows(right_tmul(query[h], keys[...]) + live[...])
        terms.append(matmul(probs.astype(bf16), value[h]))
    mixed[...] = pack_lanes(total(terms)[:, :part], width).astype(bf16)


def feed_kernel(
    part, place, mid, own, second, third, fourth, weight_out, gains, up, down, cotangent,
    late, norm, act, dhidden, keep, send,
):
    step, halfway = pl.program_id(0), pl.num_programs(0) // 2
    pieces = (own, second, third, fourth)
    terms = []
    for piece, k in zip(pieces, xor_order(len(pieces))):
        rows = weight_out[pl.ds(pl.multiple_of((place[0] ^ k) * part, part), part), :]
        terms.append(matmul(unpack_lanes(piece[...], mid.shape[0], part), rows))
    result = mid[...] + total(terms)

    @pl.when(step == 0)
    def _():
        late[...] = result

    low = norm_low(result, gains[3:4, :])
    norm[...] = low
    value, slope = gelu_both(matmul(low, up[...]))
    act[...] = value.astype(bf16)
    back = (right_tmul(cotangent[...], down[...]) * slope).astype(bf16)
    dhidden[...] = back
    dnorm = right_tmul(back, up[...]).astype(bf16)

    @pl.when(step < halfway)
    def _():
        keep[...] = dnorm

    @pl.when(step >= halfway)
    def _():
        send[...] = dnorm


def query_scores(query, keys_vis, keys_qry, causal, mask):
    masked = query * mask
    return masked, right_tmul(masked, keys_vis), right_tmul(masked, keys_qry) + causal


def joint_softmax(score_vis, score_qry):
    peak = jnp.maximum(
        jnp.max(score_vis, axis=-1, keepdims=True), jnp.max(score_qry, axis=-1, keepdims=True)
    )
    mass_vis = jnp.exp(score_vis - peak)
    mass_qry = jnp.exp(score_qry - peak)
    inverse = 1.0 / (
        jnp.sum(mass_vis, axis=-1, keepdims=True) + jnp.sum(mass_qry, axis=-1, keepdims=True)
    )
    return mass_vis * inverse, mass_qry * inverse


def query_forward_kernel(
    heads, head_size, scale, query, keys_qry, values_qry, keys_vis, values_vis, causal, out
):
    width = query.shape[1]
    terms = []
    for h in range(heads):
        _, score_vis, score_qry = query_scores(
            query[...], keys_vis[...], keys_qry[...], causal[...], head_mask(h, head_size, width, scale)
        )
        prob_vis, prob_qry = joint_softmax(score_vis, score_qry)
        mask = head_mask(h, head_size, width, 1.0)
        terms.append(matmul(prob_vis.astype(bf16), values_vis[...] * mask))
        terms.append(matmul(prob_qry.astype(bf16), values_qry[...] * mask))
    out[...] = total(terms).astype(bf16)[:, : out.shape[1]]


def query_backward_kernel(
    heads, head_size, scale, query, keys_qry, values_qry, keys_vis, values_vis, causal, upstream,
    dquery, dkeys_qry, dvalues_qry, dkeys_vis, dvalues_vis,
):
    width = query.shape[1]
    sums = [[], [], [], [], []]
    for h in range(heads):
        masked, score_vis, score_qry = query_scores(
            query[...], keys_vis[...], keys_qry[...], causal[...], head_mask(h, head_size, width, scale)
        )
        prob_vis, prob_qry = joint_softmax(score_vis, score_qry)
        given = upstream[...] * head_mask(h, head_size, width, 1.0)
        dprob_vis = right_tmul(given, values_vis[...])
        dprob_qry = right_tmul(given, values_qry[...])
        inner = jnp.sum(prob_vis * dprob_vis, axis=-1, keepdims=True) + jnp.sum(
            prob_qry * dprob_qry, axis=-1, keepdims=True
        )
        dscore_vis = (prob_vis * (dprob_vis - inner)).astype(bf16)
        dscore_qry = (prob_qry * (dprob_qry - inner)).astype(bf16)
        mask = head_mask(h, head_size, width, scale)
        sums[0].append(matmul(dscore_vis, keys_vis[...] * mask))
        sums[0].append(matmul(dscore_qry, keys_qry[...] * mask))
        sums[1].append(left_tmul(dscore_qry, masked))
        sums[2].append(left_tmul(prob_qry.astype(bf16), given))
        sums[3].append(left_tmul(dscore_vis, masked))
        sums[4].append(left_tmul(prob_vis.astype(bf16), given))
    for ref, terms in zip((dquery, dkeys_qry, dvalues_qry, dkeys_vis, dvalues_vis), sums):
        ref[...] = total(terms).astype(bf16)


def cross_backward_kernel(
    heads, head_size, scale, proj, keys, values, live, near, second, third, fourth, weight_out, mixed,
    dkeys_vis, dvalues_vis, weight, dproj, dkeys, dvalues, out_grad, keep, send, upstream,
):
    step, halfway = pl.program_id(0), pl.num_programs(0) // 2
    width = keys.shape[1]

    @pl.when(step == 0)
    def _():
        dkeys[...] = jnp.zeros_like(dkeys)
        dvalues[...] = jnp.zeros_like(dvalues)
        out_grad[...] = jnp.zeros_like(out_grad)

    pick_block((near, second, third, fourth), step, upstream)
    out_grad[...] += left_tmul(unpack_lanes(mixed[...], upstream.shape[0], heads * head_size), upstream[...])
    top = right_tmul(upstream[...], weight_out[...]).astype(bf16)
    query = by_head(proj[:, 2 * width :], heads, head_size, scale)
    given = by_head(top, heads, head_size, 1.0)
    scaled = by_head(keys[...], heads, head_size, scale)
    terms = []
    for h in range(heads):
        probs = softmax_rows(right_tmul(query[h], keys[...]) + live[...])
        dprobs = right_tmul(given[h], values[...])
        inner = jnp.sum(probs * dprobs, axis=-1, keepdims=True)
        dscores = (probs * (dprobs - inner)).astype(bf16)
        terms.append(matmul(dscores, scaled[h]))
        dkeys[...] += left_tmul(dscores, query[h])
        dvalues[...] += left_tmul(probs.astype(bf16), given[h])
    block = jnp.concatenate([dkeys_vis[...], dvalues_vis[...], total(terms).astype(bf16)], axis=1)
    dproj[...] = block
    dnorm = right_tmul(block, weight[...]).astype(bf16)

    @pl.when(step < halfway)
    def _():
        keep[...] = dnorm

    @pl.when(step >= halfway)
    def _():
        send[...] = dnorm


def norm_back_kernel(line, tensor, gains, first, second, third, residual, *outs):
    upstream = first[...].astype(f32) + second[...].astype(f32) + third[...].astype(f32)
    gain = gains[line : line + 1, :]
    result = residual[...].astype(f32) + norm_back(tensor[...].astype(f32), gain, upstream)
    for out in outs:
        out[...] = result.astype(out.dtype)


def split_columns_kernel(shards, pieces, place, *refs):
    weights, outs = refs[: len(pieces)], refs[len(pieces) :]
    for me in range(shards):

        @pl.when(place[0] == me)
        def _(me=me):
            for k in range(shards):
                j = me ^ k
                blocks = []
                for weight, count in zip(weights, pieces):
                    step = weight.shape[1] // (count * shards)
                    for s in range(count):
                        start = (s * shards + j) * step
                        blocks.append(weight[:, start : start + step])
                outs[k][...] = jnp.concatenate(blocks, axis=1)


def join_rows_kernel(shards, part, wide, place, *refs):
    blocks, out = refs[:shards], refs[shards]
    rows = blocks[0].shape[0]
    for k in range(shards):
        block = blocks[k][...]
        if wide != part:
            gap = jnp.zeros((rows, wide - part), block.dtype)
            columns = []
            for start in range(0, block.shape[1], part):
                columns += [block[:, start : start + part], gap]
            block = jnp.concatenate(columns, axis=1)
        out[pl.ds(pl.multiple_of((place[0] ^ k) * rows, rows), rows), :] = block


def entry_kernel(shards, pieces, wide, place, visual, weight, gains, to_far, to_near, chunk):
    own, rows = visual.shape[0], weight.shape[0]
    part = weight.shape[1] // (pieces * shards)
    lanes = visual.shape[1]
    gap = jnp.zeros((rows, wide - part), bf16)
    line = jnp.concatenate([gains[...], jnp.zeros((gains.shape[0], lanes - gains.shape[1]), bf16)], axis=1)
    to_far[:own, :] = visual[...]
    to_near[:own, :] = visual[...]
    to_far[own + 2 * rows :, :] = line
    to_near[own + rows :, :] = line
    for me in range(shards):

        @pl.when(place[0] == me)
        def _(me=me):
            for k in range(shards):
                columns = []
                for s in range(pieces):
                    start = (s * shards + (me ^ k)) * part
                    columns += [weight[:, start : start + part], gap]
                block = jnp.concatenate(columns, axis=1)
                if k == 0:
                    chunk[...] = block
                elif k == 1:
                    to_near[own : own + rows, :] = block
                else:
                    to_far[own + (k - 2) * rows : own + (k - 1) * rows, :] = block


def share_kernel(shards, place, first, second, third, *refs):
    outs, stack = refs[:shards], refs[shards]
    rows, model = third.shape
    height = outs[0].shape[0]
    start = pl.multiple_of(place[1] * height, 16)
    if stack.shape[0] > 3 * rows:
        stack[3 * rows :, :] = jnp.zeros((stack.shape[0] - 3 * rows, model), bf16)
    stack[2 * rows : 3 * rows, :] = third[...]
    for me in range(shards):

        @pl.when(place[0] == me)
        def _(me=me):
            for k in range(shards):
                j = me ^ k
                stack[:rows, :] = first[:, j * model : (j + 1) * model]
                stack[rows : 2 * rows, :] = second[:, j * model : (j + 1) * model]
                outs[k][...] = stack[pl.ds(start, height), :]


def unshare_kernel(place, given, out):
    pages, shards, height, model = given.shape
    rows = model // shards
    for k in range(shards):
        block = given[:, k].reshape(pages * height, model)
        for i in range(3):
            start = pl.multiple_of(i * model + (place[0] ^ k) * rows, rows)
            out[pl.ds(start, rows), :] = block[i * rows : (i + 1) * rows]


GROUPS = 8


def feed_grads_kernel(shards, norm, dhidden, act, top, norm_qry, dhidden_qry, act_qry, top_qry, out):
    up_share = 2 * norm.shape[1] // (shards * GROUPS)
    down_share = 2 * act.shape[1] // GROUPS
    size = shards * up_share + down_share
    halfway = GROUPS // 2
    ups = ((norm, dhidden), (norm_qry, dhidden_qry))
    downs = ((act, top), (act_qry, top_qry))
    for k in range(2):

        @pl.when(pl.program_id(0) == k)
        def _(k=k):
            left, right = ups[k]
            result = left_tmul(left[...], right[...]).astype(bf16)
            for g in range(halfway):
                for j in range(shards):
                    start = (j * halfway + g) * up_share
                    to = (k * halfway + g) * size + j * up_share
                    out[to : to + up_share, :] = result[start : start + up_share]

        @pl.when(pl.program_id(0) == k + 2)
        def _(k=k):
            left, right = downs[k]
            result = left_tmul(left[...], right[...]).astype(bf16)
            for g in range(halfway):
                to = (k * halfway + g) * size + shards * up_share
                out[to : to + down_share, :] = result[g * down_share : (g + 1) * down_share]


def lay_out_feed_kernel(shards, place, given, up, up_qry, down, down_qry):
    halfway = GROUPS // 2
    up_share, down_share = up.shape[0] // halfway, down.shape[0] // halfway
    size, width = shards * up_share + down_share, given.shape[1]
    for me in range(shards):

        @pl.when(place[0] == me)
        def _(me=me):
            for g in range(GROUPS):
                out = (up, up_qry)[g // halfway]
                to = g % halfway * up_share
                for j in range(shards):
                    start = g * size + (me ^ j) * up_share
                    out[to : to + up_share, j * width : (j + 1) * width] = given[start : start + up_share, :].astype(f32)

    for g in range(GROUPS):
        out = (down, down_qry)[g // halfway]
        to, start = g % halfway * down_share, g * size + shards * up_share
        out[to : to + down_share, :] = given[start : start + down_share, :].astype(f32)


def split_halves_kernel(shards, part, wide, place, *refs):
    grads, keep, give = refs[:-2], refs[-2], refs[-1]
    rows = grads[0].shape[0] // shards
    half = rows // 2
    for k in range(shards):
        for out, side in ((keep, place[1]), (give, 1 - place[1])):
            start = pl.multiple_of((place[0] ^ k) * rows + side * half, half)
            columns = []
            for grad in grads:
                block = grad[pl.ds(start, half), :]
                columns += [block[:, c : c + part] for c in range(0, block.shape[1], wide)]
            out[k * half : (k + 1) * half, :] = jnp.concatenate(columns, axis=1).astype(bf16)


def lay_out_kernel(shards, pieces, halves, place, *refs):
    blocks, outs = refs[: 2 if halves else 1], refs[2 if halves else 1 :]
    rows = blocks[0].shape[0] // shards
    for me in range(shards):

        @pl.when(place[0] == me)
        def _(me=me):
            start = 0
            for out, count in zip(outs, pieces):
                step = out.shape[1] // (count * shards)
                for b, block in enumerate(blocks):
                    columns = []
                    for s in range(count):
                        for j in range(shards):
                            k = me ^ j
                            columns.append(
                                block[k * rows : (k + 1) * rows, start + s * step : start + (s + 1) * step]
                            )
                    result = jnp.concatenate(columns, axis=1).astype(f32)
                    if halves:
                        side = place[1] if b == 0 else 1 - place[1]
                        out[pl.ds(pl.multiple_of(side * rows, rows), rows), :] = result
                    else:
                        out[...] = result
                start += step * count


def kernel_call(function, grid, ins, outs, args, scratch=(), place=None, name=None, us=2):
    prefetch = () if place is None else (place,)
    return pl.pallas_call(
        function,
        grid_spec=pltpu.PrefetchScalarGridSpec(
            num_scalar_prefetch=len(prefetch),
            grid=grid,
            in_specs=ins,
            out_specs=[spec for spec, _ in outs],
            scratch_shapes=list(scratch),
        ),
        out_shape=[shape for _, shape in outs],
        compiler_params=pltpu.CompilerParams(vmem_limit_bytes=VMEM_BYTES),
        cost_estimate=pl.CostEstimate(flops=us * 10**6, bytes_accessed=10**3, transcendentals=0),
        name=name,
    )(*prefetch, *args)


def whole(shape):
    return pl.BlockSpec(tuple(shape), lambda *_: (0,) * len(shape))


def all_of(*arrays):
    return [whole(a.shape) for a in arrays]


def full_out(shape, dtype):
    return whole(shape), jax.ShapeDtypeStruct(tuple(shape), dtype)


def window_places(page_width):
    half = WS // 2
    columns = page_width // WS + 1
    top = np.zeros((columns * half * WS, WS * page_width), np.float32)
    low = np.zeros_like(top)
    for j in range(columns):
        for r in range(half):
            for c in range(WS):
                column = j * WS + c - half
                if 0 <= column < page_width:
                    place = (j * half + r) * WS + c
                    top[place, (half + r) * page_width + column] = 1.0
                    low[place, r * page_width + column] = 1.0
    cut = half * page_width
    return [jnp.asarray(m, bf16) for m in (top, low, top[:, cut:].T, low[:, :cut].T)]


def bias_slots(table, regions, page_width):
    half = WS // 2
    columns = page_width // WS + 1
    heads = table.shape[0]
    flipped = table.reshape(heads, SPAN, SPAN)[:, ::-1, ::-1]
    wide = jnp.stack([flipped[:, :, WS - 1 - c : 2 * WS - 1 - c] for c in range(WS)], axis=1)
    wide = wide.reshape(heads, WS, SPAN * WS)
    bias = jnp.stack(
        [wide[:, :, (WS - 1 - r) * WS : (2 * WS - 1 - r) * WS] for r in range(WS)], axis=1
    ).reshape(heads, WS * WS, WS * WS)
    padded = jnp.pad(regions, (half, half), constant_values=-1).reshape(columns, WS)
    of_place = jnp.tile(padded, (1, WS))
    allowed = (of_place[:, :, None] == of_place[:, None, :]) & (of_place[:, None, :] >= 0)
    mask = jnp.where(allowed, 0.0, masked_fill).astype(f32)
    slots = bias[None] + mask[:, None]
    return slots.reshape(columns * heads * WS * WS, WS * WS)


def bias_gather(grad, heads):
    shaped = grad.reshape(heads, WS, WS, WS * WS)
    wide = sum(
        jnp.pad(shaped[:, r], ((0, 0), (0, 0), ((WS - 1 - r) * WS, r * WS))) for r in range(WS)
    ).reshape(heads, WS, SPAN, WS)
    flipped = wide[:, :, ::-1, ::-1]
    table = sum(jnp.pad(flipped[:, c], ((0, 0), (0, 0), (c, WS - 1 - c))) for c in range(WS))
    return table.reshape(heads, SPAN * SPAN)


def body(
    visual,
    queries,
    query_lengths,
    column_regions,
    gain_window,
    window_qkv,
    window_out,
    position_bias,
    gain_visual,
    gain_query,
    attend_query,
    attend_kv,
    attend_out,
    cross_query,
    cross_kv,
    cross_out,
    gain_feed,
    visual_up,
    visual_down,
    gain_query_feed,
    query_up,
    query_down,
    cotangent_visual,
    cotangent_query,
):
    shards = lax.axis_size("win")
    pages = lax.axis_size("page")
    me = lax.axis_index("win").astype(jnp.int32)
    page = lax.axis_index("page").astype(jnp.int32)
    row_count, page_width, model = visual.shape[1:]
    own = row_count * page_width
    tokens = own * shards
    slots_count = queries.shape[1]
    heads = HEADS // shards
    head_size = model // HEADS
    part = heads * head_size
    wide = -(-part // LANES) * LANES
    static = (heads, head_size, head_size ** (-0.5))
    stripes = shards + 1
    rows = model // shards
    hidden = visual_down.shape[0]
    order = xor_order(shards)
    where_me = me.reshape(1)
    where_page = jnp.stack([me, page % 2])
    short = packed_rows(own, part, wide)

    def block_of(width, column=0):
        return pl.BlockSpec((own, width), lambda i, *_: (i, column))

    def token_out(width, dtype=bf16):
        return block_of(width), jax.ShapeDtypeStruct((tokens, width), dtype)

    def packed_block():
        return pl.BlockSpec((short, wide), lambda i, *_: (i, 0))

    def packed_out():
        return packed_block(), jax.ShapeDtypeStruct((short * shards, wide), bf16)

    def half_outs():
        shape = jax.ShapeDtypeStruct((tokens // 2, model), bf16)
        count = shards // 2
        return [
            (pl.BlockSpec((own, model), lambda i, *_: (jnp.minimum(i, count - 1), 0)), shape),
            (pl.BlockSpec((own, model), lambda i, *_: (jnp.maximum(i - count, 0), 0)), shape),
        ]

    gains = jnp.concatenate(
        [gain_window, gain_visual, gain_query, gain_feed, gain_query_feed, jnp.zeros((11 * rows,), bf16)]
    ).reshape(16, rows)
    to_far, to_near, chunk = kernel_call(
        functools.partial(entry_kernel, shards, 3, wide),
        (1,),
        [whole((own, model)), whole(window_qkv.shape), whole(gains.shape)],
        [
            full_out((own + 2 * rows + 16, model), bf16),
            full_out((own + rows + 16, model), bf16),
            full_out((rows, 3 * wide), bf16),
        ],
        (visual[0].reshape(own, model), window_qkv, gains),
        place=where_me,
        name="entry",
    )
    far = swap(to_far, "win", 2)
    near = swap(to_near, "win", 1)
    slots = bias_slots(position_bias.astype(f32), column_regions[0], page_width)
    far_now = tie(slots, far)[0]
    both = swap(far_now, "win", 1)

    height = -(-3 * rows // (16 * pages)) * 16
    shares = kernel_call(
        functools.partial(share_kernel, shards),
        (1,),
        all_of(visual_up, query_up, cross_out),
        [full_out((height, model), bf16)] * shards,
        (visual_up, query_up, cross_out),
        scratch=[pltpu.VMEM((height * pages, model), bf16)],
        place=jnp.stack([me, page]),
        name="share",
    )
    spread_weights = lax.all_gather(jnp.stack(exchange(shares)), "page")

    tied = tie(far, attend_kv, cross_query, attend_query, cross_kv, window_out)
    mixed_width = 6 * part
    blocks = kernel_call(
        functools.partial(split_columns_kernel, shards, [2, 1, 1, 2]),
        (1,),
        all_of(*tied[:4]),
        [full_out((rows, mixed_width), bf16)] * shards,
        tied[:4],
        place=where_me,
        name="split_columns",
    )
    mixed_parts = exchange(blocks)
    out_parts = gather_four(tied[4])

    both = tie(blocks[1], both)[0]
    places = window_places(page_width)
    row_mask = np.zeros((stripes, 1, WS * WS), np.float32)
    row_mask[0, :, : WS * WS // 2] = masked_fill
    row_mask[-1, :, WS * WS // 2 :] = masked_fill
    row_mask = jnp.asarray(row_mask)
    position = jnp.asarray(np.argsort(order), jnp.int32)[me ^ jnp.arange(shards, dtype=jnp.int32)]
    position = jnp.concatenate([position, where_me])

    def arriving(width, height=own):
        return pl.BlockSpec((height, width), lambda i, at: (at[jnp.minimum(i, shards - 1)], 0))

    def leaving(width, height=own):
        return pl.BlockSpec((height, width), lambda i, at: (at[jnp.maximum(i - 1, 0)], 0))

    def of_tokens(spec, width):
        return spec(width), jax.ShapeDtypeStruct((tokens, width), bf16)

    window_specs = all_of(*places, slots) + [pl.BlockSpec((1, 1, WS * WS), lambda i, at: (i, 0, 0))]
    window_args = (*places, slots, row_mask)
    vis_low, qkv_w, gains_all, norm_win, packed, heads_win = kernel_call(
        functools.partial(window_forward_kernel, *static),
        (stripes,),
        all_of(to_far, far, near, both, chunk) + window_specs,
        [
            of_tokens(arriving, model),
            full_out((model, 3 * wide), bf16),
            full_out((16, model), f32),
            of_tokens(arriving, model),
            of_tokens(arriving, 3 * wide),
            (leaving(wide, short), jax.ShapeDtypeStruct((short * shards, wide), bf16)),
        ],
        (to_far, far, near, both, chunk) + window_args,
        scratch=[pltpu.VMEM((own, 3 * wide), bf16)] * 2
        + [pltpu.VMEM((own // 2, wide), f32), pltpu.VMEM((own, model), bf16)],
        place=position,
        name="window_forward",
        us=17,
    )
    win_parts = gather_four(heads_win)

    tied = tie(heads_win, *mixed_parts)
    mixed_w = kernel_call(
        functools.partial(join_rows_kernel, shards, part, wide),
        (1,),
        all_of(*tied),
        [full_out((model, 6 * wide), bf16)],
        tied,
        place=where_me,
        name="join_rows",
    )[0]
    vis_w = mixed_w[:, : 3 * wide]
    qry_w = jnp.concatenate(
        [mixed_w[:, 3 * wide : 4 * wide], mixed_w[:, : 2 * wide], mixed_w[:, 4 * wide :]], axis=1
    )
    query_in = queries[0].astype(f32)
    norm_qry = norm_low(query_in, gains_all[2:3])
    proj_qry = matmul(norm_qry, qry_w).astype(bf16)
    length = query_lengths[0]
    slot_ids = jnp.arange(slots_count, dtype=jnp.int32)
    live = slot_ids < length
    live_mask = jnp.where(live, 0.0, masked_fill).astype(f32)[None]
    reach = (slot_ids[None, :] <= slot_ids[:, None]) & live[None, :]
    causal_mask = jnp.where(reach, 0.0, masked_fill).astype(f32)
    tied = tie(win_parts[1], attend_out, cotangent_visual)
    attend_parts = gather_four(tied[0])
    top_parts = gather_four(tied[1][0].reshape(own, model))

    def qry_piece(i):
        return pl.BlockSpec((slots_count, wide), lambda *_: (0, i))

    def vis_piece(i):
        return pl.BlockSpec((tokens, wide), lambda *_: (0, i))

    def piece_specs():
        return [pl.BlockSpec((short, wide), lambda i, *_, k=k: (i ^ k, 0)) for k in range(shards)]

    mid, norm_vis, proj_vis, heads_cross = kernel_call(
        functools.partial(middle_kernel, *static),
        (shards,),
        [block_of(model)]
        + piece_specs()
        + all_of(*out_parts, gains_all, vis_w)
        + [qry_piece(3), qry_piece(4)]
        + all_of(live_mask),
        [token_out(model, f32), token_out(model), token_out(3 * wide), packed_out()],
        (vis_low, *win_parts, *out_parts, gains_all, vis_w, proj_qry, proj_qry, live_mask),
        name="middle",
        us=13,
    )
    cross_parts = gather_four(heads_cross)

    query_specs = [
        qry_piece(0),
        qry_piece(1),
        qry_piece(2),
        vis_piece(0),
        vis_piece(1),
        whole(causal_mask.shape),
    ]
    query_args = (proj_qry, proj_qry, proj_qry, proj_vis, proj_vis, causal_mask)
    (heads_qry,) = kernel_call(
        functools.partial(query_forward_kernel, *static),
        (1,),
        query_specs,
        [full_out((slots_count, part), bf16)],
        query_args,
        name="query_forward",
        us=4,
    )
    qry_parts = gather_four(heads_qry)
    tied = tie(heads_qry, spread_weights, *top_parts)
    (three,) = kernel_call(
        unshare_kernel,
        (1,),
        all_of(tied[0]),
        [full_out((3 * model, model), bf16)],
        (tied[0],),
        place=where_me,
        name="unshare",
    )
    vup_w, qup_w, cross_out_w = [three[i * model : (i + 1) * model] for i in range(3)]
    top_low = jnp.concatenate(tied[1:], axis=0)
    top_now = tie(qry_parts[3], *tie(attend_parts[3], top_low))[0]

    late, norm_feed, act_vis, dhid_vis, feed_keep, feed_send = kernel_call(
        functools.partial(feed_kernel, part),
        (shards,),
        [block_of(model)]
        + piece_specs()
        + all_of(cross_out_w, gains_all, vup_w, visual_down)
        + [block_of(model)],
        [full_out((own, model), f32), token_out(model), token_out(hidden), token_out(hidden)] + half_outs(),
        (mid, *cross_parts, cross_out_w, gains_all, vup_w, visual_down, top_now),
        place=where_me,
        name="feed",
        us=18,
    )
    feed_terms, feed_second = scatter_pieces(feed_keep, feed_send)

    tied = tie(feed_second, *qry_parts, *attend_parts)
    query_mid = query_in + matmul(
        jnp.concatenate(tied[:shards], axis=1), jnp.concatenate(tied[shards:], axis=0)
    )
    norm_qfeed = norm_low(query_mid, gains_all[4:5])
    act_qry, slope_qry = gelu_both(matmul(norm_qfeed, qup_w))
    act_qry = act_qry.astype(bf16)
    dhid_qry = (right_tmul(cotangent_query[0], query_down) * slope_qry).astype(bf16)
    dqfeed_part = right_tmul(dhid_qry, qup_w)
    dqfeed, dqfeed_last = total_sum(dqfeed_part)
    pairs = (norm_feed, dhid_vis, act_vis, top_low, norm_qfeed, dhid_qry, act_qry, cotangent_query[0])
    pairs = tie(dqfeed_last, *tie(feed_second, *pairs))
    (feed_grads,) = kernel_call(
        functools.partial(feed_grads_kernel, shards),
        (4,),
        all_of(*pairs),
        [full_out((4 * hidden, model), bf16)],
        pairs,
        name="feed_grads",
        us=10,
    )
    up_share, down_share = 2 * rows // GROUPS, 2 * hidden // GROUPS

    def to_sources(group):
        stack = group[: shards * up_share].reshape(shards, up_share, model)
        return jnp.concatenate(trade(stack) + [group[shards * up_share :]], axis=0)

    if pages == GROUPS:
        feed_sum = to_sources(lax.psum_scatter(feed_grads, "page", scatter_dimension=0, tiled=True))
    else:
        summed = lax.psum(feed_grads, "page").reshape(GROUPS, -1, model)
        feed_sum = jnp.concatenate([to_sources(summed[g]) for g in range(GROUPS)], axis=0)

    def back_through_norm(line, tensor, terms, residual, dtypes):
        own_block = pl.BlockSpec((own, model), lambda *_: (0, 0))
        return kernel_call(
            functools.partial(norm_back_kernel, line),
            (1,),
            [own_block, whole(gains_all.shape)] + [own_block] * 4,
            [(own_block, jax.ShapeDtypeStruct((own, model), d)) for d in dtypes],
            (tensor, gains_all, *terms, residual),
            name="norm_back",
        )

    (last_term,) = tie(feed_grads, feed_terms[2])
    grad_late, dz_cross = back_through_norm(
        3,
        late,
        (feed_terms[0], feed_terms[1], last_term),
        cotangent_visual[0].reshape(own, model),
        [f32, bf16],
    )
    cross_dz = gather_four(dz_cross)

    (dqfeed,) = tie(dz_cross, dqfeed)
    grad_qmid = cotangent_query[0].astype(f32) + norm_back(query_mid, gains_all[4:5], dqfeed)
    dz_attend = grad_qmid.astype(bf16)
    dheads_qry = right_tmul(dz_attend, jnp.pad(attend_out, ((0, wide - part), (0, 0)))).astype(bf16)
    dq, dkq, dvq, dkv, dvv = kernel_call(
        functools.partial(query_backward_kernel, *static),
        (1,),
        query_specs + [whole((slots_count, wide))],
        [full_out((slots_count, wide), bf16)] * 3 + [full_out((tokens, wide), bf16)] * 2,
        query_args + (dheads_qry,),
        name="query_backward",
        us=8,
    )
    grad_attend_out = left_tmul(heads_qry, dz_attend)

    out_rows = jnp.pad(cross_out, ((0, wide - part), (0, 0)))
    dproj_vis, dck, dcv, grad_cross_out, vis_keep, vis_send = kernel_call(
        functools.partial(cross_backward_kernel, *static),
        (shards,),
        [block_of(3 * wide), qry_piece(3), qry_piece(4)]
        + all_of(live_mask, *cross_dz, out_rows)
        + [packed_block(), block_of(wide), block_of(wide)]
        + all_of(vis_w),
        [token_out(3 * wide)]
        + [full_out((slots_count, wide), f32)] * 2
        + [full_out((part, model), f32)]
        + half_outs(),
        (proj_vis, proj_qry, proj_qry, live_mask, *cross_dz, out_rows, heads_cross, dkv, dvv, vis_w),
        scratch=[pltpu.VMEM((own, model), bf16)],
        name="cross_backward",
        us=16,
    )
    vis_terms, vis_second = scatter_pieces(vis_keep, vis_send)

    def halves_here(*grads):
        width = sum(g.shape[1] for g in grads) // wide * part
        return kernel_call(
            functools.partial(split_halves_kernel, shards, part, wide),
            (1,),
            all_of(*grads),
            [full_out((model // 2, width), bf16)] * 2,
            grads,
            place=where_page,
            name="split_halves",
            us=3,
        )

    depth, side = page // 2, page % 2

    def laid_out(blocks, pieces, width):
        direct = pages == 2 * LINE
        return kernel_call(
            functools.partial(lay_out_kernel, shards, pieces, True),
            (1,),
            all_of(*blocks),
            [full_out((rows, count * width * shards), f32) for count in pieces],
            blocks,
            place=jnp.stack([me ^ depth, side]) if direct else where_page,
            name="lay_out",
            us=2,
        )

    def beside(tensor):
        return lax.ppermute(tensor, "page", [(i, i ^ 1) for i in range(pages)])

    def to_rows(half):
        height = half.shape[0] // shards
        return jnp.concatenate(exchange([half[k * height : (k + 1) * height] for k in range(shards)]), axis=0)

    def pair_total(keep, give):
        return keep if pages == 1 else add_low(keep, beside(give))

    def parity_sum(tensor):
        groups = [list(range(s, pages, 2)) for s in (0, 1)]
        return lax.psum(tensor, "page", axis_index_groups=groups)

    def columns_scatter(own_half):
        own_chunk = line_scatter(own_half.reshape(shards, -1, own_half.shape[1]), depth)
        pairs = [
            (p * shards + w, p * shards + (w ^ (p // 2))) for p in range(pages) for w in range(shards)
        ]
        return lax.ppermute(own_chunk, ("page", "win"), pairs)

    def columns_gather(chunk):
        here = jnp.concatenate(line_gather(chunk), axis=0)
        return here, beside(here)

    def columns_total(own_half, give):
        if pages == 1:
            return to_rows(own_half), to_rows(give)
        here = to_rows(parity_sum(own_half))
        return here, beside(here)

    def rows_halves(grad):
        stack = grad.astype(bf16).reshape(2, -1, grad.shape[1])
        return pick(stack, side), pick(stack, 1 - side)

    def rows_scatter(own_half):
        return line_scatter(own_half.reshape(LINE, -1, own_half.shape[1]), depth)

    def rows_gather(quarter):
        stack = jnp.stack(line_gather(quarter))
        here = jnp.concatenate([pick(stack, depth ^ q) for q in range(LINE)], axis=0)
        return both_halves(here, beside(here))

    def both_halves(here, other):
        first = side == 0
        return jnp.concatenate([jnp.where(first, here, other), jnp.where(first, other, here)], axis=0).astype(f32)

    def rows_total(own_half, give):
        if pages == 1:
            return both_halves(own_half, give)
        here = parity_sum(own_half)
        return both_halves(here, beside(here))

    def scattered(columns, rows_):
        if pages == 2 * LINE and shards == LINE:
            return columns_scatter(columns), rows_scatter(rows_)
        return columns, rows_

    def gathered(columns, rows_, halves, rows_half):
        if pages == 2 * LINE and shards == LINE:
            return columns_gather(columns), rows_gather(rows_)
        return columns_total(columns, halves[1]), rows_total(rows_, rows_half[1])

    (dproj_now, norm_now, dck, dcv) = tie(vis_second, dproj_vis, norm_vis, dck, dcv)
    dproj_qry = jnp.concatenate([dq, dkq, dvq, dck.astype(bf16), dcv.astype(bf16)], axis=1)
    grad_vis_w = left_tmul(norm_now, dproj_now)
    grad_qry_w = left_tmul(norm_qry, dproj_qry)
    dnorm_qry, _ = total_sum(right_tmul(dproj_qry, qry_w))
    qry_columns = [grad_qry_w[:, i * wide : (i + 1) * wide] for i in range(5)]
    mixed_halves = halves_here(
        grad_vis_w[:, :wide] + qry_columns[1],
        grad_vis_w[:, wide : 2 * wide] + qry_columns[2],
        grad_vis_w[:, 2 * wide :],
        qry_columns[0],
        qry_columns[3],
        qry_columns[4],
    )
    outs_halves = rows_halves(jnp.concatenate([grad_cross_out, grad_attend_out], axis=0))
    (last_term,) = tie(mixed_halves[0], vis_terms[2])
    grad_mid, dz_window = back_through_norm(
        1, mid, (vis_terms[0], vis_terms[1], last_term), grad_late, [f32, bf16]
    )
    window_dz = gather_four(dz_window)

    act_now, dnorm_qry = tie(dz_window, act_vis, dnorm_qry)
    final = matmul(act_now, visual_down).astype(bf16)
    final_terms, _ = scatter_pieces(final[: tokens // 2], final[tokens // 2 :])
    query_back = (grad_qmid + norm_back(query_in, gains_all[2:3], dnorm_qry)).astype(bf16)
    query_final = query_mid + total_sum(matmul(act_qry, query_down))[0]

    out_rows = jnp.pad(window_out, ((0, wide - part), (0, 0)))
    mixed_pair, outs_pair = pair_total(*mixed_halves), pair_total(*outs_halves)
    first_dz = tie(final, *tie(mixed_pair, *tie(outs_pair, window_dz[0])))[0]
    if pages == GROUPS:
        first_dz = tie(feed_sum, first_dz)[0]
        feed_sum = lax.all_gather(feed_sum, "page", axis=0, tiled=True)
    window_dz = [first_dz] + list(window_dz[1:])
    dpacked, dnorm_win, bias_grad, grad_window_out = kernel_call(
        functools.partial(window_backward_kernel, *static),
        (stripes,),
        all_of(*window_dz)
        + [arriving(3 * wide), arriving(wide, short)]
        + all_of(out_rows, qkv_w)
        + window_specs,
        [
            of_tokens(leaving, 3 * wide),
            of_tokens(leaving, model),
            full_out((heads * WS * WS, WS * WS), f32),
            full_out((part, model), f32),
        ],
        (*window_dz, packed, heads_win, out_rows, qkv_w) + window_args,
        scratch=[pltpu.VMEM((own, 3 * wide), bf16)] * 2
        + [pltpu.VMEM((own, wide), bf16)] * 2
        + [pltpu.VMEM((own // 2, 3 * wide), f32)]
        + [pltpu.VMEM((places[0].shape[0], 3 * wide), f32)] * 2
        + [pltpu.VMEM((own, model), bf16)],
        place=position,
        name="window_backward",
        us=27,
    )
    win_terms, win_second = scatter_pieces(dnorm_win[: tokens // 2], dnorm_win[tokens // 2 :])
    grad_qkv_w = left_tmul(norm_win, dpacked)
    qkv_halves = halves_here(grad_qkv_w)
    mixed_share, outs_share = scattered(mixed_pair, outs_pair)
    mixed_share, outs_share = tie(dpacked, mixed_share, outs_share)
    mixed_t, outs_t = gathered(mixed_share, outs_share, mixed_halves, outs_halves)
    wout_halves = rows_halves(grad_window_out)
    qkv_share, wout_share = scattered(pair_total(*qkv_halves), pair_total(*wout_halves))
    qkv_t, wout_t = gathered(qkv_share, wout_share, qkv_halves, wout_halves)
    (visual_back,) = back_through_norm(0, vis_low, win_terms, grad_mid, [bf16])
    visual_final = late + (
        final_terms[0][:own].astype(f32) + final_terms[1][:own].astype(f32) + final_terms[2].astype(f32)
    )

    grouped = feed_grads.reshape(2, GROUPS // 2, -1, model)[:, :, : shards * up_share]
    up_grads = grouped.reshape(2, GROUPS // 2, shards, up_share, model).transpose(0, 2, 1, 3, 4)
    up_grads = up_grads.reshape(2, shards * up_share * (GROUPS // 2), model)

    def gain_grad(line, *pairs):
        return sum(jnp.sum(w.astype(f32) * g.astype(f32), axis=1) for w, g in pairs) / gains_all[line]

    gain_grads = jnp.stack(
        [
            gain_grad(0, (qkv_w, grad_qkv_w)),
            gain_grad(1, (vis_w, grad_vis_w)),
            gain_grad(2, (qry_w, grad_qry_w)),
            gain_grad(3, (vup_w, up_grads[0])),
            gain_grad(4, (qup_w, up_grads[1])),
        ]
    )
    (bias_grad,) = tie(qkv_halves[0], bias_grad)
    small = jnp.concatenate(
        [tiny_sum(gain_grads, ("win",)).reshape(-1), bias_gather(bias_grad, heads).reshape(-1)]
    )
    small = tiny_sum(small, ("page",))
    gain_total = lax.dynamic_slice_in_dim(small[: 5 * model].reshape(5, model), me * rows, rows, 1)
    bias_total = small[5 * model :].reshape(heads, SPAN * SPAN)

    out_vup, out_vdown, out_qup, out_qdown = [
        full_out(shape, f32) for shape in ((rows, shards * hidden), (hidden, model)) * 2
    ]
    (feed_sum,) = tie(dpacked, feed_sum)
    out_vup, out_qup, out_vdown, out_qdown = kernel_call(
        functools.partial(lay_out_feed_kernel, shards),
        (1,),
        all_of(feed_sum),
        [out_vup, out_qup, out_vdown, out_qdown],
        (feed_sum,),
        place=where_me,
        name="lay_out_feed",
        us=6,
    )
    (out_qkv,) = laid_out(qkv_t, [3], part)
    out_akv, out_cq, out_aq, out_ckv = laid_out(mixed_t, [2, 1, 1, 2], part)

    return (
        visual_final.reshape(1, row_count, page_width, model).astype(bf16),
        query_final.reshape(1, slots_count, model).astype(bf16),
        visual_back.reshape(1, row_count, page_width, model),
        query_back.reshape(1, slots_count, model),
        gain_total[0],
        out_qkv,
        wout_t,
        bias_total,
        gain_total[1],
        gain_total[2],
        out_aq,
        out_akv,
        outs_t[rows:],
        out_cq,
        out_ckv,
        outs_t[:rows],
        gain_total[3],
        out_vup,
        out_vdown,
        gain_total[4],
        out_qup,
        out_qdown,
    )


def solution(mesh):
    tokens_spec = P("page", "win", None, None)
    slots_spec = P("page", None, None)
    gain, weight = P("win"), P("win", None)
    parameters = (
        gain, weight, weight, weight, gain, gain, weight, weight, weight, weight, weight, weight,
        gain, weight, weight, gain, weight, weight,
    )
    return jax.shard_map(
        body,
        mesh=mesh,
        in_specs=(tokens_spec, slots_spec, P("page"), P("page", None)) + parameters + (tokens_spec, slots_spec),
        out_specs=(tokens_spec, slots_spec, tokens_spec, slots_spec) + parameters,
        check_vma=False,
    )
```

```python
import functools

import jax
import jax.numpy as jnp
import numpy as np
from jax import lax
from jax.experimental import pallas as pl
from jax.experimental.pallas import tpu as pltpu
from jax.sharding import PartitionSpec as P

HEADS = 12
WS = 12
SPAN = 2 * WS - 1
LANES = 256

epsilon = 1e-05
masked_fill = -1000000000.0
bf16 = jnp.bfloat16
f32 = jnp.float32
VMEM_BYTES = 48 * 1024 * 1024


def swap(tensor, axis, bit):
    count = lax.axis_size(axis)
    return lax.ppermute(tensor, axis, [(i, i ^ bit) for i in range(count)])


def bits_of(count):
    bits = []
    while count > 1:
        count //= 2
        bits.append(count)
    return bits


def gather_blocks(block, axis="win"):
    for bit in bits_of(lax.axis_size(axis)):
        block = jnp.concatenate([block, swap(block, axis, bit)], axis=0)
    return block


def scatter_sum(parts, axis="win"):
    bits = bits_of(lax.axis_size(axis))
    for bit in reversed(bits):
        half = parts.shape[0] // 2
        arrived = swap(parts[half:].astype(bf16), axis, bit)
        parts = parts[:half].astype(f32) + arrived.astype(f32)
    return parts


def total_sum(part, axis="win"):
    for bit in reversed(bits_of(lax.axis_size(axis))):
        mine = lax.reduce_precision(part.astype(f32), 8, 7)
        last = mine.astype(bf16)
        part = mine + swap(last, axis, bit).astype(f32)
    return part, last


def tiny_sum(part, axes):
    for axis in axes:
        for bit in reversed(bits_of(lax.axis_size(axis))):
            part = part + swap(part, axis, bit)
    return part


def pick(stack, index):
    return lax.dynamic_index_in_dim(stack, index, 0, False)


def trade(stack, axis="win"):
    count = lax.axis_size(axis)
    me = lax.axis_index(axis)
    return [pick(stack, me)] + [swap(pick(stack, me ^ k), axis, k) for k in range(1, count)]


def in_order(blocks, axis="win"):
    me = lax.axis_index(axis)
    stack = jnp.stack(blocks) if isinstance(blocks, (list, tuple)) else blocks
    return [pick(stack, me ^ j) for j in range(lax.axis_size(axis))]


def xor_order(count):
    order = [0]
    for bit in bits_of(count):
        order = order + [k ^ bit for k in order]
    return order


def rounded(tensor):
    return lax.reduce_precision(tensor, 8, 7)


def add_low(left, right):
    return rounded(left.astype(f32) + right.astype(f32)).astype(bf16)


LINE = 4


def line_swap(tensor, k):
    pairs = [(2 * a + x, 2 * (a ^ k) + x) for a in range(LINE) for x in (0, 1)]
    return lax.ppermute(tensor, "page", pairs)


def line_send(parts, depth):
    return [pick(parts, depth)] + [line_swap(pick(parts, depth ^ k), k) for k in range(1, LINE)]


def line_add(terms):
    return rounded(total([t.astype(f32) for t in terms])).astype(bf16)


def line_gather(own):
    return [own] + [line_swap(own, k) for k in range(1, LINE)]


def exchange(blocks):
    return [blocks[0]] + [swap(blocks[k], "win", k) for k in range(1, len(blocks))]


def tie(first, *later):
    return lax.optimization_barrier((first,) + later)[1:]


def gather_four(block, axis="win"):
    count = lax.axis_size(axis)
    parts = [block]
    for bit in bits_of(count):
        parts = parts + [swap(p, axis, bit) for p in parts]
    return parts


def fence(*values):
    return lax.optimization_barrier(values)


def scatter_pieces(keep, send):
    bits = bits_of(lax.axis_size("win"))
    arrived = swap(send, "win", bits[-1])
    half = keep.shape[0] // 2
    second = (keep[half:].astype(f32) + arrived[half:].astype(f32)).astype(bf16)
    return (keep, arrived, swap(second, "win", bits[0])), second


def normalise(tensor):
    centre = tensor - jnp.mean(tensor, axis=-1, keepdims=True)
    spread = lax.rsqrt(jnp.mean(centre * centre, axis=-1, keepdims=True) + epsilon)
    return centre * spread, spread


def norm_low(tensor, gain):
    return (normalise(tensor)[0] * gain).astype(bf16)


def norm_back(tensor, gain, upstream):
    unit, spread = normalise(tensor)
    scaled = upstream * gain
    return spread * (
        scaled
        - jnp.mean(scaled, axis=-1, keepdims=True)
        - unit * jnp.mean(scaled * unit, axis=-1, keepdims=True)
    )


def gelu_both(hidden):
    phi = 0.5 * (1.0 + lax.erf(hidden * np.float32(np.sqrt(0.5))))
    density = jnp.exp(-0.5 * hidden * hidden) * np.float32(1.0 / np.sqrt(2.0 * np.pi))
    return hidden * phi, phi + hidden * density


def matmul(left, right):
    return jnp.dot(left, right, preferred_element_type=f32)


def left_tmul(left, right):
    return lax.dot_general(left, right, (((0,), (0,)), ((), ())), preferred_element_type=f32)


def right_tmul(left, right):
    return lax.dot_general(left, right, (((1,), (1,)), ((), ())), preferred_element_type=f32)


def pad_lanes(tensor, width):
    return jnp.pad(tensor, ((0, 0), (0, width - tensor.shape[1])))


def head_mask(head, head_size, width, scale):
    lane = lax.broadcasted_iota(jnp.int32, (1, width), 1)
    inside = (lane >= head * head_size) & (lane < (head + 1) * head_size)
    return jnp.where(inside, np.float32(scale), np.float32(0.0)).astype(bf16)


def softmax_rows(scores):
    peak = jnp.max(scores, axis=-1, keepdims=True)
    mass = jnp.exp(scores - peak)
    return mass * (1.0 / jnp.sum(mass, axis=-1, keepdims=True))


def by_head(tensor, heads, head_size, scale):
    return [tensor * head_mask(h, head_size, tensor.shape[1], scale) for h in range(heads)]


def total(terms):
    result = terms[0]
    for term in terms[1:]:
        result = result + term
    return result


def window_rows(spread_top, spread_low, before, after, window, cells):
    half = cells // 2
    return jnp.concatenate(
        [spread_top[window * half : (window + 1) * half], spread_low[window * half : (window + 1) * half]],
        axis=0,
    ).astype(bf16)


def pack_lanes(tensor, wide):
    rows, part = tensor.shape
    first = packed_rows(rows, part, wide)
    spare = wide - part
    tail = tensor[first:]
    side = [tail[:, s : s + spare] for s in range(0, part, spare)]
    rest = first - tail.shape[0] * len(side)
    side.append(jnp.zeros((rest, spare), tensor.dtype))
    return jnp.concatenate([tensor[:first], jnp.concatenate(side, axis=0)], axis=1)


def packed_rows(rows, part, wide):
    return -(-rows * part // (wide * 16)) * 16


def unpack_lanes(packed, rows, part):
    first, wide = packed.shape
    spare, tail = wide - part, rows - first
    side = packed[:, part:]
    last = jnp.concatenate([side[s * tail : (s + 1) * tail] for s in range(part // spare)], axis=1)
    return jnp.concatenate([packed[:, :part], last], axis=0)


def pick_block(blocks, place, target):
    for k, block in enumerate(blocks):

        @pl.when(place == k)
        def _(block=block):
            target[...] = block[: target.shape[0], :]


def window_forward_kernel(
    heads, head_size, scale, place, near, second, third, fourth, chunk, gain_own, gain_second, gain_third,
    gain_fourth, top_in, low_in, top_out, low_out, slots, rows, visual, weight, gains, norm, packed, mixed, before, after, held, chosen,
):
    step, last = pl.program_id(0), pl.num_programs(0) - 1
    cells = WS * WS
    half = cells // 2
    width = weight.shape[1] // 3
    blocks = (near, second, third, fourth)
    shards = len(blocks)
    me = place[shards]
    own, piece, part = chosen.shape[0], chunk.shape[0], heads * head_size

    @pl.when(step == 0)
    def _():
        before[...] = jnp.zeros_like(before)
        held[...] = jnp.zeros_like(held)
        order = xor_order(shards)
        starts = (None, own, own, own + piece)
        for p, k in enumerate(order):
            source = chunk[...] if p == 0 else blocks[p][starts[p] : starts[p] + piece, :]
            rows_here = weight.shape[0] // shards
            source = unfold(source, rows_here, 3 * part)
            gap = jnp.zeros((rows_here, width - part), bf16)
            columns = [x for s in range(3) for x in (source[:, s * part : (s + 1) * part], gap)]
            at = pl.ds(pl.multiple_of((me ^ k) * rows_here, rows_here), rows_here)
            weight[at, :] = jnp.concatenate(columns, axis=1)
        for device in range(shards):

            @pl.when(me == device)
            def _(device=device):
                lines = [None] * shards
                for p, ref in enumerate((gain_own, gain_second, gain_third, gain_fourth)):
                    lines[device ^ order[p]] = ref[...].astype(f32)
                gains[...] = jnp.concatenate(lines, axis=1)

    @pl.when(step < last)
    def _():
        pick_block(blocks, place[jnp.minimum(step, last - 1)], chosen)
        visual[...] = chosen[...]
        low = norm_low(chosen[...].astype(f32), gains[0:1, :])
        norm[...] = low
        after[...] = matmul(low, weight[...]).astype(bf16)
        packed[...] = after[...]

    @pl.when(step == last)
    def _():
        after[...] = jnp.zeros_like(after)

    top = matmul(top_in[...], before[...])
    low = matmul(low_in[...], after[...])
    upper, lower = [], []
    for j in range(top.shape[0] // half):
        part = window_rows(top, low, before, after, j, cells)
        query, key, value = part[:, :width], part[:, width : 2 * width], part[:, 2 * width :]
        stacked = jnp.concatenate(by_head(query, heads, head_size, scale), axis=0)
        mask = slots[j * heads * cells : (j + 1) * heads * cells, :] + rows[0]
        probs = softmax_rows(right_tmul(stacked, key) + mask).astype(bf16)
        values = by_head(value, heads, head_size, 1.0)
        result = total([matmul(probs[h * cells : (h + 1) * cells], values[h]) for h in range(heads)])
        upper.append(result[:half])
        lower.append(result[half:])
    above = matmul(top_out[...], jnp.concatenate(upper, axis=0).astype(bf16))
    below = matmul(low_out[...], jnp.concatenate(lower, axis=0).astype(bf16))

    @pl.when(step > 0)
    def _():
        block = jnp.concatenate([held[...], above], axis=0)
        mixed[...] = pack_lanes(block[:, : heads * head_size], width).astype(bf16)

    held[...] = below
    before[...] = after[...]


def window_backward_kernel(
    heads, head_size, scale, place, near, second, third, fourth, packed, mixed, weight_out, weight, top_in,
    low_in, top_out, low_out, slots, rows, grads, dnorm, bias_out, out_grad, before, after, top_before,
    top_after, held, upper, lower, upstream,
):
    step, last = pl.program_id(0), pl.num_programs(0) - 1
    cells = WS * WS
    half = cells // 2
    width = weight.shape[1] // 3

    @pl.when(step == 0)
    def _():
        before[...] = jnp.zeros_like(before)
        top_before[...] = jnp.zeros_like(top_before)
        bias_out[...] = jnp.zeros_like(bias_out)
        out_grad[...] = jnp.zeros_like(out_grad)
        held[...] = jnp.zeros_like(held)

    @pl.when(step < last)
    def _():
        pick_block((near, second, third, fourth), place[jnp.minimum(step, last - 1)], upstream)
        after[...] = packed[...]
        top_after[...] = right_tmul(upstream[...], weight_out[...]).astype(bf16)
        whole_heads = unpack_lanes(mixed[...], upstream.shape[0], heads * head_size)
        out_grad[...] += left_tmul(whole_heads, upstream[...])

    @pl.when(step == last)
    def _():
        after[...] = jnp.zeros_like(after)
        top_after[...] = jnp.zeros_like(top_after)

    top = matmul(top_in[...], before[...])
    low = matmul(low_in[...], after[...])
    given_top = matmul(top_in[...], top_before[...])
    given_low = matmul(low_in[...], top_after[...])
    for j in range(top.shape[0] // half):
        part = window_rows(top, low, before, after, j, cells)
        given = window_rows(given_top, given_low, before, after, j, cells)
        query, key, value = part[:, :width], part[:, width : 2 * width], part[:, 2 * width :]
        stacked = jnp.concatenate(by_head(query, heads, head_size, scale), axis=0)
        mask = slots[j * heads * cells : (j + 1) * heads * cells, :] + rows[0]
        probs = softmax_rows(right_tmul(stacked, key) + mask)
        given = jnp.concatenate(by_head(given, heads, head_size, 1.0), axis=0)
        dprobs = right_tmul(given, value)
        inner = jnp.sum(probs * dprobs, axis=-1, keepdims=True)
        dscores = (probs * (dprobs - inner)).astype(bf16)
        bias_out[...] += dscores.astype(f32)
        keys = by_head(key, heads, head_size, scale)
        dquery = total([matmul(dscores[h * cells : (h + 1) * cells], keys[h]) for h in range(heads)])
        dkey = left_tmul(dscores, stacked)
        dvalue = left_tmul(probs.astype(bf16), given)
        for s, result in enumerate((dquery, dkey, dvalue)):
            upper[j * half : (j + 1) * half, s * width : (s + 1) * width] = result[:half]
            lower[j * half : (j + 1) * half, s * width : (s + 1) * width] = result[half:]
    above = matmul(top_out[...], upper[...].astype(bf16))
    below = matmul(low_out[...], lower[...].astype(bf16))

    block = jnp.concatenate([held[...], above], axis=0).astype(bf16)
    grads[...] = block
    held[...] = below
    dnorm[...] = right_tmul(block, weight[...]).astype(bf16)
    before[...] = after[...]
    top_before[...] = top_after[...]


def middle_kernel(
    heads, head_size, scale, visual, own, second, third, fourth, out_own, out_second, out_third, out_fourth,
    gains, weight, keys, values, live, mid, norm, proj, mixed,
):
    pieces = (own, second, third, fourth)
    weights = (out_own, out_second, out_third, out_fourth)
    part = heads * head_size
    result = visual[...].astype(f32) + total(
        [matmul(unpack_lanes(p[...], mid.shape[0], part), w[...]) for p, w in zip(pieces, weights)]
    )
    mid[...] = result
    low = norm_low(result, gains[1:2, :])
    norm[...] = low
    packed = matmul(low, weight[...]).astype(bf16)
    proj[...] = packed
    width = keys.shape[1]
    query = by_head(packed[:, 2 * width :], heads, head_size, scale)
    value = by_head(values[...], heads, head_size, 1.0)
    terms = []
    for h in range(heads):
        probs = softmax_rows(right_tmul(query[h], keys[...]) + live[...])
        terms.append(matmul(probs.astype(bf16), value[h]))
    mixed[...] = pack_lanes(total(terms)[:, :part], width).astype(bf16)


def feed_kernel(
    part, place, mid, own, second, third, fourth, weight_out, gains, up, down, top_own, top_second, top_third,
    top_fourth, late, norm, act, dhidden, top, keep, send, cotangent,
):
    step, halfway = pl.program_id(0), pl.num_programs(0) // 2
    pieces = (own, second, third, fourth)
    terms = []
    for piece, k in zip(pieces, xor_order(len(pieces))):
        rows = weight_out[pl.ds(pl.multiple_of((place[0] ^ k) * part, part), part), :]
        terms.append(matmul(unpack_lanes(piece[...], mid.shape[0], part), rows))
    result = mid[...] + total(terms)

    @pl.when(step == 0)
    def _():
        late[...] = result

    low = norm_low(result, gains[3:4, :])
    norm[...] = low
    value, slope = gelu_both(matmul(low, up[...]))
    act[...] = value.astype(bf16)
    for k, ref in enumerate((top_own, top_second, top_third, top_fourth)):

        @pl.when(step == k)
        def _(ref=ref):
            cotangent[...] = ref[ref.shape[0] - cotangent.shape[0] :, :]

    top[...] = cotangent[...]
    back = (right_tmul(cotangent[...], down[...]) * slope).astype(bf16)
    dhidden[...] = back
    dnorm = right_tmul(back, up[...]).astype(bf16)

    @pl.when(step < halfway)
    def _():
        keep[...] = dnorm

    @pl.when(step >= halfway)
    def _():
        send[...] = dnorm


def query_feed_kernel(
    query, own, second, third, fourth, top_own, top_second, top_third, top_fourth, gains, up, down, top,
    mid, norm, act, dhidden, dnorm,
):
    pieces, weights = (own, second, third, fourth), (top_own, top_second, top_third, top_fourth)
    result = query[...].astype(f32) + total([matmul(p[...], w[...]) for p, w in zip(pieces, weights)])
    mid[...] = result
    low = norm_low(result, gains[4:5, :])
    norm[...] = low
    value, slope = gelu_both(matmul(low, up[...]))
    act[...] = value.astype(bf16)
    back = (right_tmul(top[...], down[...]) * slope).astype(bf16)
    dhidden[...] = back
    dnorm[...] = right_tmul(back, up[...]).astype(bf16)


def halves_kernel(left, right, keep, send):
    step, halfway = pl.program_id(0), pl.num_programs(0) // 2
    result = matmul(left[...], right[...]).astype(bf16)

    @pl.when(step < halfway)
    def _():
        keep[...] = result

    @pl.when(step >= halfway)
    def _():
        send[...] = result


def query_scores(query, keys_vis, keys_qry, causal, mask):
    masked = query * mask
    return masked, right_tmul(masked, keys_vis), right_tmul(masked, keys_qry) + causal


def joint_softmax(score_vis, score_qry):
    peak = jnp.maximum(
        jnp.max(score_vis, axis=-1, keepdims=True), jnp.max(score_qry, axis=-1, keepdims=True)
    )
    mass_vis = jnp.exp(score_vis - peak)
    mass_qry = jnp.exp(score_qry - peak)
    inverse = 1.0 / (
        jnp.sum(mass_vis, axis=-1, keepdims=True) + jnp.sum(mass_qry, axis=-1, keepdims=True)
    )
    return mass_vis * inverse, mass_qry * inverse


def query_forward_kernel(
    heads, head_size, scale, query, keys_qry, values_qry, keys_vis, values_vis, causal, out
):
    width = query.shape[1]
    terms = []
    for h in range(heads):
        _, score_vis, score_qry = query_scores(
            query[...], keys_vis[...], keys_qry[...], causal[...], head_mask(h, head_size, width, scale)
        )
        prob_vis, prob_qry = joint_softmax(score_vis, score_qry)
        mask = head_mask(h, head_size, width, 1.0)
        terms.append(matmul(prob_vis.astype(bf16), values_vis[...] * mask))
        terms.append(matmul(prob_qry.astype(bf16), values_qry[...] * mask))
    out[...] = total(terms).astype(bf16)[:, : out.shape[1]]


def query_backward_kernel(
    heads, head_size, scale, query, keys_qry, values_qry, keys_vis, values_vis, causal, mid, gains, top, dnorm,
    weight_out, dquery, dkeys_qry, dvalues_qry, dkeys_vis, dvalues_vis, dmid, dz,
):
    width = query.shape[1]
    result = top[...].astype(f32) + norm_back(mid[...], gains[4:5, :], dnorm[...])
    dmid[...] = result
    low = result.astype(bf16)
    dz[...] = low
    upstream = right_tmul(low, weight_out[...]).astype(bf16)
    sums = [[], [], [], [], []]
    for h in range(heads):
        masked, score_vis, score_qry = query_scores(
            query[...], keys_vis[...], keys_qry[...], causal[...], head_mask(h, head_size, width, scale)
        )
        prob_vis, prob_qry = joint_softmax(score_vis, score_qry)
        given = upstream * head_mask(h, head_size, width, 1.0)
        dprob_vis = right_tmul(given, values_vis[...])
        dprob_qry = right_tmul(given, values_qry[...])
        inner = jnp.sum(prob_vis * dprob_vis, axis=-1, keepdims=True) + jnp.sum(
            prob_qry * dprob_qry, axis=-1, keepdims=True
        )
        dscore_vis = (prob_vis * (dprob_vis - inner)).astype(bf16)
        dscore_qry = (prob_qry * (dprob_qry - inner)).astype(bf16)
        mask = head_mask(h, head_size, width, scale)
        sums[0].append(matmul(dscore_vis, keys_vis[...] * mask))
        sums[0].append(matmul(dscore_qry, keys_qry[...] * mask))
        sums[1].append(left_tmul(dscore_qry, masked))
        sums[2].append(left_tmul(prob_qry.astype(bf16), given))
        sums[3].append(left_tmul(dscore_vis, masked))
        sums[4].append(left_tmul(prob_vis.astype(bf16), given))
    for ref, terms in zip((dquery, dkeys_qry, dvalues_qry, dkeys_vis, dvalues_vis), sums):
        ref[...] = total(terms).astype(bf16)


def cross_backward_kernel(
    heads, head_size, scale, proj, keys, values, live, near, second, third, fourth, weight_out, mixed,
    dkeys_vis, dvalues_vis, weight, dproj, dkeys, dvalues, out_grad, keep, send, upstream,
):
    step, halfway = pl.program_id(0), pl.num_programs(0) // 2
    width = keys.shape[1]

    @pl.when(step == 0)
    def _():
        dkeys[...] = jnp.zeros_like(dkeys)
        dvalues[...] = jnp.zeros_like(dvalues)
        out_grad[...] = jnp.zeros_like(out_grad)

    pick_block((near, second, third, fourth), step, upstream)
    out_grad[...] += left_tmul(unpack_lanes(mixed[...], upstream.shape[0], heads * head_size), upstream[...])
    top = right_tmul(upstream[...], weight_out[...]).astype(bf16)
    query = by_head(proj[:, 2 * width :], heads, head_size, scale)
    given = by_head(top, heads, head_size, 1.0)
    scaled = by_head(keys[...], heads, head_size, scale)
    terms = []
    for h in range(heads):
        probs = softmax_rows(right_tmul(query[h], keys[...]) + live[...])
        dprobs = right_tmul(given[h], values[...])
        inner = jnp.sum(probs * dprobs, axis=-1, keepdims=True)
        dscores = (probs * (dprobs - inner)).astype(bf16)
        terms.append(matmul(dscores, scaled[h]))
        dkeys[...] += left_tmul(dscores, query[h])
        dvalues[...] += left_tmul(probs.astype(bf16), given[h])
    block = jnp.concatenate([dkeys_vis[...], dvalues_vis[...], total(terms).astype(bf16)], axis=1)
    dproj[...] = block
    dnorm = right_tmul(block, weight[...]).astype(bf16)

    @pl.when(step < halfway)
    def _():
        keep[...] = dnorm

    @pl.when(step >= halfway)
    def _():
        send[...] = dnorm


def norm_back_kernel(line, tensor, gains, first, second, third, residual, *outs):
    upstream = first[...].astype(f32) + second[...].astype(f32) + third[...].astype(f32)
    gain = gains[line : line + 1, :]
    result = residual[...].astype(f32) + norm_back(tensor[...].astype(f32), gain, upstream)
    for out in outs:
        out[...] = result.astype(out.dtype)


def entry_kernel(shards, pieces, place, visual, weight, to_far, to_near, chunk):
    own, rows = visual.shape[0], weight.shape[0]
    part = weight.shape[1] // (pieces * shards)
    to_far[:own, :] = visual[...]
    to_near[:own, :] = visual[...]
    for me in range(shards):

        @pl.when(place[0] == me)
        def _(me=me):
            for k in range(shards):
                starts = [(s * shards + (me ^ k)) * part for s in range(pieces)]
                block = jnp.concatenate([weight[:, c : c + part] for c in starts], axis=1)
                folded = fold(block, visual.shape[1])
                height = folded.shape[0]
                if k == 0:
                    chunk[...] = folded
                elif k == 1:
                    to_near[own : own + height, :] = folded
                else:
                    to_far[own + (k - 2) * height : own + (k - 1) * height, :] = folded


def split_columns_kernel(shards, place, attend, query, attend_qry, cross, out_weight, to_far, to_near, chunk):
    rows, model = out_weight.shape
    part = model // shards
    sources = ((attend, 0), (attend, 1), (query, 0), (attend_qry, 0), (cross, 0), (cross, 1))
    to_far[3 * rows :, :] = out_weight[...]
    to_near[2 * rows :, :] = out_weight[...]
    for me in range(shards):

        @pl.when(place[0] == me)
        def _(me=me):
            blocks = []
            for k in range(shards):
                starts = [(s * shards + (me ^ k)) * part for _, s in sources]
                pieces = [ref[:, c : c + part] for (ref, _), c in zip(sources, starts)]
                blocks.append((jnp.concatenate(pieces[:4], axis=1), jnp.concatenate(pieces[4:], axis=1)))
            chunk[:rows, :] = blocks[0][0]
            chunk[rows:, : 2 * part] = blocks[0][1]
            to_near[:rows, :] = blocks[1][0]
            to_near[rows : 2 * rows, : 2 * part] = blocks[1][1]
            to_far[:rows, :] = blocks[2][0]
            to_far[rows : 2 * rows, :] = blocks[3][0]
            to_far[2 * rows : 3 * rows, :] = jnp.concatenate([blocks[2][1], blocks[3][1]], axis=1)

    chunk[rows:, 2 * part :] = jnp.zeros((rows, model - 2 * part), bf16)
    to_near[rows : 2 * rows, 2 * part :] = jnp.zeros((rows, model - 2 * part), bf16)


def join_columns_kernel(shards, wide, place, chunk, near, far, both, visual, query):
    rows, model = chunk.shape[0] // 2, chunk.shape[1]
    part = model // shards
    gap = jnp.zeros((rows, wide - part), bf16)
    sources = (
        (0, chunk, 0, rows, 0), (1, near, 0, rows, 0), (2, far, 0, 2 * rows, 0), (3, both, rows, 2 * rows, 2 * part)
    )
    for k, ref, first, second, lane in sources:
        block = ref[first : first + rows, :]
        rest = ref[second : second + rows, :][:, lane : lane + 2 * part]
        pieces = [block[:, s * part : (s + 1) * part] for s in range(4)]
        pieces += [rest[:, s * part : (s + 1) * part] for s in range(2)]

        at = pl.ds(pl.multiple_of((place[0] ^ k) * rows, rows), rows)
        for out, items in ((visual, (0, 1, 2)), (query, (3, 0, 1, 4, 5))):
            for place_, item in enumerate(items):
                out[at, place_ * wide : (place_ + 1) * wide] = jnp.concatenate([pieces[item], gap], axis=1)


def share_kernel(shards, place, first, second, third, *refs):
    outs, stack = refs[:shards], refs[shards]
    rows, model = third.shape
    height = outs[0].shape[0]
    start = pl.multiple_of(place[1] * height, 16)
    if stack.shape[0] > 3 * rows:
        stack[3 * rows :, :] = jnp.zeros((stack.shape[0] - 3 * rows, model), bf16)
    stack[2 * rows : 3 * rows, :] = third[...]
    for me in range(shards):

        @pl.when(place[0] == me)
        def _(me=me):
            for k in range(shards):
                j = me ^ k
                stack[:rows, :] = first[:, j * model : (j + 1) * model]
                stack[rows : 2 * rows, :] = second[:, j * model : (j + 1) * model]
                outs[k][...] = stack[pl.ds(start, height), :]


def unshare_kernel(place, given, out):
    pages, shards, height, model = given.shape
    rows = model // shards
    for k in range(shards):
        block = given[:, k].reshape(pages * height, model)
        for i in range(3):
            start = pl.multiple_of(i * model + (place[0] ^ k) * rows, rows)
            out[pl.ds(start, rows), :] = block[i * rows : (i + 1) * rows]


GROUPS = 8


def feed_grads_kernel(shards, norm, dhidden, act, top, norm_qry, dhidden_qry, act_qry, top_qry, out):
    up_share = 2 * norm.shape[1] // (shards * GROUPS)
    down_share = 2 * act.shape[1] // GROUPS
    size = shards * up_share + down_share
    halfway = GROUPS // 2
    ups = ((norm, dhidden), (norm_qry, dhidden_qry))
    downs = ((act, top), (act_qry, top_qry))
    for k in range(2):

        @pl.when(pl.program_id(0) == k)
        def _(k=k):
            left, right = ups[k]
            result = left_tmul(left[...], right[...]).astype(bf16)
            for g in range(halfway):
                for j in range(shards):
                    start = (j * halfway + g) * up_share
                    to = (k * halfway + g) * size + j * up_share
                    out[to : to + up_share, :] = result[start : start + up_share]

        @pl.when(pl.program_id(0) == k + 2)
        def _(k=k):
            left, right = downs[k]
            result = left_tmul(left[...], right[...]).astype(bf16)
            for g in range(halfway):
                to = (k * halfway + g) * size + shards * up_share
                out[to : to + down_share, :] = result[g * down_share : (g + 1) * down_share]


def lay_out_feed_kernel(shards, place, ups, downs, up, up_qry, down, down_qry):
    rows, height, width = up.shape[0], down.shape[0], ups.shape[1]
    for me in range(shards):

        @pl.when(place[0] == me)
        def _(me=me):
            for j in range(shards):
                start = (me ^ j) * 2 * rows
                at = slice(j * width, (j + 1) * width)
                up[:, at] = ups[start : start + rows, :].astype(f32)
                up_qry[:, at] = ups[start + rows : start + 2 * rows, :].astype(f32)

    down[...] = downs[:height, :].astype(f32)
    down_qry[...] = downs[height:, :].astype(f32)


def fold(block, width):
    rows, lanes = block.shape
    if lanes > width:
        rest = block[:, width:]
        count = width // rest.shape[1]
        step = rows // count
        return jnp.concatenate(
            [block[:, :width], jnp.concatenate([rest[i * step : (i + 1) * step] for i in range(count)], axis=1)], axis=0
        )
    half = rows // 2
    first, second = block[:half], block[half:]
    gap = width - lanes
    rest = second[:, gap:]
    count = width // rest.shape[1]
    step = half // count
    return jnp.concatenate(
        [
            jnp.concatenate([first, second[:, :gap]], axis=1),
            jnp.concatenate([rest[i * step : (i + 1) * step] for i in range(count)], axis=1),
        ],
        axis=0,
    )


def unfold(block, rows, lanes):
    width = block.shape[1]
    if lanes > width:
        count = width // (lanes - width)
        part = lanes - width
        last = block[rows:]
        return jnp.concatenate(
            [block[:rows], jnp.concatenate([last[:, i * part : (i + 1) * part] for i in range(count)], axis=0)], axis=1
        )
    half = rows // 2
    gap = width - lanes
    part = lanes - gap
    last = block[half:]
    rest = jnp.concatenate([last[:, i * part : (i + 1) * part] for i in range(width // part)], axis=0)
    first = block[:half]
    return jnp.concatenate(
        [first[:, :lanes], jnp.concatenate([first[:, lanes:], rest], axis=1)], axis=0
    )


def split_halves_kernel(shards, part, wide, place, *refs):
    grads, own_rows, keep, give = refs[:-3], refs[-3], refs[-2], refs[-1]
    rows = grads[0].shape[0] // shards
    half, entry = rows // 2, keep.shape[0] // shards
    quarter = own_rows.shape[0] // (2 * shards)
    for k in range(shards):
        for out, side in ((keep, place[1]), (give, 1 - place[1])):
            start = pl.multiple_of((place[0] ^ k) * rows + side * half, half)
            columns = []
            for grad in grads:
                block = grad[pl.ds(start, half), :]
                columns += [block[:, c : c + part] for c in range(0, block.shape[1], wide)]
            out[k * entry : k * entry + half, :] = jnp.concatenate(columns, axis=1).astype(bf16)
            start = pl.multiple_of(side * quarter * shards + k * quarter, 8)
            block = own_rows[pl.ds(start, quarter), :]
            out[k * entry + half : (k + 1) * entry, :] = fold(block, out.shape[1]).astype(bf16)


def lay_out_kernel(shards, pieces, direct, place, here, other, *outs):
    outs, own_rows = outs[:-1], outs[-1]
    half = outs[0].shape[0] // 2
    entry = here.shape[0] // shards
    quarter = own_rows.shape[0] // (2 * shards)
    depth = place[2] if direct else 0
    for first in range(shards):

        @pl.when((place[0] ^ depth) == first)
        def _(first=first):
            for block, side in ((here, place[1]), (other, 1 - place[1])):
                start = 0
                for out, count in zip(outs, pieces):
                    step = out.shape[1] // (count * shards)
                    columns = []
                    for s in range(count):
                        for j in range(shards):
                            at = (first ^ j) * entry
                            columns.append(block[at : at + half, start + s * step : start + (s + 1) * step])
                    result = jnp.concatenate(columns, axis=1).astype(f32)
                    out[pl.ds(pl.multiple_of(side * half, 8), half), :] = result
                    start += step * count

    for block, side in ((here, place[1]), (other, 1 - place[1])):
        for k in range(shards):
            piece = block[k * entry + half : (k + 1) * entry, :].astype(f32)
            start = pl.multiple_of(side * quarter * shards + (k ^ depth) * quarter, 8)
            own_rows[pl.ds(start, quarter), :] = unfold(piece, quarter, own_rows.shape[1])


def lay_out_pages_kernel(shards, pieces, place, blocks, *outs):
    outs, own_rows = outs[:-1], outs[-1]
    half = outs[0].shape[0] // 2
    entry = blocks.shape[0] // (2 * shards)
    quarter = own_rows.shape[0] // (2 * shards)
    for me in range(shards):

        @pl.when(place[0] == me)
        def _(me=me):
            for side in range(2):
                start = 0
                for out, count in zip(outs, pieces):
                    step = out.shape[1] // (count * shards)
                    columns = []
                    for s in range(count):
                        for j in range(shards):
                            at = (2 * (me ^ j) + side) * entry
                            columns.append(blocks[at : at + half, start + s * step : start + (s + 1) * step])
                    out[side * half : (side + 1) * half, :] = jnp.concatenate(columns, axis=1).astype(f32)
                    start += step * count

    for side in range(2):
        for k in range(shards):
            at = (2 * k + side) * entry
            piece = blocks[at + half : at + entry, :].astype(f32)
            start = (side * shards + k) * quarter
            own_rows[start : start + quarter, :] = unfold(piece, quarter, own_rows.shape[1])


def kernel_call(function, grid, ins, outs, args, scratch=(), place=None, name=None, us=2):
    prefetch = () if place is None else (place,)
    return pl.pallas_call(
        function,
        grid_spec=pltpu.PrefetchScalarGridSpec(
            num_scalar_prefetch=len(prefetch),
            grid=grid,
            in_specs=ins,
            out_specs=[spec for spec, _ in outs],
            scratch_shapes=list(scratch),
        ),
        out_shape=[shape for _, shape in outs],
        compiler_params=pltpu.CompilerParams(vmem_limit_bytes=VMEM_BYTES),
        cost_estimate=pl.CostEstimate(flops=us * 10**6, bytes_accessed=10**3, transcendentals=0),
        name=name,
    )(*prefetch, *args)


def whole(shape):
    return pl.BlockSpec(tuple(shape), lambda *_: (0,) * len(shape))


def all_of(*arrays):
    return [whole(a.shape) for a in arrays]


def full_out(shape, dtype):
    return whole(shape), jax.ShapeDtypeStruct(tuple(shape), dtype)


def window_places(page_width):
    half = WS // 2
    columns = page_width // WS + 1
    top = np.zeros((columns * half * WS, WS * page_width), np.float32)
    low = np.zeros_like(top)
    for j in range(columns):
        for r in range(half):
            for c in range(WS):
                column = j * WS + c - half
                if 0 <= column < page_width:
                    place = (j * half + r) * WS + c
                    top[place, (half + r) * page_width + column] = 1.0
                    low[place, r * page_width + column] = 1.0
    cut = half * page_width
    return [jnp.asarray(m, bf16) for m in (top, low, top[:, cut:].T, low[:, :cut].T)]


def bias_slots(table, regions, page_width):
    half = WS // 2
    columns = page_width // WS + 1
    heads = table.shape[0]
    flipped = table.reshape(heads, SPAN, SPAN)[:, ::-1, ::-1]
    wide = jnp.stack([flipped[:, :, WS - 1 - c : 2 * WS - 1 - c] for c in range(WS)], axis=1)
    wide = wide.reshape(heads, WS, SPAN * WS)
    bias = jnp.stack(
        [wide[:, :, (WS - 1 - r) * WS : (2 * WS - 1 - r) * WS] for r in range(WS)], axis=1
    ).reshape(heads, WS * WS, WS * WS)
    padded = jnp.pad(regions, (half, half), constant_values=-1).reshape(columns, WS)
    of_place = jnp.tile(padded, (1, WS))
    allowed = (of_place[:, :, None] == of_place[:, None, :]) & (of_place[:, None, :] >= 0)
    mask = jnp.where(allowed, 0.0, masked_fill).astype(f32)
    slots = bias[None] + mask[:, None]
    return slots.reshape(columns * heads * WS * WS, WS * WS)


def bias_gather(grad, heads):
    shaped = grad.reshape(heads, WS, WS, WS * WS)
    wide = sum(
        jnp.pad(shaped[:, r], ((0, 0), (0, 0), ((WS - 1 - r) * WS, r * WS))) for r in range(WS)
    ).reshape(heads, WS, SPAN, WS)
    flipped = wide[:, :, ::-1, ::-1]
    table = sum(jnp.pad(flipped[:, c], ((0, 0), (0, 0), (c, WS - 1 - c))) for c in range(WS))
    return table.reshape(heads, SPAN * SPAN)


def body(
    visual,
    queries,
    query_lengths,
    column_regions,
    gain_window,
    window_qkv,
    window_out,
    position_bias,
    gain_visual,
    gain_query,
    attend_query,
    attend_kv,
    attend_out,
    cross_query,
    cross_kv,
    cross_out,
    gain_feed,
    visual_up,
    visual_down,
    gain_query_feed,
    query_up,
    query_down,
    cotangent_visual,
    cotangent_query,
):
    shards = lax.axis_size("win")
    pages = lax.axis_size("page")
    me = lax.axis_index("win").astype(jnp.int32)
    page = lax.axis_index("page").astype(jnp.int32)
    row_count, page_width, model = visual.shape[1:]
    own = row_count * page_width
    tokens = own * shards
    slots_count = queries.shape[1]
    heads = HEADS // shards
    head_size = model // HEADS
    part = heads * head_size
    wide = -(-part // LANES) * LANES
    static = (heads, head_size, head_size ** (-0.5))
    stripes = shards + 1
    rows = model // shards
    hidden = visual_down.shape[0]
    order = xor_order(shards)
    where_me = me.reshape(1)
    where_page = jnp.stack([me, page % 2])
    short = packed_rows(own, part, wide)

    def block_of(width, column=0):
        return pl.BlockSpec((own, width), lambda i, *_: (i, column))

    def token_out(width, dtype=bf16):
        return block_of(width), jax.ShapeDtypeStruct((tokens, width), dtype)

    def packed_block():
        return pl.BlockSpec((short, wide), lambda i, *_: (i, 0))

    def packed_out():
        return packed_block(), jax.ShapeDtypeStruct((short * shards, wide), bf16)

    def half_outs():
        shape = jax.ShapeDtypeStruct((tokens // 2, model), bf16)
        count = shards // 2
        return [
            (pl.BlockSpec((own, model), lambda i, *_: (jnp.minimum(i, count - 1), 0)), shape),
            (pl.BlockSpec((own, model), lambda i, *_: (jnp.maximum(i - count, 0), 0)), shape),
        ]

    visual_own = visual[0].reshape(own, model)
    folded_rows = rows * 3 * part // model
    to_far, to_near, chunk = kernel_call(
        functools.partial(entry_kernel, shards, 3),
        (1,),
        [whole((own, model)), whole(window_qkv.shape)],
        [
            full_out((own + 2 * folded_rows, model), bf16),
            full_out((own + folded_rows, model), bf16),
            full_out((folded_rows, model), bf16),
        ],
        (visual_own, window_qkv),
        place=where_me,
        name="entry",
    )
    far = swap(to_far, "win", 2)
    near = swap(to_near, "win", 1)
    gain_tied = tie(to_far, gain_window, gain_visual, gain_query, gain_feed, gain_query_feed)
    gains = jnp.concatenate([*gain_tied, jnp.zeros((11 * rows,), bf16)]).reshape(16, rows)
    gain_parts = gather_four(gains)

    height = -(-3 * rows // (16 * pages)) * 16
    shares = kernel_call(
        functools.partial(share_kernel, shards),
        (1,),
        all_of(visual_up, query_up, cross_out),
        [full_out((height, model), bf16)] * shards,
        (visual_up, query_up, cross_out),
        scratch=[pltpu.VMEM((height * pages, model), bf16)],
        place=jnp.stack([me, page]),
        name="share",
    )
    shares = exchange(shares)

    mixed_far, mixed_near, mixed_own = kernel_call(
        functools.partial(split_columns_kernel, shards),
        (1,),
        all_of(attend_kv, cross_query, attend_query, cross_kv, window_out),
        [
            full_out((4 * rows, model), bf16),
            full_out((3 * rows, model), bf16),
            full_out((2 * rows, model), bf16),
        ],
        (attend_kv, cross_query, attend_query, cross_kv, window_out),
        place=where_me,
        name="split_columns",
    )
    slots = bias_slots(position_bias.astype(f32), column_regions[0], page_width)
    far, slots, mixed_far, mixed_near, mixed_own, *rest = fence(
        far, slots, mixed_far, mixed_near, mixed_own, *shares, *gain_parts
    )
    shares, gain_parts = rest[:shards], rest[shards:]
    spread_weights = lax.all_gather(jnp.stack(shares), "page")
    both = swap(far, "win", 1)
    mixed_from_far = swap(mixed_far, "win", 2)
    mixed_from_near = swap(mixed_near, "win", 1)

    places = window_places(page_width)
    row_mask = np.zeros((stripes, 1, WS * WS), np.float32)
    row_mask[0, :, : WS * WS // 2] = masked_fill
    row_mask[-1, :, WS * WS // 2 :] = masked_fill
    row_mask = jnp.asarray(row_mask)
    position = jnp.asarray(np.argsort(order), jnp.int32)[me ^ jnp.arange(shards, dtype=jnp.int32)]
    position = jnp.concatenate([position, where_me])

    def arriving(width, height=own):
        return pl.BlockSpec((height, width), lambda i, at: (at[jnp.minimum(i, shards - 1)], 0))

    def leaving(width, height=own):
        return pl.BlockSpec((height, width), lambda i, at: (at[jnp.maximum(i - 1, 0)], 0))

    def of_tokens(spec, width):
        return spec(width), jax.ShapeDtypeStruct((tokens, width), bf16)

    window_specs = all_of(*places, slots) + [pl.BlockSpec((1, 1, WS * WS), lambda i, at: (i, 0, 0))]
    window_args = (*places, slots, row_mask)
    vis_low, qkv_w, gains_all, norm_win, packed, heads_win = kernel_call(
        functools.partial(window_forward_kernel, *static),
        (stripes,),
        all_of(to_far, far, near, both, chunk, *gain_parts) + window_specs,
        [
            of_tokens(arriving, model),
            full_out((model, 3 * wide), bf16),
            full_out((16, model), f32),
            of_tokens(arriving, model),
            of_tokens(arriving, 3 * wide),
            (leaving(wide, short), jax.ShapeDtypeStruct((short * shards, wide), bf16)),
        ],
        (to_far, far, near, both, chunk, *gain_parts) + window_args,
        scratch=[pltpu.VMEM((own, 3 * wide), bf16)] * 2
        + [pltpu.VMEM((own // 2, wide), f32), pltpu.VMEM((own, model), bf16)],
        place=position,
        name="window_forward",
        us=17,
    )
    packed, norm_win, vis_low, gains_all, qkv_w, heads_win, mixed_from_far, mixed_from_near = fence(
        packed, norm_win, vis_low, gains_all, qkv_w, heads_win, mixed_from_far, mixed_from_near
    )
    win_far, win_near = swap(heads_win, "win", 2), swap(heads_win, "win", 1)
    late_inputs = tie(heads_win, window_out, cross_out, attend_out, cotangent_visual)
    length = query_lengths[0]
    slot_ids = jnp.arange(slots_count, dtype=jnp.int32)
    live = slot_ids < length
    live_mask = jnp.where(live, 0.0, masked_fill).astype(f32)[None]
    reach = (slot_ids[None, :] <= slot_ids[:, None]) & live[None, :]
    causal_mask = jnp.where(reach, 0.0, masked_fill).astype(f32)
    window_rows_out = jnp.pad(late_inputs[0], ((0, wide - part), (0, 0)))
    cross_rows_out = jnp.pad(late_inputs[1], ((0, wide - part), (0, 0)))
    attend_rows_out = jnp.pad(late_inputs[2], ((0, wide - part), (0, 0)))
    top_own = late_inputs[3][0].reshape(own, model)
    mixed_from_both = swap(mixed_from_far, "win", 1)

    vis_w, qry_w = kernel_call(
        functools.partial(join_columns_kernel, shards, wide),
        (1,),
        all_of(mixed_own, mixed_from_near, mixed_from_far, mixed_from_both),
        [full_out((model, 3 * wide), bf16), full_out((model, 5 * wide), bf16)],
        (mixed_own, mixed_from_near, mixed_from_far, mixed_from_both),
        place=where_me,
        name="join_columns",
    )
    query_in = queries[0].astype(f32)
    norm_qry = norm_low(query_in, gains_all[2:3])
    proj_qry = matmul(norm_qry, qry_w).astype(bf16)
    (
        vis_w, qry_w, proj_qry, live_mask, causal_mask, window_rows_out, cross_rows_out, attend_rows_out, top_own,
        win_far
    ) = fence(
        vis_w, qry_w, proj_qry, live_mask, causal_mask, window_rows_out, cross_rows_out, attend_rows_out, top_own,
        win_far
    )
    win_parts = [heads_win, win_far, win_near, swap(win_far, "win", 1)]
    top_far = swap(top_own, "win", 2)

    def qry_piece(i):
        return pl.BlockSpec((slots_count, wide), lambda *_: (0, i))

    def vis_piece(i):
        return pl.BlockSpec((tokens, wide), lambda *_: (0, i))

    def piece_specs():
        return [pl.BlockSpec((short, wide), lambda i, *_, k=k: (i ^ k, 0)) for k in range(shards)]

    def rows_block(i):
        return pl.BlockSpec((rows, model), lambda *_: (i, 0))

    mid, norm_vis, proj_vis, heads_cross = kernel_call(
        functools.partial(middle_kernel, *static),
        (shards,),
        [block_of(model)]
        + piece_specs()
        + [rows_block(0), rows_block(3), rows_block(2), rows_block(3)]
        + all_of(gains_all, vis_w)
        + [qry_piece(3), qry_piece(4)]
        + all_of(live_mask),
        [token_out(model, f32), token_out(model), token_out(3 * wide), packed_out()],
        (
            vis_low, *win_parts, window_out, mixed_from_far, mixed_from_near, mixed_from_both, gains_all, vis_w,
            proj_qry, proj_qry, live_mask,
        ),
        name="middle",
        us=13,
    )
    mid, norm_vis, proj_vis, heads_cross, top_far = fence(mid, norm_vis, proj_vis, heads_cross, top_far)
    cross_far, cross_near = swap(heads_cross, "win", 2), swap(heads_cross, "win", 1)
    top_near = swap(top_own, "win", 1)
    top_both = swap(top_far, "win", 1)

    query_specs = [
        qry_piece(0),
        qry_piece(1),
        qry_piece(2),
        vis_piece(0),
        vis_piece(1),
        whole(causal_mask.shape),
    ]
    query_args = (proj_qry, proj_qry, proj_qry, proj_vis, proj_vis, causal_mask)
    (heads_qry,) = kernel_call(
        functools.partial(query_forward_kernel, *static),
        (1,),
        query_specs,
        [full_out((slots_count, part), bf16)],
        query_args,
        name="query_forward",
        us=4,
    )
    (three,) = kernel_call(
        unshare_kernel,
        (1,),
        all_of(spread_weights),
        [full_out((3 * model, model), bf16)],
        tie(heads_qry, spread_weights),
        place=where_me,
        name="unshare",
    )
    vup_w, qup_w, cross_out_w = [three[i * model : (i + 1) * model] for i in range(3)]
    qry_far = swap(heads_qry, "win", 2)
    qry_near = swap(heads_qry, "win", 1)
    vup_w, qup_w, cross_out_w, qry_far, cross_far = fence(vup_w, qup_w, cross_out_w, qry_far, cross_far)
    qry_parts = [heads_qry, qry_far, qry_near, swap(qry_far, "win", 1)]
    cross_parts = [heads_cross, cross_far, cross_near, swap(cross_far, "win", 1)]
    top_parts = [top_own, top_far, top_near, top_both]
    attend_far = swap(tie(cross_far, attend_out)[0], "win", 2)
    attend_near = swap(attend_out, "win", 1)

    late, norm_feed, act_vis, dhid_vis, top_low, feed_keep, feed_send = kernel_call(
        functools.partial(feed_kernel, part),
        (shards,),
        [block_of(model)]
        + piece_specs()
        + all_of(cross_out_w, gains_all, vup_w, visual_down, *top_parts),
        [full_out((own, model), f32), token_out(model), token_out(hidden), token_out(hidden), token_out(model)]
        + half_outs(),
        (mid, *cross_parts, cross_out_w, gains_all, vup_w, visual_down, *top_parts),
        scratch=[pltpu.VMEM((own, model), bf16)],
        place=where_me,
        name="feed",
        us=18,
    )
    late, norm_feed, act_vis, dhid_vis, top_low, feed_keep, feed_send, attend_far, *qry_parts = fence(
        late, norm_feed, act_vis, dhid_vis, top_low, feed_keep, feed_send, attend_far, *qry_parts
    )
    attend_parts = [attend_out, attend_far, attend_near, swap(attend_far, "win", 1)]
    feed_terms, feed_second = scatter_pieces(feed_keep, feed_send)

    tied = tie(feed_send, *qry_parts, *attend_parts)
    feed_args = (queries[0], *tied, gains_all, qup_w, query_down, cotangent_query[0])
    slot_shape = (slots_count, model)
    query_mid, norm_qfeed, act_qry, dhid_qry, dqfeed_part = kernel_call(
        query_feed_kernel,
        (1,),
        all_of(*feed_args),
        [full_out(slot_shape, f32)] + [full_out(slot_shape, bf16)] * 4,
        feed_args,
        name="query_feed",
        us=6,
    )
    dqfeed, dqfeed_last = total_sum(dqfeed_part)
    pairs = (norm_feed, dhid_vis, act_vis, top_low, norm_qfeed, dhid_qry, act_qry, cotangent_query[0])
    pairs = tie(dqfeed_last, *pairs)
    (feed_grads,) = kernel_call(
        functools.partial(feed_grads_kernel, shards),
        (4,),
        all_of(*pairs),
        [full_out((4 * hidden, model), bf16)],
        pairs,
        name="feed_grads",
        us=10,
    )
    act_now, act_qry_now = tie(feed_grads, act_vis, act_qry)
    final_keep, final_send = kernel_call(
        halves_kernel,
        (shards,),
        [block_of(hidden), whole(visual_down.shape)],
        half_outs(),
        (act_now, visual_down),
        name="visual_final",
        us=4,
    )
    query_final_part = matmul(act_qry_now, query_down).astype(bf16)
    query_mid, dqfeed_last, feed_last, feed_grads, final_keep, final_send, query_final_part = fence(
        query_mid, dqfeed_last, feed_terms[2], feed_grads, final_keep, final_send, query_final_part
    )
    feed_terms = (feed_terms[0], feed_terms[1], feed_last)
    up_share, down_share = 2 * rows // GROUPS, 2 * hidden // GROUPS

    def to_sources(summed):
        groups = summed.reshape(GROUPS, -1, model)
        ups = groups[:, : shards * up_share].reshape(GROUPS, shards, up_share, model).transpose(1, 0, 2, 3)
        ups = trade(ups.reshape(shards, GROUPS * up_share, model))
        return jnp.concatenate(ups, axis=0), groups[:, shards * up_share :].reshape(-1, model)

    if pages == GROUPS:
        feed_sum = lax.psum_scatter(feed_grads, "page", scatter_dimension=0, tiled=True)
    else:
        feed_sum = lax.psum(feed_grads, "page")

    def back_through_norm(line, tensor, terms, residual, dtypes):
        own_block = pl.BlockSpec((own, model), lambda *_: (0, 0))
        return kernel_call(
            functools.partial(norm_back_kernel, line),
            (1,),
            [own_block, whole(gains_all.shape)] + [own_block] * 4,
            [(own_block, jax.ShapeDtypeStruct((own, model), d)) for d in dtypes],
            (tensor, gains_all, *terms, residual),
            name="norm_back",
        )

    grad_late, dz_cross = back_through_norm(3, late, feed_terms, top_own, [f32, bf16])
    grad_late, dz_cross = fence(grad_late, dz_cross)
    cross_dz = gather_four(dz_cross)

    back_args = query_args + (query_mid, gains_all, cotangent_query[0], dqfeed, attend_rows_out)
    dq, dkq, dvq, dkv, dvv, grad_qmid, dz_attend = kernel_call(
        functools.partial(query_backward_kernel, *static),
        (1,),
        query_specs + all_of(*back_args[len(query_args) :]),
        [full_out((slots_count, wide), bf16)] * 3
        + [full_out((tokens, wide), bf16)] * 2
        + [full_out(slot_shape, f32), full_out(slot_shape, bf16)],
        back_args,
        name="query_backward",
        us=8,
    )
    query_total, query_last = total_sum(query_final_part)
    (final_own, final_near, final_last), final_second = scatter_pieces(final_keep, final_send)
    dkv, final_second, query_last, cross_far = fence(dkv, final_second, query_last, cross_dz[1])
    cross_dz = [cross_dz[0], cross_far, cross_dz[2], swap(cross_far, "win", 1)]

    out_rows = cross_rows_out
    dproj_vis, dck, dcv, grad_cross_out, vis_keep, vis_send = kernel_call(
        functools.partial(cross_backward_kernel, *static),
        (shards,),
        [block_of(3 * wide), qry_piece(3), qry_piece(4)]
        + all_of(live_mask, *cross_dz, out_rows)
        + [packed_block(), block_of(wide), block_of(wide)]
        + all_of(vis_w),
        [token_out(3 * wide)]
        + [full_out((slots_count, wide), f32)] * 2
        + [full_out((part, model), f32)]
        + half_outs(),
        (proj_vis, proj_qry, proj_qry, live_mask, *cross_dz, out_rows, heads_cross, dkv, dvv, vis_w),
        scratch=[pltpu.VMEM((own, model), bf16)],
        name="cross_backward",
        us=16,
    )
    dproj_vis, dck, dcv, grad_cross_out, vis_keep, vis_send, grad_qmid, dz_attend, final_last, query_total = fence(
        dproj_vis, dck, dcv, grad_cross_out, vis_keep, vis_send, grad_qmid, dz_attend, final_last, query_total
    )
    vis_terms, vis_second = scatter_pieces(vis_keep, vis_send)

    depth, side = page // 2, page % 2
    direct = pages == 2 * LINE and shards == LINE
    where_all = jnp.stack([me, side, depth])

    def halves_here(grads, own_rows):
        width = sum(g.shape[1] for g in grads) // wide * part
        entry = rows // 2 + own_rows.shape[0] * model // (2 * shards * width)
        return kernel_call(
            functools.partial(split_halves_kernel, shards, part, wide),
            (1,),
            all_of(*grads, own_rows),
            [full_out((shards * entry, width), bf16)] * 2,
            (*grads, own_rows),
            place=where_all,
            name="split_halves",
            us=3,
        )

    def laid_out(here, other, pieces, width, row_count_):
        return kernel_call(
            functools.partial(lay_out_kernel, shards, pieces, direct),
            (1,),
            all_of(here, other),
            [full_out((rows, count * width * shards), f32) for count in pieces]
            + [full_out((row_count_, model), f32)],
            (here, other),
            place=where_all,
            name="lay_out",
            us=2,
        )

    def laid_out_pages(blocks, pieces, width, row_count_):
        return kernel_call(
            functools.partial(lay_out_pages_kernel, shards, pieces),
            (1,),
            all_of(blocks),
            [full_out((rows, count * width * shards), f32) for count in pieces]
            + [full_out((row_count_, model), f32)],
            (blocks,),
            place=where_all,
            name="lay_out_pages",
            us=2,
        )

    def beside(tensor):
        return lax.ppermute(tensor, "page", [(i, i ^ 1) for i in range(pages)]) if pages > 1 else tensor

    def pair_total(keep, give):
        return keep if pages == 1 else add_low(keep, beside(give))

    def line_terms(own_half):
        return line_send(own_half.reshape(shards, -1, own_half.shape[1]), depth) if direct else [own_half]

    def line_entry(terms):
        if not direct:
            return terms[0]
        entry = line_add(terms)
        pairs = [
            (p * shards + w, p * shards + (w ^ (p // 2))) for p in range(pages) for w in range(shards)
        ]
        moved = lax.ppermute(entry[: rows // 2], ("page", "win"), pairs)
        return jnp.concatenate([moved, entry[rows // 2 :]], axis=0)

    def line_here(entry):
        return jnp.concatenate(line_gather(entry), axis=0) if direct else entry

    def page_gather(entry, give):
        if direct:
            return entry, beside(entry)

        def to_columns(half):
            entries = half.reshape(shards, -1, half.shape[1])
            moved = exchange([entries[k, : rows // 2] for k in range(shards)])
            return jnp.concatenate(
                [x for k in range(shards) for x in (moved[k], entries[k, rows // 2 :])], axis=0
            )

        if pages == 1:
            return to_columns(entry), to_columns(give)
        groups = [list(range(s, pages, 2)) for s in (0, 1)]
        here = to_columns(lax.psum(entry, "page", axis_index_groups=groups))
        return here, beside(here)

    grouped = feed_grads.reshape(2, GROUPS // 2, -1, model)[:, :, : shards * up_share]
    up_grads = grouped.reshape(2, GROUPS // 2, shards, up_share, model).transpose(0, 2, 1, 3, 4)
    up_grads = up_grads.reshape(2, shards * up_share * (GROUPS // 2), model)

    def gain_sum(line, weight, grad):
        return jnp.sum(weight.astype(f32) * grad.astype(f32), axis=1) / gains_all[line]

    dproj_now, norm_now, dck, dcv, dz_attend = tie(vis_second, dproj_vis, norm_vis, dck, dcv, dz_attend)
    dproj_qry = jnp.concatenate([dq, dkq, dvq, dck.astype(bf16), dcv.astype(bf16)], axis=1)
    dnorm_qry, dnorm_last = total_sum(right_tmul(dproj_qry, qry_w))
    grad_vis_w = left_tmul(norm_now, dproj_now)
    grad_qry_w = left_tmul(norm_qry, dproj_qry)
    grad_attend_out = left_tmul(heads_qry, dz_attend)
    qry_columns = [grad_qry_w[:, i * wide : (i + 1) * wide] for i in range(5)]
    mixed_halves = halves_here(
        (
            grad_vis_w[:, :wide] + qry_columns[1],
            grad_vis_w[:, wide : 2 * wide] + qry_columns[2],
            grad_vis_w[:, 2 * wide :],
            qry_columns[0],
            qry_columns[3],
            qry_columns[4],
        ),
        jnp.concatenate([grad_cross_out, grad_attend_out], axis=0),
    )
    *mixed_halves, vis_last = fence(*mixed_halves, vis_terms[2])
    vis_terms = (vis_terms[0], vis_terms[1], vis_last)
    grad_mid, dz_window = back_through_norm(1, mid, vis_terms, grad_late, [f32, bf16])
    grad_mid, dz_window = fence(grad_mid, dz_window)
    window_dz = gather_four(dz_window)
    mixed_pair = pair_total(*mixed_halves)

    final_last, query_total = tie(dz_window, final_last, query_total)
    visual_final = late + (
        final_own[:own].astype(f32) + final_near[:own].astype(f32) + final_last.astype(f32)
    )
    visual_final = visual_final.astype(bf16)
    query_final = (query_mid + query_total).astype(bf16)
    query_back = (grad_qmid + norm_back(query_in, gains_all[2:3], dnorm_qry)).astype(bf16)
    if pages == GROUPS:
        feed_sum = tie(window_dz[1], feed_sum)[0]
    gain_rows = [
        gain_sum(i, w, g)
        for i, w, g in (
            (1, vis_w, grad_vis_w),
            (2, qry_w, grad_qry_w),
            (3, vup_w, up_grads[0]),
            (4, qup_w, up_grads[1]),
        )
    ]
    mixed_pair, feed_sum, query_back, visual_final, query_final, *rest = fence(
        mixed_pair, feed_sum, query_back, visual_final, query_final, *window_dz, *gain_rows
    )
    window_dz, gain_rows = rest[:shards], rest[shards:]
    if pages == GROUPS:
        feed_sum = lax.all_gather(feed_sum, "page", axis=0, tiled=True)
    mixed_terms = line_terms(mixed_pair)

    out_rows = window_rows_out
    dpacked, dnorm_win, bias_grad, grad_window_out = kernel_call(
        functools.partial(window_backward_kernel, *static),
        (stripes,),
        all_of(*window_dz)
        + [arriving(3 * wide), arriving(wide, short)]
        + all_of(out_rows, qkv_w)
        + window_specs,
        [
            of_tokens(leaving, 3 * wide),
            of_tokens(leaving, model),
            full_out((heads * WS * WS, WS * WS), f32),
            full_out((part, model), f32),
        ],
        (*window_dz, packed, heads_win, out_rows, qkv_w) + window_args,
        scratch=[pltpu.VMEM((own, 3 * wide), bf16)] * 2
        + [pltpu.VMEM((own, wide), bf16)] * 2
        + [pltpu.VMEM((own // 2, 3 * wide), f32)]
        + [pltpu.VMEM((places[0].shape[0], 3 * wide), f32)] * 2
        + [pltpu.VMEM((own, model), bf16)],
        place=position,
        name="window_backward",
        us=27,
    )
    dpacked, dnorm_win, bias_grad, grad_window_out, *mixed_terms = fence(
        dpacked, dnorm_win, bias_grad, grad_window_out, *mixed_terms
    )
    mixed_entry = line_entry(mixed_terms)
    grad_qkv_w = left_tmul(norm_win, dpacked)
    qkv_halves = halves_here((grad_qkv_w,), grad_window_out)
    qkv_keep, qkv_give, dnorm_win, bias_grad, grad_qkv_w, mixed_entry = fence(
        *qkv_halves, dnorm_win, bias_grad, grad_qkv_w, mixed_entry
    )
    qkv_halves = (qkv_keep, qkv_give)
    qkv_beside = beside(qkv_give)
    if direct:
        mixed_all = lax.all_gather(mixed_entry, "page", axis=0, tiled=True)
    else:
        mixed_here, mixed_other = page_gather(mixed_entry, mixed_halves[1])

    (win_own, win_near, win_last), win_second = scatter_pieces(dnorm_win[: tokens // 2], dnorm_win[tokens // 2 :])
    bias_part = bias_gather(bias_grad, heads)
    qkv_beside, win_second, bias_part, grad_qkv_w = fence(qkv_beside, win_second, bias_part, grad_qkv_w)
    qkv_terms = line_terms(qkv_keep if pages == 1 else add_low(qkv_keep, qkv_beside))
    small = tiny_sum(jnp.stack([gain_sum(0, qkv_w, grad_qkv_w)] + gain_rows), ("win",))
    small = jnp.concatenate([small.reshape(-1), bias_part.reshape(-1)])
    win_last, small, *qkv_terms = fence(win_last, small, *qkv_terms)
    qkv_entry = line_entry(qkv_terms)
    (visual_back,) = back_through_norm(0, vis_low, (win_own, win_near, win_last), grad_mid, [bf16])
    page_bits = [k for k in reversed(bits_of(pages))]
    for bit in page_bits[:1]:
        small = small + swap(small, "page", bit)
    qkv_entry, small, visual_back = fence(qkv_entry, small, visual_back)
    feed_rows = to_sources(tie(dpacked, feed_sum)[0])
    out_vup, out_vdown, out_qup, out_qdown = [
        full_out(shape, f32) for shape in ((rows, shards * hidden), (hidden, model)) * 2
    ]
    out_vup, out_qup, out_vdown, out_qdown = kernel_call(
        functools.partial(lay_out_feed_kernel, shards),
        (1,),
        all_of(*feed_rows),
        [out_vup, out_qup, out_vdown, out_qdown],
        feed_rows,
        place=where_me,
        name="lay_out_feed",
        us=6,
    )
    qkv_here = line_here(qkv_entry)
    for bit in page_bits[1:]:
        small = small + swap(small, "page", bit)
    out_vup, out_qup, out_vdown, out_qdown, qkv_here = fence(out_vup, out_qup, out_vdown, out_qdown, qkv_here)
    qkv_here, qkv_other = page_gather(qkv_here, qkv_halves[1])
    gain_total = lax.dynamic_slice_in_dim(small[: 5 * model].reshape(5, model), me * rows, rows, 1)
    bias_total = small[5 * model :].reshape(heads, SPAN * SPAN)

    out_qkv, out_wout = laid_out(qkv_here, qkv_other, [3], part, rows)
    mixed_pieces = [2, 1, 1, 2]
    if direct:
        mixed_outs = laid_out_pages(mixed_all, mixed_pieces, part, 2 * rows)
    else:
        mixed_outs = laid_out(mixed_here, mixed_other, mixed_pieces, part, 2 * rows)
    out_akv, out_cq, out_aq, out_ckv, outs_t = mixed_outs

    return (
        visual_final.reshape(1, row_count, page_width, model),
        query_final.reshape(1, slots_count, model),
        visual_back.reshape(1, row_count, page_width, model),
        query_back.reshape(1, slots_count, model),
        gain_total[0],
        out_qkv,
        out_wout,
        bias_total,
        gain_total[1],
        gain_total[2],
        out_aq,
        out_akv,
        outs_t[rows:],
        out_cq,
        out_ckv,
        outs_t[:rows],
        gain_total[3],
        out_vup,
        out_vdown,
        gain_total[4],
        out_qup,
        out_qdown,
    )


def solution(mesh):
    tokens_spec = P("page", "win", None, None)
    slots_spec = P("page", None, None)
    gain, weight = P("win"), P("win", None)
    parameters = (
        gain, weight, weight, weight, gain, gain, weight, weight, weight, weight, weight, weight,
        gain, weight, weight, gain, weight, weight,
    )
    return jax.shard_map(
        body,
        mesh=mesh,
        in_specs=(tokens_spec, slots_spec, P("page"), P("page", None)) + parameters + (tokens_spec, slots_spec),
        out_specs=(tokens_spec, slots_spec, tokens_spec, slots_spec) + parameters,
        check_vma=False,
    )
```

```python
import functools

import jax
import jax.numpy as jnp
import numpy as np
from jax import lax
from jax.experimental import pallas as pl
from jax.experimental.pallas import tpu as pltpu
from jax.sharding import PartitionSpec as P

HEADS = 12
WS = 12
SPAN = 2 * WS - 1
LANES = 256

epsilon = 1e-05
masked_fill = -1000000000.0
bf16 = jnp.bfloat16
f32 = jnp.float32
VMEM_BYTES = 48 * 1024 * 1024


def swap(tensor, axis, bit):
    count = lax.axis_size(axis)
    return lax.ppermute(tensor, axis, [(i, i ^ bit) for i in range(count)])


def bits_of(count):
    bits = []
    while count > 1:
        count //= 2
        bits.append(count)
    return bits


def gather_blocks(block, axis="win"):
    for bit in bits_of(lax.axis_size(axis)):
        block = jnp.concatenate([block, swap(block, axis, bit)], axis=0)
    return block


def scatter_sum(parts, axis="win"):
    bits = bits_of(lax.axis_size(axis))
    for bit in reversed(bits):
        half = parts.shape[0] // 2
        arrived = swap(parts[half:].astype(bf16), axis, bit)
        parts = parts[:half].astype(f32) + arrived.astype(f32)
    return parts


def total_sum(part, axis="win"):
    for bit in reversed(bits_of(lax.axis_size(axis))):
        mine = lax.reduce_precision(part.astype(f32), 8, 7)
        last = mine.astype(bf16)
        part = mine + swap(last, axis, bit).astype(f32)
    return part, last


def total_terms(part, axis="win"):
    bits = list(reversed(bits_of(lax.axis_size(axis))))
    for bit in bits[:-1]:
        mine = lax.reduce_precision(part.astype(f32), 8, 7)
        part = mine + swap(mine.astype(bf16), axis, bit).astype(f32)
    mine = lax.reduce_precision(part.astype(f32), 8, 7).astype(bf16)
    return mine, swap(mine, axis, bits[-1])


def tiny_sum(part, axes):
    for axis in axes:
        for bit in reversed(bits_of(lax.axis_size(axis))):
            part = part + swap(part, axis, bit)
    return part


def pick(stack, index):
    return lax.dynamic_index_in_dim(stack, index, 0, False)


def trade(stack, axis="win"):
    count = lax.axis_size(axis)
    me = lax.axis_index(axis)
    return [pick(stack, me)] + [swap(pick(stack, me ^ k), axis, k) for k in range(1, count)]


def in_order(blocks, axis="win"):
    me = lax.axis_index(axis)
    stack = jnp.stack(blocks) if isinstance(blocks, (list, tuple)) else blocks
    return [pick(stack, me ^ j) for j in range(lax.axis_size(axis))]


def xor_order(count):
    order = [0]
    for bit in bits_of(count):
        order = order + [k ^ bit for k in order]
    return order


def rounded(tensor):
    return lax.reduce_precision(tensor, 8, 7)


def add_low(left, right):
    return rounded(left.astype(f32) + right.astype(f32)).astype(bf16)


LINE = 4


def line_swap(tensor, k):
    pairs = [(2 * a + x, 2 * (a ^ k) + x) for a in range(LINE) for x in (0, 1)]
    return lax.ppermute(tensor, "page", pairs)


def line_send(parts, depth):
    return [pick(parts, depth)] + [line_swap(pick(parts, depth ^ k), k) for k in range(1, LINE)]


def line_add(terms):
    return rounded(total([t.astype(f32) for t in terms])).astype(bf16)


def line_gather(own):
    return [own] + [line_swap(own, k) for k in range(1, LINE)]


def exchange(blocks):
    return [blocks[0]] + [swap(blocks[k], "win", k) for k in range(1, len(blocks))]


def tie(first, *later):
    return lax.optimization_barrier((first,) + later)[1:]


def gather_four(block, axis="win"):
    count = lax.axis_size(axis)
    parts = [block]
    for bit in bits_of(count):
        parts = parts + [swap(p, axis, bit) for p in parts]
    return parts


def fence(*values):
    return lax.optimization_barrier(values)


def scatter_pieces(keep, send):
    bits = bits_of(lax.axis_size("win"))
    arrived = swap(send, "win", bits[-1])
    half = keep.shape[0] // 2
    second = (keep[half:].astype(f32) + arrived[half:].astype(f32)).astype(bf16)
    return (keep, arrived, swap(second, "win", bits[0])), second


def normalise(tensor):
    centre = tensor - jnp.mean(tensor, axis=-1, keepdims=True)
    spread = lax.rsqrt(jnp.mean(centre * centre, axis=-1, keepdims=True) + epsilon)
    return centre * spread, spread


def norm_low(tensor, gain):
    return (normalise(tensor)[0] * gain).astype(bf16)


def norm_back(tensor, gain, upstream):
    unit, spread = normalise(tensor)
    scaled = upstream * gain
    return spread * (
        scaled
        - jnp.mean(scaled, axis=-1, keepdims=True)
        - unit * jnp.mean(scaled * unit, axis=-1, keepdims=True)
    )


def gelu_both(hidden):
    phi = 0.5 * (1.0 + lax.erf(hidden * np.float32(np.sqrt(0.5))))
    density = jnp.exp(-0.5 * hidden * hidden) * np.float32(1.0 / np.sqrt(2.0 * np.pi))
    return hidden * phi, phi + hidden * density


def matmul(left, right):
    return jnp.dot(left, right, preferred_element_type=f32)


def left_tmul(left, right):
    return lax.dot_general(left, right, (((0,), (0,)), ((), ())), preferred_element_type=f32)


def right_tmul(left, right):
    return lax.dot_general(left, right, (((1,), (1,)), ((), ())), preferred_element_type=f32)


def pad_lanes(tensor, width):
    return jnp.pad(tensor, ((0, 0), (0, width - tensor.shape[1])))


def head_mask(head, head_size, width, scale):
    lane = lax.broadcasted_iota(jnp.int32, (1, width), 1)
    inside = (lane >= head * head_size) & (lane < (head + 1) * head_size)
    return jnp.where(inside, np.float32(scale), np.float32(0.0)).astype(bf16)


def softmax_rows(scores):
    peak = jnp.max(scores, axis=-1, keepdims=True)
    mass = jnp.exp(scores - peak)
    return mass * (1.0 / jnp.sum(mass, axis=-1, keepdims=True))


def by_head(tensor, heads, head_size, scale):
    return [tensor * head_mask(h, head_size, tensor.shape[1], scale) for h in range(heads)]


def total(terms):
    result = terms[0]
    for term in terms[1:]:
        result = result + term
    return result


def window_rows(spread_top, spread_low, before, after, window, cells):
    half = cells // 2
    return jnp.concatenate(
        [spread_top[window * half : (window + 1) * half], spread_low[window * half : (window + 1) * half]],
        axis=0,
    ).astype(bf16)


def pack_lanes(tensor, wide):
    rows, part = tensor.shape
    first = packed_rows(rows, part, wide)
    spare = wide - part
    tail = tensor[first:]
    side = [tail[:, s : s + spare] for s in range(0, part, spare)]
    rest = first - tail.shape[0] * len(side)
    side.append(jnp.zeros((rest, spare), tensor.dtype))
    return jnp.concatenate([tensor[:first], jnp.concatenate(side, axis=0)], axis=1)


def packed_rows(rows, part, wide):
    return -(-rows * part // (wide * 16)) * 16


def unpack_lanes(packed, rows, part):
    first, wide = packed.shape
    spare, tail = wide - part, rows - first
    side = packed[:, part:]
    last = jnp.concatenate([side[s * tail : (s + 1) * tail] for s in range(part // spare)], axis=1)
    return jnp.concatenate([packed[:, :part], last], axis=0)


def pick_block(blocks, place, target):
    for k, block in enumerate(blocks):

        @pl.when(place == k)
        def _(block=block):
            target[...] = block[: target.shape[0], :]


def window_forward_kernel(
    heads, head_size, scale, place, near, second, third, fourth, chunk, gain_own, gain_second, gain_third,
    gain_fourth, top_in, low_in, top_out, low_out, slots, rows, visual, weight, gains, norm, packed, mixed, before, after, held, chosen,
):
    step, last = pl.program_id(0), pl.num_programs(0) - 1
    cells = WS * WS
    half = cells // 2
    width = weight.shape[1] // 3
    blocks = (near, second, third, fourth)
    shards = len(blocks)
    me = place[shards]
    own, piece, part = chosen.shape[0], chunk.shape[0], heads * head_size

    @pl.when(step == 0)
    def _():
        before[...] = jnp.zeros_like(before)
        held[...] = jnp.zeros_like(held)
        order = xor_order(shards)
        starts = (None, own, own, own + piece)
        for p, k in enumerate(order):
            source = chunk[...] if p == 0 else blocks[p][starts[p] : starts[p] + piece, :]
            rows_here = weight.shape[0] // shards
            source = unfold(source, rows_here, 3 * part)
            gap = jnp.zeros((rows_here, width - part), bf16)
            columns = [x for s in range(3) for x in (source[:, s * part : (s + 1) * part], gap)]
            at = pl.ds(pl.multiple_of((me ^ k) * rows_here, rows_here), rows_here)
            weight[at, :] = jnp.concatenate(columns, axis=1)
        for device in range(shards):

            @pl.when(me == device)
            def _(device=device):
                lines = [None] * shards
                for p, ref in enumerate((gain_own, gain_second, gain_third, gain_fourth)):
                    lines[device ^ order[p]] = ref[...].astype(f32)
                gains[...] = jnp.concatenate(lines, axis=1)

    @pl.when(step < last)
    def _():
        pick_block(blocks, place[jnp.minimum(step, last - 1)], chosen)
        visual[...] = chosen[...]
        low = norm_low(chosen[...].astype(f32), gains[0:1, :])
        norm[...] = low
        after[...] = matmul(low, weight[...]).astype(bf16)
        packed[...] = after[...]

    @pl.when(step == last)
    def _():
        after[...] = jnp.zeros_like(after)

    top = matmul(top_in[...], before[...])
    low = matmul(low_in[...], after[...])
    upper, lower = [], []
    for j in range(top.shape[0] // half):
        part = window_rows(top, low, before, after, j, cells)
        query, key, value = part[:, :width], part[:, width : 2 * width], part[:, 2 * width :]
        stacked = jnp.concatenate(by_head(query, heads, head_size, scale), axis=0)
        mask = slots[j * heads * cells : (j + 1) * heads * cells, :] + rows[0]
        probs = softmax_rows(right_tmul(stacked, key) + mask).astype(bf16)
        values = by_head(value, heads, head_size, 1.0)
        result = total([matmul(probs[h * cells : (h + 1) * cells], values[h]) for h in range(heads)])
        upper.append(result[:half])
        lower.append(result[half:])
    above = matmul(top_out[...], jnp.concatenate(upper, axis=0).astype(bf16))
    below = matmul(low_out[...], jnp.concatenate(lower, axis=0).astype(bf16))

    @pl.when(step > 0)
    def _():
        block = jnp.concatenate([held[...], above], axis=0)
        mixed[...] = pack_lanes(block[:, : heads * head_size], width).astype(bf16)

    held[...] = below
    before[...] = after[...]


def window_backward_kernel(
    heads, head_size, scale, place, near, second, third, fourth, packed, mixed, weight_out, weight, top_in,
    low_in, top_out, low_out, slots, rows, grads, dnorm, bias_out, out_grad, before, after, top_before,
    top_after, held, upper, lower, upstream,
):
    step, last = pl.program_id(0), pl.num_programs(0) - 1
    cells = WS * WS
    half = cells // 2
    width = weight.shape[1] // 3

    @pl.when(step == 0)
    def _():
        before[...] = jnp.zeros_like(before)
        top_before[...] = jnp.zeros_like(top_before)
        bias_out[...] = jnp.zeros_like(bias_out)
        out_grad[...] = jnp.zeros_like(out_grad)
        held[...] = jnp.zeros_like(held)

    @pl.when(step < last)
    def _():
        pick_block((near, second, third, fourth), place[jnp.minimum(step, last - 1)], upstream)
        after[...] = packed[...]
        top_after[...] = right_tmul(upstream[...], weight_out[...]).astype(bf16)
        whole_heads = unpack_lanes(mixed[...], upstream.shape[0], heads * head_size)
        out_grad[...] += left_tmul(whole_heads, upstream[...])

    @pl.when(step == last)
    def _():
        after[...] = jnp.zeros_like(after)
        top_after[...] = jnp.zeros_like(top_after)

    top = matmul(top_in[...], before[...])
    low = matmul(low_in[...], after[...])
    given_top = matmul(top_in[...], top_before[...])
    given_low = matmul(low_in[...], top_after[...])
    for j in range(top.shape[0] // half):
        part = window_rows(top, low, before, after, j, cells)
        given = window_rows(given_top, given_low, before, after, j, cells)
        query, key, value = part[:, :width], part[:, width : 2 * width], part[:, 2 * width :]
        stacked = jnp.concatenate(by_head(query, heads, head_size, scale), axis=0)
        mask = slots[j * heads * cells : (j + 1) * heads * cells, :] + rows[0]
        probs = softmax_rows(right_tmul(stacked, key) + mask)
        given = jnp.concatenate(by_head(given, heads, head_size, 1.0), axis=0)
        dprobs = right_tmul(given, value)
        inner = jnp.sum(probs * dprobs, axis=-1, keepdims=True)
        dscores = (probs * (dprobs - inner)).astype(bf16)
        bias_out[...] += dscores.astype(f32)
        keys = by_head(key, heads, head_size, scale)
        dquery = total([matmul(dscores[h * cells : (h + 1) * cells], keys[h]) for h in range(heads)])
        dkey = left_tmul(dscores, stacked)
        dvalue = left_tmul(probs.astype(bf16), given)
        for s, result in enumerate((dquery, dkey, dvalue)):
            upper[j * half : (j + 1) * half, s * width : (s + 1) * width] = result[:half]
            lower[j * half : (j + 1) * half, s * width : (s + 1) * width] = result[half:]
    above = matmul(top_out[...], upper[...].astype(bf16))
    below = matmul(low_out[...], lower[...].astype(bf16))

    block = jnp.concatenate([held[...], above], axis=0).astype(bf16)
    grads[...] = block
    held[...] = below
    dnorm[...] = right_tmul(block, weight[...]).astype(bf16)
    before[...] = after[...]
    top_before[...] = top_after[...]


def middle_kernel(
    heads, head_size, scale, visual, own, second, third, fourth, out_own, out_second, out_third, out_fourth,
    gains, weight, keys, values, live, mid, norm, proj, mixed,
):
    pieces = (own, second, third, fourth)
    weights = (out_own, out_second, out_third, out_fourth)
    part = heads * head_size
    result = visual[...].astype(f32) + total(
        [matmul(unpack_lanes(p[...], mid.shape[0], part), w[...]) for p, w in zip(pieces, weights)]
    )
    mid[...] = result
    low = norm_low(result, gains[1:2, :])
    norm[...] = low
    packed = matmul(low, weight[...]).astype(bf16)
    proj[...] = packed
    width = keys.shape[1]
    query = by_head(packed[:, 2 * width :], heads, head_size, scale)
    value = by_head(values[...], heads, head_size, 1.0)
    terms = []
    for h in range(heads):
        probs = softmax_rows(right_tmul(query[h], keys[...]) + live[...])
        terms.append(matmul(probs.astype(bf16), value[h]))
    mixed[...] = pack_lanes(total(terms)[:, :part], width).astype(bf16)


def feed_kernel(
    part, place, mid, own, second, third, fourth, weight_out, gains, up, down, top_own, top_second, top_third,
    top_fourth, late, norm, act, dhidden, top, keep, send, cotangent,
):
    step, halfway = pl.program_id(0), pl.num_programs(0) // 2
    pieces = (own, second, third, fourth)
    terms = []
    for piece, k in zip(pieces, xor_order(len(pieces))):
        rows = weight_out[pl.ds(pl.multiple_of((place[0] ^ k) * part, part), part), :]
        terms.append(matmul(unpack_lanes(piece[...], mid.shape[0], part), rows))
    result = mid[...] + total(terms)

    @pl.when(step == 0)
    def _():
        late[...] = result

    low = norm_low(result, gains[3:4, :])
    norm[...] = low
    value, slope = gelu_both(matmul(low, up[...]))
    act[...] = value.astype(bf16)
    for k, ref in enumerate((top_own, top_second, top_third, top_fourth)):

        @pl.when(step == k)
        def _(ref=ref):
            cotangent[...] = ref[ref.shape[0] - cotangent.shape[0] :, :]

    top[...] = cotangent[...]
    back = (right_tmul(cotangent[...], down[...]) * slope).astype(bf16)
    dhidden[...] = back
    dnorm = right_tmul(back, up[...]).astype(bf16)

    @pl.when(step < halfway)
    def _():
        keep[...] = dnorm

    @pl.when(step >= halfway)
    def _():
        send[...] = dnorm


def query_feed_kernel(
    query, own, second, third, fourth, top_own, top_second, top_third, top_fourth, gains, up, down, top,
    mid, norm, act, dhidden, dnorm,
):
    pieces, weights = (own, second, third, fourth), (top_own, top_second, top_third, top_fourth)
    result = query[...].astype(f32) + total([matmul(p[...], w[...]) for p, w in zip(pieces, weights)])
    mid[...] = result
    low = norm_low(result, gains[4:5, :])
    norm[...] = low
    value, slope = gelu_both(matmul(low, up[...]))
    act[...] = value.astype(bf16)
    back = (right_tmul(top[...], down[...]) * slope).astype(bf16)
    dhidden[...] = back
    dnorm[...] = right_tmul(back, up[...]).astype(bf16)


def halves_kernel(left, right, keep, send):
    step, halfway = pl.program_id(0), pl.num_programs(0) // 2
    result = matmul(left[...], right[...]).astype(bf16)

    @pl.when(step < halfway)
    def _():
        keep[...] = result

    @pl.when(step >= halfway)
    def _():
        send[...] = result


def query_scores(query, keys_vis, keys_qry, causal, mask):
    masked = query * mask
    return masked, right_tmul(masked, keys_vis), right_tmul(masked, keys_qry) + causal


def joint_softmax(score_vis, score_qry):
    peak = jnp.maximum(
        jnp.max(score_vis, axis=-1, keepdims=True), jnp.max(score_qry, axis=-1, keepdims=True)
    )
    mass_vis = jnp.exp(score_vis - peak)
    mass_qry = jnp.exp(score_qry - peak)
    inverse = 1.0 / (
        jnp.sum(mass_vis, axis=-1, keepdims=True) + jnp.sum(mass_qry, axis=-1, keepdims=True)
    )
    return mass_vis * inverse, mass_qry * inverse


def query_forward_kernel(
    heads, head_size, scale, query, keys_qry, values_qry, keys_vis, values_vis, causal, out
):
    width = query.shape[1]
    terms = []
    for h in range(heads):
        _, score_vis, score_qry = query_scores(
            query[...], keys_vis[...], keys_qry[...], causal[...], head_mask(h, head_size, width, scale)
        )
        prob_vis, prob_qry = joint_softmax(score_vis, score_qry)
        mask = head_mask(h, head_size, width, 1.0)
        terms.append(matmul(prob_vis.astype(bf16), values_vis[...] * mask))
        terms.append(matmul(prob_qry.astype(bf16), values_qry[...] * mask))
    out[...] = total(terms).astype(bf16)[:, : out.shape[1]]


def query_backward_kernel(
    heads, head_size, scale, query, keys_qry, values_qry, keys_vis, values_vis, causal, mid, gains, top, dnorm,
    weight_out, dquery, dkeys_qry, dvalues_qry, dkeys_vis, dvalues_vis, dmid, dz,
):
    width = query.shape[1]
    result = top[...].astype(f32) + norm_back(mid[...], gains[4:5, :], dnorm[...])
    dmid[...] = result
    low = result.astype(bf16)
    dz[...] = low
    upstream = right_tmul(low, weight_out[...]).astype(bf16)
    sums = [[], [], [], [], []]
    for h in range(heads):
        masked, score_vis, score_qry = query_scores(
            query[...], keys_vis[...], keys_qry[...], causal[...], head_mask(h, head_size, width, scale)
        )
        prob_vis, prob_qry = joint_softmax(score_vis, score_qry)
        given = upstream * head_mask(h, head_size, width, 1.0)
        dprob_vis = right_tmul(given, values_vis[...])
        dprob_qry = right_tmul(given, values_qry[...])
        inner = jnp.sum(prob_vis * dprob_vis, axis=-1, keepdims=True) + jnp.sum(
            prob_qry * dprob_qry, axis=-1, keepdims=True
        )
        dscore_vis = (prob_vis * (dprob_vis - inner)).astype(bf16)
        dscore_qry = (prob_qry * (dprob_qry - inner)).astype(bf16)
        mask = head_mask(h, head_size, width, scale)
        sums[0].append(matmul(dscore_vis, keys_vis[...] * mask))
        sums[0].append(matmul(dscore_qry, keys_qry[...] * mask))
        sums[1].append(left_tmul(dscore_qry, masked))
        sums[2].append(left_tmul(prob_qry.astype(bf16), given))
        sums[3].append(left_tmul(dscore_vis, masked))
        sums[4].append(left_tmul(prob_vis.astype(bf16), given))
    for ref, terms in zip((dquery, dkeys_qry, dvalues_qry, dkeys_vis, dvalues_vis), sums):
        ref[...] = total(terms).astype(bf16)


def cross_backward_kernel(
    heads, head_size, scale, proj, keys, values, live, near, second, third, fourth, weight_out, mixed,
    dkeys_vis, dvalues_vis, weight, dproj, dkeys, dvalues, out_grad, keep, send, upstream,
):
    step, halfway = pl.program_id(0), pl.num_programs(0) // 2
    width = keys.shape[1]

    @pl.when(step == 0)
    def _():
        dkeys[...] = jnp.zeros_like(dkeys)
        dvalues[...] = jnp.zeros_like(dvalues)
        out_grad[...] = jnp.zeros_like(out_grad)

    pick_block((near, second, third, fourth), step, upstream)
    out_grad[...] += left_tmul(unpack_lanes(mixed[...], upstream.shape[0], heads * head_size), upstream[...])
    top = right_tmul(upstream[...], weight_out[...]).astype(bf16)
    query = by_head(proj[:, 2 * width :], heads, head_size, scale)
    given = by_head(top, heads, head_size, 1.0)
    scaled = by_head(keys[...], heads, head_size, scale)
    terms = []
    for h in range(heads):
        probs = softmax_rows(right_tmul(query[h], keys[...]) + live[...])
        dprobs = right_tmul(given[h], values[...])
        inner = jnp.sum(probs * dprobs, axis=-1, keepdims=True)
        dscores = (probs * (dprobs - inner)).astype(bf16)
        terms.append(matmul(dscores, scaled[h]))
        dkeys[...] += left_tmul(dscores, query[h])
        dvalues[...] += left_tmul(probs.astype(bf16), given[h])
    block = jnp.concatenate([dkeys_vis[...], dvalues_vis[...], total(terms).astype(bf16)], axis=1)
    dproj[...] = block
    dnorm = right_tmul(block, weight[...]).astype(bf16)

    @pl.when(step < halfway)
    def _():
        keep[...] = dnorm

    @pl.when(step >= halfway)
    def _():
        send[...] = dnorm


def norm_back_kernel(line, tensor, gains, first, second, third, residual, *outs):
    upstream = first[...].astype(f32) + second[...].astype(f32) + third[...].astype(f32)
    gain = gains[line : line + 1, :]
    result = residual[...].astype(f32) + norm_back(tensor[...].astype(f32), gain, upstream)
    for out in outs:
        out[...] = result.astype(out.dtype)


def entry_kernel(shards, pieces, place, visual, weight, to_far, to_near, chunk):
    own, rows = visual.shape[0], weight.shape[0]
    part = weight.shape[1] // (pieces * shards)
    to_far[:own, :] = visual[...]
    to_near[:own, :] = visual[...]
    for me in range(shards):

        @pl.when(place[0] == me)
        def _(me=me):
            for k in range(shards):
                starts = [(s * shards + (me ^ k)) * part for s in range(pieces)]
                block = jnp.concatenate([weight[:, c : c + part] for c in starts], axis=1)
                folded = fold(block, visual.shape[1])
                height = folded.shape[0]
                if k == 0:
                    chunk[...] = folded
                elif k == 1:
                    to_near[own : own + height, :] = folded
                else:
                    to_far[own + (k - 2) * height : own + (k - 1) * height, :] = folded


def split_columns_kernel(shards, place, attend, query, attend_qry, cross, out_weight, to_far, to_near, chunk):
    rows, model = out_weight.shape
    part = model // shards
    sources = ((attend, 0), (attend, 1), (query, 0), (attend_qry, 0), (cross, 0), (cross, 1))
    to_far[3 * rows :, :] = out_weight[...]
    to_near[2 * rows :, :] = out_weight[...]
    for me in range(shards):

        @pl.when(place[0] == me)
        def _(me=me):
            blocks = []
            for k in range(shards):
                starts = [(s * shards + (me ^ k)) * part for _, s in sources]
                pieces = [ref[:, c : c + part] for (ref, _), c in zip(sources, starts)]
                blocks.append((jnp.concatenate(pieces[:4], axis=1), jnp.concatenate(pieces[4:], axis=1)))
            chunk[:rows, :] = blocks[0][0]
            chunk[rows:, : 2 * part] = blocks[0][1]
            to_near[:rows, :] = blocks[1][0]
            to_near[rows : 2 * rows, : 2 * part] = blocks[1][1]
            to_far[:rows, :] = blocks[2][0]
            to_far[rows : 2 * rows, :] = blocks[3][0]
            to_far[2 * rows : 3 * rows, :] = jnp.concatenate([blocks[2][1], blocks[3][1]], axis=1)

    chunk[rows:, 2 * part :] = jnp.zeros((rows, model - 2 * part), bf16)
    to_near[rows : 2 * rows, 2 * part :] = jnp.zeros((rows, model - 2 * part), bf16)


def join_columns_kernel(shards, wide, place, chunk, near, far, both, visual, query):
    rows, model = chunk.shape[0] // 2, chunk.shape[1]
    part = model // shards
    gap = jnp.zeros((rows, wide - part), bf16)
    sources = (
        (0, chunk, 0, rows, 0), (1, near, 0, rows, 0), (2, far, 0, 2 * rows, 0), (3, both, rows, 2 * rows, 2 * part)
    )
    for k, ref, first, second, lane in sources:
        block = ref[first : first + rows, :]
        rest = ref[second : second + rows, :][:, lane : lane + 2 * part]
        pieces = [block[:, s * part : (s + 1) * part] for s in range(4)]
        pieces += [rest[:, s * part : (s + 1) * part] for s in range(2)]

        at = pl.ds(pl.multiple_of((place[0] ^ k) * rows, rows), rows)
        for out, items in ((visual, (0, 1, 2)), (query, (3, 0, 1, 4, 5))):
            for place_, item in enumerate(items):
                out[at, place_ * wide : (place_ + 1) * wide] = jnp.concatenate([pieces[item], gap], axis=1)


def share_kernel(shards, place, first, second, third, *refs):
    outs, stack = refs[:shards], refs[shards]
    rows, model = third.shape
    height = outs[0].shape[0]
    start = pl.multiple_of(place[1] * height, 16)
    if stack.shape[0] > 3 * rows:
        stack[3 * rows :, :] = jnp.zeros((stack.shape[0] - 3 * rows, model), bf16)
    stack[2 * rows : 3 * rows, :] = third[...]
    for me in range(shards):

        @pl.when(place[0] == me)
        def _(me=me):
            for k in range(shards):
                j = me ^ k
                stack[:rows, :] = first[:, j * model : (j + 1) * model]
                stack[rows : 2 * rows, :] = second[:, j * model : (j + 1) * model]
                outs[k][...] = stack[pl.ds(start, height), :]


def unshare_kernel(place, given, out):
    pages, shards, height, model = given.shape
    rows = model // shards
    for k in range(shards):
        block = given[:, k].reshape(pages * height, model)
        for i in range(3):
            start = pl.multiple_of(i * model + (place[0] ^ k) * rows, rows)
            out[pl.ds(start, rows), :] = block[i * rows : (i + 1) * rows]


GROUPS = 8


def feed_grads_kernel(shards, norm, dhidden, act, top, norm_qry, dhidden_qry, act_qry, top_qry, out):
    up_share = 2 * norm.shape[1] // (shards * GROUPS)
    down_share = 2 * act.shape[1] // GROUPS
    size = shards * up_share + down_share
    halfway = GROUPS // 2
    ups = ((norm, dhidden), (norm_qry, dhidden_qry))
    downs = ((act, top), (act_qry, top_qry))
    for k in range(2):

        @pl.when(pl.program_id(0) == k)
        def _(k=k):
            left, right = ups[k]
            result = left_tmul(left[...], right[...]).astype(bf16)
            for g in range(halfway):
                for j in range(shards):
                    start = (j * halfway + g) * up_share
                    to = (k * halfway + g) * size + j * up_share
                    out[to : to + up_share, :] = result[start : start + up_share]

        @pl.when(pl.program_id(0) == k + 2)
        def _(k=k):
            left, right = downs[k]
            result = left_tmul(left[...], right[...]).astype(bf16)
            for g in range(halfway):
                to = (k * halfway + g) * size + shards * up_share
                out[to : to + down_share, :] = result[g * down_share : (g + 1) * down_share]


def lay_out_feed_kernel(shards, place, ups, downs, up, up_qry, down, down_qry):
    rows, height, width = up.shape[0], down.shape[0], ups.shape[1]
    for me in range(shards):

        @pl.when(place[0] == me)
        def _(me=me):
            for j in range(shards):
                start = (me ^ j) * 2 * rows
                at = slice(j * width, (j + 1) * width)
                up[:, at] = ups[start : start + rows, :].astype(f32)
                up_qry[:, at] = ups[start + rows : start + 2 * rows, :].astype(f32)

    down[...] = downs[:height, :].astype(f32)
    down_qry[...] = downs[height:, :].astype(f32)


def fold(block, width):
    rows, lanes = block.shape
    if lanes > width:
        rest = block[:, width:]
        count = width // rest.shape[1]
        step = rows // count
        return jnp.concatenate(
            [block[:, :width], jnp.concatenate([rest[i * step : (i + 1) * step] for i in range(count)], axis=1)], axis=0
        )
    half = rows // 2
    first, second = block[:half], block[half:]
    gap = width - lanes
    rest = second[:, gap:]
    count = width // rest.shape[1]
    step = half // count
    return jnp.concatenate(
        [
            jnp.concatenate([first, second[:, :gap]], axis=1),
            jnp.concatenate([rest[i * step : (i + 1) * step] for i in range(count)], axis=1),
        ],
        axis=0,
    )


def unfold(block, rows, lanes):
    width = block.shape[1]
    if lanes > width:
        count = width // (lanes - width)
        part = lanes - width
        last = block[rows:]
        return jnp.concatenate(
            [block[:rows], jnp.concatenate([last[:, i * part : (i + 1) * part] for i in range(count)], axis=0)], axis=1
        )
    half = rows // 2
    gap = width - lanes
    part = lanes - gap
    last = block[half:]
    rest = jnp.concatenate([last[:, i * part : (i + 1) * part] for i in range(width // part)], axis=0)
    first = block[:half]
    return jnp.concatenate(
        [first[:, :lanes], jnp.concatenate([first[:, lanes:], rest], axis=1)], axis=0
    )


def split_halves_kernel(shards, part, wide, place, *refs):
    grads, own_rows, keep, give = refs[:-3], refs[-3], refs[-2], refs[-1]
    rows = grads[0].shape[0] // shards
    half, entry = rows // 2, keep.shape[0] // shards
    quarter = own_rows.shape[0] // (2 * shards)
    for k in range(shards):
        for out, side in ((keep, place[1]), (give, 1 - place[1])):
            start = pl.multiple_of((place[0] ^ k) * rows + side * half, half)
            columns = []
            for grad in grads:
                block = grad[pl.ds(start, half), :]
                columns += [block[:, c : c + part] for c in range(0, block.shape[1], wide)]
            out[k * entry : k * entry + half, :] = jnp.concatenate(columns, axis=1).astype(bf16)
            start = pl.multiple_of(side * quarter * shards + k * quarter, 8)
            block = own_rows[pl.ds(start, quarter), :]
            out[k * entry + half : (k + 1) * entry, :] = fold(block, out.shape[1]).astype(bf16)


def lay_out_kernel(shards, pieces, direct, place, here, other, *outs):
    outs, own_rows = outs[:-1], outs[-1]
    half = outs[0].shape[0] // 2
    entry = here.shape[0] // shards
    quarter = own_rows.shape[0] // (2 * shards)
    depth = place[2] if direct else 0
    for first in range(shards):

        @pl.when((place[0] ^ depth) == first)
        def _(first=first):
            for block, side in ((here, place[1]), (other, 1 - place[1])):
                start = 0
                for out, count in zip(outs, pieces):
                    step = out.shape[1] // (count * shards)
                    columns = []
                    for s in range(count):
                        for j in range(shards):
                            at = (first ^ j) * entry
                            columns.append(block[at : at + half, start + s * step : start + (s + 1) * step])
                    result = jnp.concatenate(columns, axis=1).astype(f32)
                    out[pl.ds(pl.multiple_of(side * half, 8), half), :] = result
                    start += step * count

    for block, side in ((here, place[1]), (other, 1 - place[1])):
        for k in range(shards):
            piece = block[k * entry + half : (k + 1) * entry, :].astype(f32)
            start = pl.multiple_of(side * quarter * shards + (k ^ depth) * quarter, 8)
            own_rows[pl.ds(start, quarter), :] = unfold(piece, quarter, own_rows.shape[1])


def lay_out_pages_kernel(shards, pieces, place, blocks, *outs):
    outs, own_rows = outs[:-1], outs[-1]
    half = outs[0].shape[0] // 2
    entry = blocks.shape[0] // (2 * shards)
    quarter = own_rows.shape[0] // (2 * shards)
    for me in range(shards):

        @pl.when(place[0] == me)
        def _(me=me):
            for side in range(2):
                start = 0
                for out, count in zip(outs, pieces):
                    step = out.shape[1] // (count * shards)
                    columns = []
                    for s in range(count):
                        for j in range(shards):
                            at = (2 * (me ^ j) + side) * entry
                            columns.append(blocks[at : at + half, start + s * step : start + (s + 1) * step])
                    out[side * half : (side + 1) * half, :] = jnp.concatenate(columns, axis=1).astype(f32)
                    start += step * count

    for side in range(2):
        for k in range(shards):
            at = (2 * k + side) * entry
            piece = blocks[at + half : at + entry, :].astype(f32)
            start = (side * shards + k) * quarter
            own_rows[start : start + quarter, :] = unfold(piece, quarter, own_rows.shape[1])


def kernel_call(function, grid, ins, outs, args, scratch=(), place=None, name=None, us=2):
    prefetch = () if place is None else (place,)
    return pl.pallas_call(
        function,
        grid_spec=pltpu.PrefetchScalarGridSpec(
            num_scalar_prefetch=len(prefetch),
            grid=grid,
            in_specs=ins,
            out_specs=[spec for spec, _ in outs],
            scratch_shapes=list(scratch),
        ),
        out_shape=[shape for _, shape in outs],
        compiler_params=pltpu.CompilerParams(vmem_limit_bytes=VMEM_BYTES),
        cost_estimate=pl.CostEstimate(flops=us * 10**6, bytes_accessed=10**3, transcendentals=0),
        name=name,
    )(*prefetch, *args)


def whole(shape):
    return pl.BlockSpec(tuple(shape), lambda *_: (0,) * len(shape))


def all_of(*arrays):
    return [whole(a.shape) for a in arrays]


def full_out(shape, dtype):
    return whole(shape), jax.ShapeDtypeStruct(tuple(shape), dtype)


def window_places(page_width):
    half = WS // 2
    columns = page_width // WS + 1
    top = np.zeros((columns * half * WS, WS * page_width), np.float32)
    low = np.zeros_like(top)
    for j in range(columns):
        for r in range(half):
            for c in range(WS):
                column = j * WS + c - half
                if 0 <= column < page_width:
                    place = (j * half + r) * WS + c
                    top[place, (half + r) * page_width + column] = 1.0
                    low[place, r * page_width + column] = 1.0
    cut = half * page_width
    return [jnp.asarray(m, bf16) for m in (top, low, top[:, cut:].T, low[:, :cut].T)]


def bias_slots(table, regions, page_width):
    half = WS // 2
    columns = page_width // WS + 1
    heads = table.shape[0]
    flipped = table.reshape(heads, SPAN, SPAN)[:, ::-1, ::-1]
    wide = jnp.stack([flipped[:, :, WS - 1 - c : 2 * WS - 1 - c] for c in range(WS)], axis=1)
    wide = wide.reshape(heads, WS, SPAN * WS)
    bias = jnp.stack(
        [wide[:, :, (WS - 1 - r) * WS : (2 * WS - 1 - r) * WS] for r in range(WS)], axis=1
    ).reshape(heads, WS * WS, WS * WS)
    padded = jnp.pad(regions, (half, half), constant_values=-1).reshape(columns, WS)
    of_place = jnp.tile(padded, (1, WS))
    allowed = (of_place[:, :, None] == of_place[:, None, :]) & (of_place[:, None, :] >= 0)
    mask = jnp.where(allowed, 0.0, masked_fill).astype(f32)
    slots = bias[None] + mask[:, None]
    return slots.reshape(columns * heads * WS * WS, WS * WS)


def bias_gather(grad, heads):
    shaped = grad.reshape(heads, WS, WS, WS * WS)
    wide = sum(
        jnp.pad(shaped[:, r], ((0, 0), (0, 0), ((WS - 1 - r) * WS, r * WS))) for r in range(WS)
    ).reshape(heads, WS, SPAN, WS)
    flipped = wide[:, :, ::-1, ::-1]
    table = sum(jnp.pad(flipped[:, c], ((0, 0), (0, 0), (c, WS - 1 - c))) for c in range(WS))
    return table.reshape(heads, SPAN * SPAN)


def body(
    visual,
    queries,
    query_lengths,
    column_regions,
    gain_window,
    window_qkv,
    window_out,
    position_bias,
    gain_visual,
    gain_query,
    attend_query,
    attend_kv,
    attend_out,
    cross_query,
    cross_kv,
    cross_out,
    gain_feed,
    visual_up,
    visual_down,
    gain_query_feed,
    query_up,
    query_down,
    cotangent_visual,
    cotangent_query,
):
    shards = lax.axis_size("win")
    pages = lax.axis_size("page")
    me = lax.axis_index("win").astype(jnp.int32)
    page = lax.axis_index("page").astype(jnp.int32)
    row_count, page_width, model = visual.shape[1:]
    own = row_count * page_width
    tokens = own * shards
    slots_count = queries.shape[1]
    heads = HEADS // shards
    head_size = model // HEADS
    part = heads * head_size
    wide = -(-part // LANES) * LANES
    static = (heads, head_size, head_size ** (-0.5))
    stripes = shards + 1
    rows = model // shards
    hidden = visual_down.shape[0]
    order = xor_order(shards)
    where_me = me.reshape(1)
    where_page = jnp.stack([me, page % 2])
    short = packed_rows(own, part, wide)

    def block_of(width, column=0):
        return pl.BlockSpec((own, width), lambda i, *_: (i, column))

    def token_out(width, dtype=bf16):
        return block_of(width), jax.ShapeDtypeStruct((tokens, width), dtype)

    def packed_block():
        return pl.BlockSpec((short, wide), lambda i, *_: (i, 0))

    def packed_out():
        return packed_block(), jax.ShapeDtypeStruct((short * shards, wide), bf16)

    def half_outs():
        shape = jax.ShapeDtypeStruct((tokens // 2, model), bf16)
        count = shards // 2
        return [
            (pl.BlockSpec((own, model), lambda i, *_: (jnp.minimum(i, count - 1), 0)), shape),
            (pl.BlockSpec((own, model), lambda i, *_: (jnp.maximum(i - count, 0), 0)), shape),
        ]

    visual_own = visual[0].reshape(own, model)
    folded_rows = rows * 3 * part // model
    to_far, to_near, chunk = kernel_call(
        functools.partial(entry_kernel, shards, 3),
        (1,),
        [whole((own, model)), whole(window_qkv.shape)],
        [
            full_out((own + 2 * folded_rows, model), bf16),
            full_out((own + folded_rows, model), bf16),
            full_out((folded_rows, model), bf16),
        ],
        (visual_own, window_qkv),
        place=where_me,
        name="entry",
    )
    far = swap(to_far, "win", 2)
    near = swap(to_near, "win", 1)
    gain_tied = tie(to_far, gain_window, gain_visual, gain_query, gain_feed, gain_query_feed)
    gains = jnp.concatenate([*gain_tied, jnp.zeros((11 * rows,), bf16)]).reshape(16, rows)
    gain_parts = gather_four(gains)

    height = -(-3 * rows // (16 * pages)) * 16
    shares = kernel_call(
        functools.partial(share_kernel, shards),
        (1,),
        all_of(visual_up, query_up, cross_out),
        [full_out((height, model), bf16)] * shards,
        (visual_up, query_up, cross_out),
        scratch=[pltpu.VMEM((height * pages, model), bf16)],
        place=jnp.stack([me, page]),
        name="share",
    )
    shares = exchange(shares)

    mixed_far, mixed_near, mixed_own = kernel_call(
        functools.partial(split_columns_kernel, shards),
        (1,),
        all_of(attend_kv, cross_query, attend_query, cross_kv, window_out),
        [
            full_out((4 * rows, model), bf16),
            full_out((3 * rows, model), bf16),
            full_out((2 * rows, model), bf16),
        ],
        (attend_kv, cross_query, attend_query, cross_kv, window_out),
        place=where_me,
        name="split_columns",
    )
    slots = bias_slots(position_bias.astype(f32), column_regions[0], page_width)
    far, slots, mixed_far, mixed_near, mixed_own, *rest = fence(
        far, slots, mixed_far, mixed_near, mixed_own, *shares, *gain_parts
    )
    shares, gain_parts = rest[:shards], rest[shards:]
    spread_weights = lax.all_gather(jnp.stack(shares), "page")
    both = swap(far, "win", 1)
    mixed_from_far = swap(mixed_far, "win", 2)
    mixed_from_near = swap(mixed_near, "win", 1)

    places = window_places(page_width)
    row_mask = np.zeros((stripes, 1, WS * WS), np.float32)
    row_mask[0, :, : WS * WS // 2] = masked_fill
    row_mask[-1, :, WS * WS // 2 :] = masked_fill
    row_mask = jnp.asarray(row_mask)
    position = jnp.asarray(np.argsort(order), jnp.int32)[me ^ jnp.arange(shards, dtype=jnp.int32)]
    position = jnp.concatenate([position, where_me])

    def arriving(width, height=own):
        return pl.BlockSpec((height, width), lambda i, at: (at[jnp.minimum(i, shards - 1)], 0))

    def leaving(width, height=own):
        return pl.BlockSpec((height, width), lambda i, at: (at[jnp.maximum(i - 1, 0)], 0))

    def of_tokens(spec, width):
        return spec(width), jax.ShapeDtypeStruct((tokens, width), bf16)

    window_specs = all_of(*places, slots) + [pl.BlockSpec((1, 1, WS * WS), lambda i, at: (i, 0, 0))]
    window_args = (*places, slots, row_mask)
    vis_low, qkv_w, gains_all, norm_win, packed, heads_win = kernel_call(
        functools.partial(window_forward_kernel, *static),
        (stripes,),
        all_of(to_far, far, near, both, chunk, *gain_parts) + window_specs,
        [
            of_tokens(arriving, model),
            full_out((model, 3 * wide), bf16),
            full_out((16, model), f32),
            of_tokens(arriving, model),
            of_tokens(arriving, 3 * wide),
            (leaving(wide, short), jax.ShapeDtypeStruct((short * shards, wide), bf16)),
        ],
        (to_far, far, near, both, chunk, *gain_parts) + window_args,
        scratch=[pltpu.VMEM((own, 3 * wide), bf16)] * 2
        + [pltpu.VMEM((own // 2, wide), f32), pltpu.VMEM((own, model), bf16)],
        place=position,
        name="window_forward",
        us=17,
    )
    packed, norm_win, vis_low, gains_all, qkv_w, heads_win, mixed_from_far, mixed_from_near = fence(
        packed, norm_win, vis_low, gains_all, qkv_w, heads_win, mixed_from_far, mixed_from_near
    )
    win_far, win_near = swap(heads_win, "win", 2), swap(heads_win, "win", 1)
    late_inputs = tie(heads_win, window_out, cross_out, attend_out, cotangent_visual)
    length = query_lengths[0]
    slot_ids = jnp.arange(slots_count, dtype=jnp.int32)
    live = slot_ids < length
    live_mask = jnp.where(live, 0.0, masked_fill).astype(f32)[None]
    reach = (slot_ids[None, :] <= slot_ids[:, None]) & live[None, :]
    causal_mask = jnp.where(reach, 0.0, masked_fill).astype(f32)
    window_rows_out = jnp.pad(late_inputs[0], ((0, wide - part), (0, 0)))
    cross_rows_out = jnp.pad(late_inputs[1], ((0, wide - part), (0, 0)))
    attend_rows_out = jnp.pad(late_inputs[2], ((0, wide - part), (0, 0)))
    top_own = late_inputs[3][0].reshape(own, model)
    mixed_from_both = swap(mixed_from_far, "win", 1)

    vis_w, qry_w = kernel_call(
        functools.partial(join_columns_kernel, shards, wide),
        (1,),
        all_of(mixed_own, mixed_from_near, mixed_from_far, mixed_from_both),
        [full_out((model, 3 * wide), bf16), full_out((model, 5 * wide), bf16)],
        (mixed_own, mixed_from_near, mixed_from_far, mixed_from_both),
        place=where_me,
        name="join_columns",
    )
    query_in = queries[0].astype(f32)
    norm_qry = norm_low(query_in, gains_all[2:3])
    proj_qry = matmul(norm_qry, qry_w).astype(bf16)
    (
        vis_w, qry_w, proj_qry, live_mask, causal_mask, window_rows_out, cross_rows_out, attend_rows_out, top_own,
        win_far
    ) = fence(
        vis_w, qry_w, proj_qry, live_mask, causal_mask, window_rows_out, cross_rows_out, attend_rows_out, top_own,
        win_far
    )
    win_parts = [heads_win, win_far, win_near, swap(win_far, "win", 1)]
    top_far = swap(top_own, "win", 2)

    def qry_piece(i):
        return pl.BlockSpec((slots_count, wide), lambda *_: (0, i))

    def vis_piece(i):
        return pl.BlockSpec((tokens, wide), lambda *_: (0, i))

    def piece_specs():
        return [pl.BlockSpec((short, wide), lambda i, *_, k=k: (i ^ k, 0)) for k in range(shards)]

    def rows_block(i):
        return pl.BlockSpec((rows, model), lambda *_: (i, 0))

    mid, norm_vis, proj_vis, heads_cross = kernel_call(
        functools.partial(middle_kernel, *static),
        (shards,),
        [block_of(model)]
        + piece_specs()
        + [rows_block(0), rows_block(3), rows_block(2), rows_block(3)]
        + all_of(gains_all, vis_w)
        + [qry_piece(3), qry_piece(4)]
        + all_of(live_mask),
        [token_out(model, f32), token_out(model), token_out(3 * wide), packed_out()],
        (
            vis_low, *win_parts, window_out, mixed_from_far, mixed_from_near, mixed_from_both, gains_all, vis_w,
            proj_qry, proj_qry, live_mask,
        ),
        name="middle",
        us=13,
    )
    mid, norm_vis, proj_vis, heads_cross, top_far = fence(mid, norm_vis, proj_vis, heads_cross, top_far)
    cross_far, cross_near = swap(heads_cross, "win", 2), swap(heads_cross, "win", 1)
    top_near = swap(top_own, "win", 1)
    top_both = swap(top_far, "win", 1)

    query_specs = [
        qry_piece(0),
        qry_piece(1),
        qry_piece(2),
        vis_piece(0),
        vis_piece(1),
        whole(causal_mask.shape),
    ]
    query_args = (proj_qry, proj_qry, proj_qry, proj_vis, proj_vis, causal_mask)
    (heads_qry,) = kernel_call(
        functools.partial(query_forward_kernel, *static),
        (1,),
        query_specs,
        [full_out((slots_count, part), bf16)],
        query_args,
        name="query_forward",
        us=4,
    )
    (three,) = kernel_call(
        unshare_kernel,
        (1,),
        all_of(spread_weights),
        [full_out((3 * model, model), bf16)],
        tie(heads_qry, spread_weights),
        place=where_me,
        name="unshare",
    )
    vup_w, qup_w, cross_out_w = [three[i * model : (i + 1) * model] for i in range(3)]
    qry_far = swap(heads_qry, "win", 2)
    qry_near = swap(heads_qry, "win", 1)
    vup_w, qup_w, cross_out_w, qry_far, cross_far = fence(vup_w, qup_w, cross_out_w, qry_far, cross_far)
    qry_parts = [heads_qry, qry_far, qry_near, swap(qry_far, "win", 1)]
    cross_parts = [heads_cross, cross_far, cross_near, swap(cross_far, "win", 1)]
    top_parts = [top_own, top_far, top_near, top_both]
    attend_far = swap(tie(cross_far, attend_out)[0], "win", 2)
    attend_near = swap(attend_out, "win", 1)

    late, norm_feed, act_vis, dhid_vis, top_low, feed_keep, feed_send = kernel_call(
        functools.partial(feed_kernel, part),
        (shards,),
        [block_of(model)]
        + piece_specs()
        + all_of(cross_out_w, gains_all, vup_w, visual_down, *top_parts),
        [full_out((own, model), f32), token_out(model), token_out(hidden), token_out(hidden), token_out(model)]
        + half_outs(),
        (mid, *cross_parts, cross_out_w, gains_all, vup_w, visual_down, *top_parts),
        scratch=[pltpu.VMEM((own, model), bf16)],
        place=where_me,
        name="feed",
        us=18,
    )
    late, norm_feed, act_vis, dhid_vis, top_low, feed_keep, feed_send, attend_far, *qry_parts = fence(
        late, norm_feed, act_vis, dhid_vis, top_low, feed_keep, feed_send, attend_far, *qry_parts
    )
    attend_parts = [attend_out, attend_far, attend_near, swap(attend_far, "win", 1)]
    feed_terms, feed_second = scatter_pieces(feed_keep, feed_send)

    tied = tie(feed_send, *qry_parts, *attend_parts)
    feed_args = (queries[0], *tied, gains_all, qup_w, query_down, cotangent_query[0])
    slot_shape = (slots_count, model)
    query_mid, norm_qfeed, act_qry, dhid_qry, dqfeed_part = kernel_call(
        query_feed_kernel,
        (1,),
        all_of(*feed_args),
        [full_out(slot_shape, f32)] + [full_out(slot_shape, bf16)] * 4,
        feed_args,
        name="query_feed",
        us=6,
    )
    dqfeed, dqfeed_last = total_sum(dqfeed_part)
    pairs = (norm_feed, dhid_vis, act_vis, top_low, norm_qfeed, dhid_qry, act_qry, cotangent_query[0])
    pairs = tie(dqfeed_last, *pairs)
    (feed_grads,) = kernel_call(
        functools.partial(feed_grads_kernel, shards),
        (4,),
        all_of(*pairs),
        [full_out((4 * hidden, model), bf16)],
        pairs,
        name="feed_grads",
        us=10,
    )
    act_now, act_qry_now = tie(feed_grads, act_vis, act_qry)
    final_keep, final_send = kernel_call(
        halves_kernel,
        (shards,),
        [block_of(hidden), whole(visual_down.shape)],
        half_outs(),
        (act_now, visual_down),
        name="visual_final",
        us=4,
    )
    query_final_part = matmul(act_qry_now, query_down).astype(bf16)
    query_mid, dqfeed_last, feed_last, feed_grads, final_keep, final_send, query_final_part = fence(
        query_mid, dqfeed_last, feed_terms[2], feed_grads, final_keep, final_send, query_final_part
    )
    feed_terms = (feed_terms[0], feed_terms[1], feed_last)
    up_share, down_share = 2 * rows // GROUPS, 2 * hidden // GROUPS

    def to_sources(summed):
        groups = summed.reshape(GROUPS, -1, model)
        ups = groups[:, : shards * up_share].reshape(GROUPS, shards, up_share, model).transpose(1, 0, 2, 3)
        ups = trade(ups.reshape(shards, GROUPS * up_share, model))
        return jnp.concatenate(ups, axis=0), groups[:, shards * up_share :].reshape(-1, model)

    if pages == GROUPS:
        feed_sum = lax.psum_scatter(feed_grads, "page", scatter_dimension=0, tiled=True)
    else:
        feed_sum = lax.psum(feed_grads, "page")

    def back_through_norm(line, tensor, terms, residual, dtypes):
        own_block = pl.BlockSpec((own, model), lambda *_: (0, 0))
        return kernel_call(
            functools.partial(norm_back_kernel, line),
            (1,),
            [own_block, whole(gains_all.shape)] + [own_block] * 4,
            [(own_block, jax.ShapeDtypeStruct((own, model), d)) for d in dtypes],
            (tensor, gains_all, *terms, residual),
            name="norm_back",
        )

    grad_late, dz_cross = back_through_norm(3, late, feed_terms, top_own, [f32, bf16])
    grad_late, dz_cross = fence(grad_late, dz_cross)
    cross_dz = gather_four(dz_cross)

    back_args = query_args + (query_mid, gains_all, cotangent_query[0], dqfeed, attend_rows_out)
    dq, dkq, dvq, dkv, dvv, grad_qmid, dz_attend = kernel_call(
        functools.partial(query_backward_kernel, *static),
        (1,),
        query_specs + all_of(*back_args[len(query_args) :]),
        [full_out((slots_count, wide), bf16)] * 3
        + [full_out((tokens, wide), bf16)] * 2
        + [full_out(slot_shape, f32), full_out(slot_shape, bf16)],
        back_args,
        name="query_backward",
        us=8,
    )
    query_last, query_arrived = total_terms(query_final_part)
    (final_own, final_near, final_last), final_second = scatter_pieces(final_keep, final_send)
    dkv, final_second, query_last, cross_far = fence(dkv, final_second, query_last, cross_dz[1])
    cross_dz = [cross_dz[0], cross_far, cross_dz[2], swap(cross_far, "win", 1)]

    out_rows = cross_rows_out
    dproj_vis, dck, dcv, grad_cross_out, vis_keep, vis_send = kernel_call(
        functools.partial(cross_backward_kernel, *static),
        (shards,),
        [block_of(3 * wide), qry_piece(3), qry_piece(4)]
        + all_of(live_mask, *cross_dz, out_rows)
        + [packed_block(), block_of(wide), block_of(wide)]
        + all_of(vis_w),
        [token_out(3 * wide)]
        + [full_out((slots_count, wide), f32)] * 2
        + [full_out((part, model), f32)]
        + half_outs(),
        (proj_vis, proj_qry, proj_qry, live_mask, *cross_dz, out_rows, heads_cross, dkv, dvv, vis_w),
        scratch=[pltpu.VMEM((own, model), bf16)],
        name="cross_backward",
        us=16,
    )
    dproj_vis, dck, dcv, grad_cross_out, vis_keep, vis_send, grad_qmid, dz_attend, final_last, query_arrived = fence(
        dproj_vis, dck, dcv, grad_cross_out, vis_keep, vis_send, grad_qmid, dz_attend, final_last, query_arrived
    )
    vis_terms, vis_second = scatter_pieces(vis_keep, vis_send)

    depth, side = page // 2, page % 2
    direct = pages == 2 * LINE and shards == LINE
    where_all = jnp.stack([me, side, depth])

    def halves_here(grads, own_rows):
        width = sum(g.shape[1] for g in grads) // wide * part
        entry = rows // 2 + own_rows.shape[0] * model // (2 * shards * width)
        return kernel_call(
            functools.partial(split_halves_kernel, shards, part, wide),
            (1,),
            all_of(*grads, own_rows),
            [full_out((shards * entry, width), bf16)] * 2,
            (*grads, own_rows),
            place=where_all,
            name="split_halves",
            us=3,
        )

    def laid_out(here, other, pieces, width, row_count_):
        return kernel_call(
            functools.partial(lay_out_kernel, shards, pieces, direct),
            (1,),
            all_of(here, other),
            [full_out((rows, count * width * shards), f32) for count in pieces]
            + [full_out((row_count_, model), f32)],
            (here, other),
            place=where_all,
            name="lay_out",
            us=2,
        )

    def laid_out_pages(blocks, pieces, width, row_count_):
        return kernel_call(
            functools.partial(lay_out_pages_kernel, shards, pieces),
            (1,),
            all_of(blocks),
            [full_out((rows, count * width * shards), f32) for count in pieces]
            + [full_out((row_count_, model), f32)],
            (blocks,),
            place=where_all,
            name="lay_out_pages",
            us=2,
        )

    def beside(tensor):
        return lax.ppermute(tensor, "page", [(i, i ^ 1) for i in range(pages)]) if pages > 1 else tensor

    def pair_total(keep, give):
        return keep if pages == 1 else add_low(keep, beside(give))

    def line_terms(own_half):
        return line_send(own_half.reshape(shards, -1, own_half.shape[1]), depth) if direct else [own_half]

    def line_entry(terms):
        if not direct:
            return terms[0]
        entry = line_add(terms)
        pairs = [
            (p * shards + w, p * shards + (w ^ (p // 2))) for p in range(pages) for w in range(shards)
        ]
        moved = lax.ppermute(entry[: rows // 2], ("page", "win"), pairs)
        return jnp.concatenate([moved, entry[rows // 2 :]], axis=0)

    def line_here(entry):
        return jnp.concatenate(line_gather(entry), axis=0) if direct else entry

    def page_gather(entry, give):
        if direct:
            return entry, beside(entry)

        def to_columns(half):
            entries = half.reshape(shards, -1, half.shape[1])
            moved = exchange([entries[k, : rows // 2] for k in range(shards)])
            return jnp.concatenate(
                [x for k in range(shards) for x in (moved[k], entries[k, rows // 2 :])], axis=0
            )

        if pages == 1:
            return to_columns(entry), to_columns(give)
        groups = [list(range(s, pages, 2)) for s in (0, 1)]
        here = to_columns(lax.psum(entry, "page", axis_index_groups=groups))
        return here, beside(here)

    grouped = feed_grads.reshape(2, GROUPS // 2, -1, model)[:, :, : shards * up_share]
    up_grads = grouped.reshape(2, GROUPS // 2, shards, up_share, model).transpose(0, 2, 1, 3, 4)
    up_grads = up_grads.reshape(2, shards * up_share * (GROUPS // 2), model)

    def gain_sum(line, weight, grad):
        return jnp.sum(weight.astype(f32) * grad.astype(f32), axis=1) / gains_all[line]

    dproj_now, norm_now, dck, dcv, dz_attend = tie(vis_second, dproj_vis, norm_vis, dck, dcv, dz_attend)
    dproj_qry = jnp.concatenate([dq, dkq, dvq, dck.astype(bf16), dcv.astype(bf16)], axis=1)
    dnorm_qry, dnorm_last = total_sum(right_tmul(dproj_qry, qry_w))
    grad_vis_w = left_tmul(norm_now, dproj_now)
    grad_qry_w = left_tmul(norm_qry, dproj_qry)
    grad_attend_out = left_tmul(heads_qry, dz_attend)
    qry_columns = [grad_qry_w[:, i * wide : (i + 1) * wide] for i in range(5)]
    mixed_halves = halves_here(
        (
            grad_vis_w[:, :wide] + qry_columns[1],
            grad_vis_w[:, wide : 2 * wide] + qry_columns[2],
            grad_vis_w[:, 2 * wide :],
            qry_columns[0],
            qry_columns[3],
            qry_columns[4],
        ),
        jnp.concatenate([grad_cross_out, grad_attend_out], axis=0),
    )
    *mixed_halves, vis_last = fence(*mixed_halves, vis_terms[2])
    vis_terms = (vis_terms[0], vis_terms[1], vis_last)
    grad_mid, dz_window = back_through_norm(1, mid, vis_terms, grad_late, [f32, bf16])
    grad_mid, dz_window = fence(grad_mid, dz_window)
    window_dz = gather_four(dz_window)
    mixed_pair = pair_total(*mixed_halves)

    final_last, query_arrived = tie(dz_window, final_last, query_arrived)
    query_total = query_last.astype(f32) + query_arrived.astype(f32)
    visual_final = late + (
        final_own[:own].astype(f32) + final_near[:own].astype(f32) + final_last.astype(f32)
    )
    visual_final = visual_final.astype(bf16)
    query_final = (query_mid + query_total).astype(bf16)
    query_back = (grad_qmid + norm_back(query_in, gains_all[2:3], dnorm_qry)).astype(bf16)
    if pages == GROUPS:
        feed_sum = tie(window_dz[1], feed_sum)[0]
    gain_rows = [
        gain_sum(i, w, g)
        for i, w, g in (
            (1, vis_w, grad_vis_w),
            (2, qry_w, grad_qry_w),
            (3, vup_w, up_grads[0]),
            (4, qup_w, up_grads[1]),
        )
    ]
    mixed_pair, feed_sum, query_back, visual_final, query_final, *rest = fence(
        mixed_pair, feed_sum, query_back, visual_final, query_final, *window_dz, *gain_rows
    )
    window_dz, gain_rows = rest[:shards], rest[shards:]
    if pages == GROUPS:
        feed_sum = lax.all_gather(feed_sum, "page", axis=0, tiled=True)
    mixed_terms = line_terms(mixed_pair)

    out_rows = window_rows_out
    dpacked, dnorm_win, bias_grad, grad_window_out = kernel_call(
        functools.partial(window_backward_kernel, *static),
        (stripes,),
        all_of(*window_dz)
        + [arriving(3 * wide), arriving(wide, short)]
        + all_of(out_rows, qkv_w)
        + window_specs,
        [
            of_tokens(leaving, 3 * wide),
            of_tokens(leaving, model),
            full_out((heads * WS * WS, WS * WS), f32),
            full_out((part, model), f32),
        ],
        (*window_dz, packed, heads_win, out_rows, qkv_w) + window_args,
        scratch=[pltpu.VMEM((own, 3 * wide), bf16)] * 2
        + [pltpu.VMEM((own, wide), bf16)] * 2
        + [pltpu.VMEM((own // 2, 3 * wide), f32)]
        + [pltpu.VMEM((places[0].shape[0], 3 * wide), f32)] * 2
        + [pltpu.VMEM((own, model), bf16)],
        place=position,
        name="window_backward",
        us=27,
    )
    dpacked, dnorm_win, bias_grad, grad_window_out, *mixed_terms = fence(
        dpacked, dnorm_win, bias_grad, grad_window_out, *mixed_terms
    )
    mixed_entry = line_entry(mixed_terms)
    grad_qkv_w = left_tmul(norm_win, dpacked)
    qkv_halves = halves_here((grad_qkv_w,), grad_window_out)
    qkv_keep, qkv_give, dnorm_win, bias_grad, grad_qkv_w, mixed_entry = fence(
        *qkv_halves, dnorm_win, bias_grad, grad_qkv_w, mixed_entry
    )
    qkv_halves = (qkv_keep, qkv_give)
    qkv_beside = beside(qkv_give)
    if direct:
        mixed_all = lax.all_gather(mixed_entry, "page", axis=0, tiled=True)
    else:
        mixed_here, mixed_other = page_gather(mixed_entry, mixed_halves[1])

    (win_own, win_near, win_last), win_second = scatter_pieces(dnorm_win[: tokens // 2], dnorm_win[tokens // 2 :])
    bias_part = bias_gather(bias_grad, heads)
    qkv_beside, win_second, bias_part, grad_qkv_w = fence(qkv_beside, win_second, bias_part, grad_qkv_w)
    qkv_terms = line_terms(qkv_keep if pages == 1 else add_low(qkv_keep, qkv_beside))
    small = tiny_sum(jnp.stack([gain_sum(0, qkv_w, grad_qkv_w)] + gain_rows), ("win",))
    small = jnp.concatenate([small.reshape(-1), bias_part.reshape(-1)])
    win_last, small, *qkv_terms = fence(win_last, small, *qkv_terms)
    qkv_entry = line_entry(qkv_terms)
    (visual_back,) = back_through_norm(0, vis_low, (win_own, win_near, win_last), grad_mid, [bf16])
    page_bits = [k for k in reversed(bits_of(pages))]
    for bit in page_bits[:1]:
        small = small + swap(small, "page", bit)
    qkv_entry, small, visual_back = fence(qkv_entry, small, visual_back)
    feed_rows = to_sources(tie(dpacked, feed_sum)[0])
    out_vup, out_vdown, out_qup, out_qdown = [
        full_out(shape, f32) for shape in ((rows, shards * hidden), (hidden, model)) * 2
    ]
    out_vup, out_qup, out_vdown, out_qdown = kernel_call(
        functools.partial(lay_out_feed_kernel, shards),
        (1,),
        all_of(*feed_rows),
        [out_vup, out_qup, out_vdown, out_qdown],
        feed_rows,
        place=where_me,
        name="lay_out_feed",
        us=6,
    )
    qkv_here = line_here(qkv_entry)
    for bit in page_bits[1:]:
        small = small + swap(small, "page", bit)
    out_vup, out_qup, out_vdown, out_qdown, qkv_here = fence(out_vup, out_qup, out_vdown, out_qdown, qkv_here)
    qkv_here, qkv_other = page_gather(qkv_here, qkv_halves[1])
    gain_total = lax.dynamic_slice_in_dim(small[: 5 * model].reshape(5, model), me * rows, rows, 1)
    bias_total = small[5 * model :].reshape(heads, SPAN * SPAN)

    out_qkv, out_wout = laid_out(qkv_here, qkv_other, [3], part, rows)
    mixed_pieces = [2, 1, 1, 2]
    if direct:
        mixed_outs = laid_out_pages(tie(out_wout, mixed_all)[0], mixed_pieces, part, 2 * rows)
    else:
        mixed_outs = laid_out(mixed_here, mixed_other, mixed_pieces, part, 2 * rows)
    out_akv, out_cq, out_aq, out_ckv, outs_t = mixed_outs

    return (
        visual_final.reshape(1, row_count, page_width, model),
        query_final.reshape(1, slots_count, model),
        visual_back.reshape(1, row_count, page_width, model),
        query_back.reshape(1, slots_count, model),
        gain_total[0],
        out_qkv,
        out_wout,
        bias_total,
        gain_total[1],
        gain_total[2],
        out_aq,
        out_akv,
        outs_t[rows:],
        out_cq,
        out_ckv,
        outs_t[:rows],
        gain_total[3],
        out_vup,
        out_vdown,
        gain_total[4],
        out_qup,
        out_qdown,
    )


def solution(mesh):
    tokens_spec = P("page", "win", None, None)
    slots_spec = P("page", None, None)
    gain, weight = P("win"), P("win", None)
    parameters = (
        gain, weight, weight, weight, gain, gain, weight, weight, weight, weight, weight, weight,
        gain, weight, weight, gain, weight, weight,
    )
    return jax.shard_map(
        body,
        mesh=mesh,
        in_specs=(tokens_spec, slots_spec, P("page"), P("page", None)) + parameters + (tokens_spec, slots_spec),
        out_specs=(tokens_spec, slots_spec, tokens_spec, slots_spec) + parameters,
        check_vma=False,
    )
```
